32 devices in a mesh: wide: 8 (over y, x, core), narrow: 4 (over z).
Axes of the slice: x: 2, y: 2, z: 4, core: 2. Of those that a mesh axis runs over, the one named last changes fastest.
Arguments:
- tokens: bfloat16 [32, 576, 768], P(('wide', 'narrow')), may hold values from -6 to 6
- live_mask: int32 [32, 576], P(('wide', 'narrow')), may hold values from 0 to 1, as said below
- routes: int32 [32, 576, 2], P(('wide', 'narrow')), may hold values from 0 to 7, all different within a row
- priority: int32 [32, 576], P(('wide', 'narrow')), may hold values from 0 to 575, each once within a row
- cotangent: bfloat16 [32, 576, 768], P(('wide', 'narrow')), may hold values from -6 to 6
- first_gain: float32 [768], replicated, may hold values from 0.25 to 1.75
- first_shift: float32 [768], replicated, may hold values from -1.75 to 1.75
- query_weight: bfloat16 [768, 768], replicated, may hold values from -0.21875 to 0.21875
- query_bias: float32 [768], replicated, may hold values from -3 to 3
- key_weight: bfloat16 [768, 768], replicated, may hold values from -0.21875 to 0.21875
- value_weight: bfloat16 [768, 768], replicated, may hold values from -0.21875 to 0.21875
- value_bias: float32 [768], replicated, may hold values from -3 to 3
- out_weight: bfloat16 [768, 768], replicated, may hold values from -2.5 to 2.5
- out_bias: float32 [768], replicated, may hold values from -1.75 to 1.75
- second_gain: float32 [768], replicated, may hold values from 0.25 to 1.75
- second_shift: float32 [768], replicated, may hold values from -1.75 to 1.75
- router_weight: bfloat16 [768, 8], replicated, may hold values from -0.15625 to 0.15625
- expert_in: bfloat16 [8, 768, 3072], P('wide', None, 'narrow'), may hold values from -0.21875 to 0.21875
- expert_in_bias: bfloat16 [8, 3072], P('wide', 'narrow'), may hold values from -3 to 3
- expert_out: bfloat16 [8, 3072, 768], P('wide', 'narrow'), may hold values from -0.75 to 0.75
- expert_out_bias: float32 [8, 768], replicated, may hold values from -12 to 12
Outputs:
- mixed_out: bfloat16 [32, 576, 768], P(('wide', 'narrow'))
- tokens_grad: float32 [32, 576, 768], P(('wide', 'narrow'))
- first_gain_grad: float32 [768], replicated
- first_shift_grad: float32 [768], replicated
- query_weight_grad: float32 [768, 768], replicated
- query_bias_grad: float32 [768], replicated
- key_weight_grad: float32 [768, 768], replicated
- value_weight_grad: float32 [768, 768], replicated
- value_bias_grad: float32 [768], replicated
- out_weight_grad: float32 [768, 768], replicated
- out_bias_grad: float32 [768], replicated
- second_gain_grad: float32 [768], replicated
- second_shift_grad: float32 [768], replicated
- router_grad: float32 [768, 8], replicated
- expert_in_grad: float32 [8, 768, 3072], P('wide', None, 'narrow')
- expert_in_bias_grad: float32 [8, 3072], P('wide', 'narrow')
- expert_out_grad: float32 [8, 3072, 768], P('wide', 'narrow')
- expert_out_bias_grad: float32 [8, 768], replicated
The draws below stay inside these ranges and needn't reach their ends.
Inputs may be any that keep to these rules, and one draw needn't show every extreme that they name: `live_mask`: in each row, 1 on a leading run of at least 432 patches and 0 after it. The two experts of a patch differ; routes of padded patches are not used. `priority`: each row holds every number of 0 to 575 once; a smaller number is served first.
All inputs are finite; a program needn't handle non-finite values.
Results may differ from the reference program's by a relative error of at most 0.02.
Values may be sent and summed in bfloat16 or wider, within the bound.
No kernel may reach another device: no remote copies, remote signals or barrier semaphores. Data moves between devices by JAX's collectives and lax.ppermute only.
A program may use at most 256 MiB of HBM per device.

```python
import jax
import jax.numpy as jnp
from jax import lax

D = 768
HEADS = 12
HEAD_DIM = 64
FF = 3072
PATCHES = 576
SEQ_DEV = 1
EXPERTS = 8
ROWS = 32
CAP = 152


def draw_live_mask(key, part):
    key = jax.random.fold_in(key, 7)
    lengths = jax.random.randint(key, (ROWS, 1), PATCHES - PATCHES // 4, PATCHES + 1)
    places = lax.broadcasted_iota(jnp.int32, (ROWS, PATCHES), 1)
    return (places < lengths).astype(jnp.int32)


def level_of(rng, dims, split, least, largest):
    loudness = 1.0
    for dim, shards_of in split:
        steps = jax.random.uniform(jax.random.fold_in(jax.random.fold_in(rng, 6), dim), (shards_of,), jnp.float32, least / len(split), largest / len(split))
        loudness = loudness * jnp.repeat(jnp.exp(steps), dims[dim] // shards_of).reshape((-1,) + (1,) * (len(dims) - 1 - dim))
    return loudness


def distinct(stream_key, rows, amount, top, lift):
    order = jax.random.permutation(jax.random.fold_in(stream_key, 1), amount)
    favour = order
    for power in range(3):
        favour = favour * favour // amount
    favour = favour * lift // amount
    tickets = jax.random.randint(jax.random.fold_in(stream_key, 2), (rows, amount), 0, 4096) + favour
    sure = jax.random.permutation(jax.random.fold_in(stream_key, 3), rows)[jnp.arange(amount) % rows]
    tickets = jnp.where(jnp.arange(rows)[:, None] == sure[None, :], 1 << 14, tickets)
    merit = tickets * amount + jnp.arange(amount)
    return lax.top_k(merit.astype(jnp.int32), top)[1].astype(jnp.int32)


def normal_values(stream_key, dims, scale, most, split=(), kind=jnp.bfloat16):
    loudness = level_of(stream_key, dims, split, -0.22, 0.18) if split else 1.0
    entries = jax.random.normal(stream_key, dims, jnp.float32) * scale * loudness
    return jnp.minimum(jnp.maximum(entries, -most), most).astype(kind)


def setup_inputs(seed: int = 0) -> dict:
    key_list = jax.random.split(jax.random.key(seed), 22)
    tokens = normal_values(key_list[0], (ROWS, PATCHES, D), 1.0, 6.0, ((0, 32),))
    live_mask = draw_live_mask(jax.random.fold_in(key_list[21], 71), 0)
    routes = distinct(key_list[2], ROWS * PATCHES, EXPERTS, 2, 2048).reshape((ROWS, PATCHES, 2))
    priority = jax.vmap(lambda own: jax.random.permutation(own, PATCHES))(jax.random.split(key_list[3], ROWS)).reshape((ROWS, PATCHES)).astype(jnp.int32)
    cotangent = normal_values(key_list[4], (ROWS, PATCHES, D), 1.0, 6.0, ((0, 32),))
    first_gain = jnp.clip(1.0 + 0.15 * jax.random.normal(key_list[5], (D,), jnp.float32), 0.25, 1.75)
    first_shift = normal_values(key_list[6], (D,), 0.3, 1.75, (), jnp.float32)
    query_weight = normal_values(key_list[7], (D, D), D ** -0.5, 0.21875)
    query_bias = normal_values(key_list[8], (D,), 0.5, 3.0, (), jnp.float32)
    key_weight = normal_values(key_list[9], (D, D), D ** -0.5, 0.21875)
    value_weight = normal_values(key_list[10], (D, D), D ** -0.5, 0.21875)
    value_bias = normal_values(key_list[11], (D,), 0.5, 3.0, (), jnp.float32)
    out_weight = normal_values(key_list[12], (D, D), (max(4 * D // PATCHES, 1)) ** -0.5, 2.5)
    out_bias = normal_values(key_list[13], (D,), 0.3, 1.75, (), jnp.float32)
    second_gain = jnp.clip(1.0 + 0.15 * jax.random.normal(key_list[14], (D,), jnp.float32), 0.25, 1.75)
    second_shift = normal_values(key_list[15], (D,), 0.3, 1.75, (), jnp.float32)
    router_weight = normal_values(key_list[16], (D, EXPERTS), (2 * D) ** -0.5, 0.15625)
    expert_in = normal_values(key_list[17], (EXPERTS, D, FF), D ** -0.5, 0.21875, ((0, 8), (2, 4)))
    expert_in_bias = normal_values(key_list[18], (EXPERTS, FF), 0.5, 3.0, ((0, 8), (1, 4)))
    expert_out = normal_values(key_list[19], (EXPERTS, FF, D), (max(3 * FF // (2 * EXPERTS * EXPERTS), 1)) ** -0.5, 0.75, ((0, 8), (1, 4)))
    expert_out_bias = normal_values(key_list[20], (EXPERTS, D), 2.0, 12.0, (), jnp.float32)
    return dict(tokens=tokens, live_mask=live_mask, routes=routes, priority=priority, cotangent=cotangent, first_gain=first_gain, first_shift=first_shift, query_weight=query_weight, query_bias=query_bias, key_weight=key_weight, value_weight=value_weight, value_bias=value_bias, out_weight=out_weight, out_bias=out_bias, second_gain=second_gain, second_shift=second_shift, router_weight=router_weight, expert_in=expert_in, expert_in_bias=expert_in_bias, expert_out=expert_out, expert_out_bias=expert_out_bias)


@jax.custom_vjp
def low(v):
    return lax.optimization_barrier(v.astype(jnp.bfloat16)).astype(jnp.float32)

@jax.custom_vjp
def low_back(v):
    return v

def low_keep(v):
    return (low(v), None)

def low_pass(kept, grad):
    return (grad,)

def back_keep(v):
    return (v, None)

def back_low(kept, grad):
    return (low(grad),)
low.defvjp(low_keep, low_pass)
low_back.defvjp(back_keep, back_low)
epsilon = 1e-06
highest = lax.Precision.HIGHEST

def layer_norm(source, gain_vec, shift_vec):
    average = lax.optimization_barrier(jnp.mean(source, axis=-1, keepdims=True))
    centred = source - average
    variance = lax.optimization_barrier(jnp.mean(centred * centred, axis=-1, keepdims=True))
    return centred * lax.rsqrt(variance + epsilon) * gain_vec + shift_vec

def slot_table(alive, route_pair, order_key):
    earlier = (order_key[None, :] < order_key[:, None]).astype(jnp.float32)
    columns = lax.broadcasted_iota(jnp.int32, (1, EXPERTS), 1)
    first_pick = ((route_pair[:, 0:1] == columns) & alive[:, None]).astype(jnp.float32)
    second = ((route_pair[:, 1:2] == columns) & alive[:, None]).astype(jnp.float32)
    place_first = lax.optimization_barrier(jnp.sum(jnp.dot(earlier, first_pick, precision=highest) * first_pick, axis=1))
    already = lax.optimization_barrier(jnp.sum(first_pick, axis=0, keepdims=True))
    place_second = lax.optimization_barrier(jnp.sum((jnp.dot(earlier, second, precision=highest) + already) * second, axis=1))
    slots = lax.broadcasted_iota(jnp.int32, (1, EXPERTS * CAP), 1)

    def one_table(route_col, position, onehot):
        kept_mask = alive & (position < CAP)
        target = route_col * CAP + position.astype(jnp.int32)
        spread = ((slots == target[:, None]) & kept_mask[:, None]).astype(jnp.float32)
        return (spread, onehot * kept_mask[:, None].astype(jnp.float32))
    spread_first, first_kept = one_table(route_pair[:, 0], place_first, first_pick)
    spread_second, second_kept = one_table(route_pair[:, 1], place_second, second)
    return (first_pick, second, spread_first, spread_second, first_kept, second_kept)

def group_forward(weights, block, alive_rows, route_rows, order_rows):
    first_gain, first_shift, query_weight, query_bias, key_weight, value_weight, value_bias, out_weight, out_bias, second_gain, second_shift, router_weight, expert_in, expert_in_bias, expert_out, expert_out_bias = weights
    group_size = SEQ_DEV * PATCHES
    scaling = HEAD_DIM ** (-0.5)
    head_shape = (SEQ_DEV, PATCHES, HEADS, HEAD_DIM)
    normed = low(layer_norm(block, first_gain, first_shift))

    def project(matrix):
        return jnp.einsum('spd,de->spe', normed, matrix, precision=highest)
    queries = low(low_back(project(query_weight) + query_bias)).reshape(head_shape)
    key_rows = low(low_back(project(key_weight))).reshape(head_shape)
    value_rows = low(low_back(project(value_weight) + value_bias)).reshape(head_shape)
    scores = low_back(jnp.einsum('sqhd,skhd->shqk', queries, key_rows, precision=highest) * scaling)
    scores = jnp.where(alive_rows[:, None, None, :] > 0, scores, -1e+30)
    attention_probs = low(jax.nn.softmax(scores, axis=-1))
    mixed_heads = low(low_back(jnp.einsum('shqk,skhd->sqhd', attention_probs, value_rows, precision=highest)))
    mixed_heads = mixed_heads.reshape(group_size, D)
    attended = low_back(jnp.dot(mixed_heads, out_weight, precision=highest) + out_bias)
    residual = block.reshape(group_size, D) + attended
    second_normed = low(layer_norm(residual, second_gain, second_shift))
    logits = low_back(jnp.dot(second_normed, router_weight, precision=highest))
    chance = jax.nn.softmax(logits, axis=-1)
    order_key = (order_rows * SEQ_DEV + lax.broadcasted_iota(jnp.int32, (SEQ_DEV, PATCHES), 0)).reshape(group_size)
    first_pick, second, spread_first, spread_second, first_kept, second_kept = slot_table(alive_rows.reshape(group_size) > 0, route_rows.reshape(group_size, 2), order_key)
    buffers = low_back(jnp.dot((spread_first + spread_second).T, second_normed, precision=highest))
    buffers = buffers.reshape(EXPERTS, CAP, D)
    before = low_back(jnp.einsum('ecd,edf->ecf', buffers, expert_in, precision=highest) + expert_in_bias[:, None, :])
    hidden = low(jax.nn.gelu(before, approximate=True))
    produced = low_back(low(jnp.einsum('ecf,efd->ecd', hidden, expert_out, precision=highest)))
    produced = produced.reshape(EXPERTS * CAP, D)
    picked_first = jnp.dot(spread_first, produced, precision=highest) + jnp.dot(first_kept, expert_out_bias, precision=highest)
    picked_second = jnp.dot(spread_second, produced, precision=highest) + jnp.dot(second_kept, expert_out_bias, precision=highest)
    gate_first = lax.optimization_barrier(jnp.sum(chance * first_pick, axis=1, keepdims=True))
    gate_second = lax.optimization_barrier(jnp.sum(chance * second, axis=1, keepdims=True))
    result = residual + gate_first * picked_first + gate_second * picked_second
    return result.reshape(SEQ_DEV, PATCHES, D)

def reference(tokens, live_mask, routes, priority, cotangent, first_gain, first_shift, query_weight, query_bias, key_weight, value_weight, value_bias, out_weight, out_bias, second_gain, second_shift, router_weight, expert_in, expert_in_bias, expert_out, expert_out_bias):
    weights = tuple((member.astype(jnp.float32) for member in (first_gain, first_shift, query_weight, query_bias, key_weight, value_weight, value_bias, out_weight, out_bias, second_gain, second_shift, router_weight, expert_in, expert_in_bias, expert_out, expert_out_bias)))
    groups = ROWS // SEQ_DEV
    alive_all = live_mask.reshape(groups, SEQ_DEV, PATCHES)
    route_all = routes.reshape(groups, SEQ_DEV, PATCHES, 2)
    order_all = priority.reshape(groups, SEQ_DEV, PATCHES)

    def forward(weight_set, blocks):

        def run_group(member):
            return group_forward(weight_set, member[0], member[1], member[2], member[3])
        return lax.map(jax.checkpoint(run_group), (blocks, alive_all, route_all, order_all))
    blocks = tokens.astype(jnp.float32).reshape(groups, SEQ_DEV, PATCHES, D)
    result, pullback = jax.vjp(forward, weights, blocks)
    weight_grads, block_grads = pullback(cotangent.astype(jnp.float32).reshape(groups, SEQ_DEV, PATCHES, D))
    return (result.reshape(ROWS, PATCHES, D).astype(jnp.bfloat16), block_grads.reshape(ROWS, PATCHES, D), weight_grads[0], weight_grads[1], weight_grads[2], weight_grads[3], weight_grads[4], weight_grads[5], weight_grads[6], weight_grads[7], weight_grads[8], weight_grads[9], weight_grads[10], weight_grads[11], weight_grads[12], weight_grads[13], weight_grads[14], weight_grads[15])
```

```python
from functools import partial

import jax
import jax.numpy as jnp
from jax import lax
from jax.experimental import pallas as pl
from jax.experimental.pallas import tpu as pltpu
from jax.sharding import PartitionSpec as P

HEADS = 12
HEAD_DIM = 64


epsilon = 1e-06
highest = lax.Precision.HIGHEST


def layer_norm(source, gain_vec, shift_vec):
    average = jnp.mean(source, axis=-1, keepdims=True)
    centred = source - average
    variance = jnp.mean(centred * centred, axis=-1, keepdims=True)
    return centred * lax.rsqrt(variance + epsilon) * gain_vec + shift_vec


def masked_scores(queries, key_rows, live_row, scaling):
    scores = (
        jnp.einsum("qhd,khd->hqk", queries, key_rows, preferred_element_type=jnp.float32) * scaling
    )
    return jnp.where(live_row[None, None, :] > 0, scores, -1e30)


def attend_forward(queries, key_rows, value_rows, live_row, scaling):
    scores = masked_scores(queries, key_rows, live_row, scaling)
    maximum = jnp.max(scores, axis=-1, keepdims=True)
    weights = jnp.exp(scores - maximum)
    summed_weights = jnp.sum(weights, axis=-1, keepdims=True)
    attention_probs = (weights / summed_weights).astype(jnp.bfloat16)
    mixed_heads = jnp.einsum(
        "hqk,khd->qhd", attention_probs, value_rows, preferred_element_type=jnp.float32
    )
    return (mixed_heads.astype(jnp.bfloat16), maximum + jnp.log(summed_weights))


def attend_backward(queries, key_rows, value_rows, live_row, log_total, mixed_grad, scaling):
    scores = masked_scores(queries, key_rows, live_row, scaling)
    attention_probs = jnp.exp(scores - log_total)
    prob_grad = jnp.einsum(
        "qhd,khd->hqk", mixed_grad, value_rows, preferred_element_type=jnp.float32
    )
    value_grad = jnp.einsum(
        "hqk,qhd->khd",
        attention_probs.astype(jnp.bfloat16),
        mixed_grad,
        preferred_element_type=jnp.float32,
    )
    score_grad = attention_probs * (
        prob_grad - jnp.sum(attention_probs * prob_grad, axis=-1, keepdims=True)
    )
    score_grad = score_grad.astype(jnp.bfloat16)
    query_grad = (
        jnp.einsum("hqk,khd->qhd", score_grad, key_rows, preferred_element_type=jnp.float32)
        * scaling
    )
    key_grad = (
        jnp.einsum("hqk,qhd->khd", score_grad, queries, preferred_element_type=jnp.float32)
        * scaling
    )
    return (
        query_grad.astype(jnp.bfloat16),
        key_grad.astype(jnp.bfloat16),
        value_grad.astype(jnp.bfloat16),
    )


f32 = jnp.float32
bf16 = jnp.bfloat16
GELU_SCALE = 0.7978845608028654
GELU_CUBE = 0.044715
BIAS_ROWS = 16


def slot_columns(alive, route_pair, order_key, experts, capacity, padded, own):
    earlier = (order_key[None, :] < order_key[:, None]).astype(bf16)
    columns = lax.broadcasted_iota(jnp.int32, (1, experts), 1)
    first_pick = ((route_pair[:, 0:1] == columns) & alive[:, None]).astype(f32)
    second = ((route_pair[:, 1:2] == columns) & alive[:, None]).astype(f32)
    both = jnp.concatenate([first_pick, second], axis=1).astype(bf16)
    ahead = jnp.dot(earlier, both, preferred_element_type=f32)
    place_first = jnp.sum(ahead[:, :experts] * first_pick, axis=1)
    already = jnp.sum(first_pick, axis=0, keepdims=True)
    place_second = jnp.sum((ahead[:, experts:] + already) * second, axis=1)
    slots = lax.broadcasted_iota(jnp.int32, (1, experts * padded), 1)

    def one_table(route_col, position, onehot):
        kept_mask = alive & (position < capacity)
        target = jnp.where(kept_mask, (route_col ^ own) * padded + position.astype(jnp.int32), -1)
        spread = (slots == target[:, None]).astype(bf16)
        return (spread, onehot * kept_mask[:, None].astype(f32))

    spread_first, first_kept = one_table(route_pair[:, 0], place_first, first_pick)
    spread_second, second_kept = one_table(route_pair[:, 1], place_second, second)
    return (first_pick, second, spread_first, spread_second, first_kept, second_kept)


def dot_nt(a, b):
    return lax.dot_general(a, b, (((1,), (1,)), ((), ())), preferred_element_type=f32)


def dot_tn(a, b):
    return lax.dot_general(a, b, (((0,), (0,)), ((), ())), preferred_element_type=f32)


def expert_kernel(first, last, *refs):
    refs = list(refs)
    x_ref, g_ref, in_ref, out_ref = refs[:4]
    del refs[:4]
    if first:
        router_ref, pick_ref = refs[:2]
        del refs[:2]
    else:
        made_ref, back_ref = refs[:2]
        del refs[:2]
    if first:
        slot_ref = refs.pop(0)
    prod_ref, ig_ref, gin_ref, gout_ref, gin, gout, gbias = refs
    step = pl.program_id(0)
    width = x_ref.shape[1]

    @pl.when(step == 0)
    def _():
        gin[...] = jnp.zeros_like(gin)
        gout[...] = jnp.zeros_like(gout)
        gbias[...] = jnp.zeros_like(gbias)

    x = x_ref[...]
    if first:
        logits = jnp.dot(x, router_ref[...], preferred_element_type=f32) + pick_ref[0:1, :]
        weights = jnp.exp(logits - jnp.max(logits, axis=1, keepdims=True))
        own = jnp.sum(weights * pick_ref[1:2, :], axis=1, keepdims=True)
        gate = own / jnp.sum(weights, axis=1, keepdims=True)
        slot_grad = (gate * g_ref[...].astype(f32)).astype(bf16)
        slot_ref[...] = slot_grad
    else:
        slot_grad = g_ref[...]
    w_in = in_ref[0:width, :]
    bias = in_ref[width : width + BIAS_ROWS, :].astype(f32)[0:1, :]
    v = jnp.dot(x, w_in, preferred_element_type=f32) + bias
    square = v * v
    t = jnp.tanh(GELU_SCALE * v * (1.0 + GELU_CUBE * square))
    half = 0.5 * (1.0 + t)
    hidden = (v * half).astype(bf16)
    slope = half + 0.5 * v * (1.0 - t * t) * (GELU_SCALE * (1.0 + 3.0 * GELU_CUBE * square))
    made = jnp.dot(hidden, out_ref[...], preferred_element_type=f32)
    before_grad = dot_nt(slot_grad, out_ref[...]) * slope
    before_grad_b = before_grad.astype(bf16)
    back = dot_nt(before_grad_b, w_in)
    if not first:
        made = made + made_ref[...]
        back = back + back_ref[...]
    prod_ref[...] = made.astype(prod_ref.dtype)
    ig_ref[...] = back.astype(ig_ref.dtype)
    gin[...] += dot_tn(x, before_grad_b)
    gout[...] += dot_tn(hidden, slot_grad)
    gbias[0:1, :] += jnp.sum(before_grad_b.astype(f32), axis=0, keepdims=True)

    @pl.when(step == pl.num_programs(0) - 1)
    def _():
        gin_ref[0:width, :] = gin[...].astype(gin_ref.dtype)
        gout_ref[...] = gout[...].astype(gout_ref.dtype)
        gin_ref[width : width + BIAS_ROWS, :] = jnp.broadcast_to(
            gbias[0:1, :], (BIAS_ROWS, gbias.shape[1])
        ).astype(gin_ref.dtype)


def expert_step(first, last, grad_type, x, g, w_in, w_out, extra):
    rows, width = x.shape
    block = 256 if rows % 256 == 0 else 128
    steps = rows // block
    hid = w_out.shape[0]
    row_spec = pl.BlockSpec((block, width), lambda i: (i, 0))
    whole = lambda a: pl.BlockSpec(a.shape, lambda i: (0, 0))
    in_specs = [row_spec, row_spec, whole(w_in), whole(w_out)]
    outs = []
    specs = []
    if first:
        in_specs += [whole(extra[0]), whole(extra[1])]
        outs.append(jax.ShapeDtypeStruct((rows, width), bf16))
        specs.append(row_spec)
    else:
        in_specs += [row_spec, row_spec]
    acc_type = bf16 if last else f32
    outs += [jax.ShapeDtypeStruct((rows, width), acc_type)] * 2
    outs += [
        jax.ShapeDtypeStruct((width + BIAS_ROWS, hid), grad_type),
        jax.ShapeDtypeStruct((hid, width), grad_type),
    ]
    specs += [row_spec, row_spec]
    specs += [
        pl.BlockSpec((width + BIAS_ROWS, hid), lambda i: (0, 0)),
        pl.BlockSpec((hid, width), lambda i: (0, 0)),
    ]
    return pl.pallas_call(
        partial(expert_kernel, first, last),
        grid=(steps,),
        in_specs=in_specs,
        out_specs=specs,
        out_shape=outs,
        scratch_shapes=[
            pltpu.VMEM((width, hid), f32),
            pltpu.VMEM((hid, width), f32),
            pltpu.VMEM((8, hid), f32),
        ],
        compiler_params=pltpu.CompilerParams(
            vmem_limit_bytes=40 * 1024 * 1024, dimension_semantics=("arbitrary",)
        ),
        cost_estimate=pl.CostEstimate(
            flops=12 * rows * width * hid,
            bytes_accessed=20 * rows * width,
            transcendentals=rows * hid,
        ),
        name="expert_step",
    )(x, g, w_in, w_out, *extra)


def place_kernel(order_ref, src_ref, dst_ref):
    base = pl.program_id(0) * dst_ref.shape[0]
    for j in range(dst_ref.shape[0]):
        dst_ref[j] = src_ref[order_ref[base + j]].astype(f32)


def put_in_place(pieces, order, group):
    count, rows, width = pieces.shape
    return pl.pallas_call(
        place_kernel,
        grid_spec=pltpu.PrefetchScalarGridSpec(
            num_scalar_prefetch=1,
            grid=(count // group,),
            in_specs=[pl.BlockSpec((count, rows, width), lambda i, o: (0, 0, 0))],
            out_specs=pl.BlockSpec((group, rows, width), lambda i, o: (i, 0, 0)),
        ),
        out_shape=jax.ShapeDtypeStruct((count, rows, width), f32),
        compiler_params=pltpu.CompilerParams(
            vmem_limit_bytes=32 * 1024 * 1024, dimension_semantics=("arbitrary",)
        ),
        name="put_in_place",
    )(order, pieces)


class Links:
    def __init__(self, wide, narrow):
        self.wide, self.narrow = wide, narrow
        self.chips = wide // 2
        self.w = lax.axis_index("wide")
        self.z = lax.axis_index("narrow")

    def swap(self, x, k):
        return lax.ppermute(x, "wide", [(i, i ^ k) for i in range(self.wide)])

    def shift(self, x, k=1):
        n = self.narrow
        return lax.ppermute(x, "narrow", [(i, (i + k) % n) for i in range(n)])

    def exchange(self, blocks):
        got = [blocks[0:1]] + [self.swap(blocks[k : k + 1], k) for k in range(1, self.wide)]
        return jnp.concatenate(got, axis=0)

    def sum_all(self, x):
        rows, d = x.shape
        core, chip = self.w & 1, self.w >> 1
        pick = lambda a, i: lax.dynamic_index_in_dim(a, i, 0, keepdims=False)
        x = x.astype(bf16).reshape(2, rows // 2, d)
        y = pick(x, core).astype(f32) + self.swap(pick(x, 1 - core), 1).astype(f32)
        y = y.astype(bf16).reshape(self.chips, rows // self.wide, d)
        total = pick(y, chip).astype(f32)
        for k in range(1, self.chips):
            total = total + self.swap(pick(y, chip ^ k), 2 * k).astype(f32)
        n = self.narrow
        total = total.astype(bf16).reshape(n, rows // (self.wide * n), d)
        part = pick(total, self.z).astype(f32)
        for k in range(1, n):
            part = part + self.shift(pick(total, (self.z + k) % n), k).astype(f32)
        part = part.astype(bf16)
        pieces = jnp.stack([part] + [self.shift(part, k) for k in range(1, n)])
        pieces = jnp.stack([pieces] + [self.swap(pieces, 2 * k) for k in range(1, self.chips)])
        pieces = jnp.stack([pieces, self.swap(pieces, 1)])
        pieces = pieces.reshape((self.wide * n,) + part.shape)
        place = jnp.arange(self.wide * n, dtype=jnp.int32)
        c, ch, j = place // (self.chips * n), (place // n) % self.chips, place % n
        order = ((c ^ core) * self.chips + (ch ^ chip)) * n + (self.z - j) % n
        return put_in_place(pieces, order.astype(jnp.int32), n).reshape(rows, d)

    def sum_small(self, x):
        k = 1
        while k < self.wide:
            x = x + self.swap(x, k)
            k *= 2
        return x + sum(self.shift(x, k) for k in range(1, self.narrow))


def local(
    wide,
    narrow,
    tokens,
    live_mask,
    routes,
    priority,
    cotangent,
    first_gain,
    first_shift,
    query_weight,
    query_bias,
    key_weight,
    value_weight,
    value_bias,
    out_weight,
    out_bias,
    second_gain,
    second_shift,
    router_weight,
    expert_in,
    expert_in_bias,
    expert_out,
    expert_out_bias,
):
    links = Links(wide, narrow)
    sequences, patches, features = tokens.shape
    patches_dev = sequences * patches
    experts = expert_out_bias.shape[0]
    capacity = max(2, (210 * patches_dev + 100 * experts - 1) // (100 * experts))
    padded = (capacity + 15) // 16 * 16
    scaling = HEAD_DIM ** (-0.5)
    head_shape = (patches, HEADS, HEAD_DIM)

    bias_rows = jnp.broadcast_to(expert_in_bias, (BIAS_ROWS, expert_in_bias.shape[1]))
    weights_in = [jnp.concatenate([expert_in[0], bias_rows], axis=0)]
    weights_out = [expert_out[0]]
    for _ in range(1, narrow):
        weights_in.append(links.shift(weights_in[-1]))
        weights_out.append(links.shift(weights_out[-1]))

    order_key = (
        priority * sequences + lax.broadcasted_iota(jnp.int32, (sequences, patches), 0)
    ).reshape(patches_dev)
    first_pick, second, spread_first, spread_second, first_kept, second_kept = slot_columns(
        live_mask.reshape(patches_dev) > 0,
        routes.reshape(patches_dev, 2),
        order_key,
        experts,
        capacity,
        padded,
        links.w,
    )
    spread = spread_first + spread_second

    def to_slots(rows):
        return dot_tn(spread, rows).astype(bf16).reshape(experts, padded, features)

    upstream_b = cotangent.reshape(patches_dev, features)
    up_slots = links.exchange(to_slots(upstream_b)).reshape(experts * padded, features)

    inputs = tokens.astype(f32).reshape(patches_dev, features)
    normed = layer_norm(inputs, first_gain, first_shift).astype(bf16)
    queries = (jnp.dot(normed, query_weight, preferred_element_type=f32) + query_bias).astype(bf16)
    key_rows = jnp.dot(normed, key_weight, preferred_element_type=f32).astype(bf16)
    value_rows = (jnp.dot(normed, value_weight, preferred_element_type=f32) + value_bias).astype(
        bf16
    )
    queries = queries.reshape(head_shape)
    key_rows = key_rows.reshape(head_shape)
    value_rows = value_rows.reshape(head_shape)
    mixed_heads, log_total = attend_forward(queries, key_rows, value_rows, live_mask[0], scaling)
    mixed_heads = mixed_heads.reshape(patches_dev, features)
    residual = inputs + jnp.dot(mixed_heads, out_weight, preferred_element_type=f32) + out_bias
    second_normed = layer_norm(residual, second_gain, second_shift).astype(bf16)
    logits = jnp.dot(second_normed, router_weight, preferred_element_type=f32)
    chance = jax.nn.softmax(logits, axis=-1)

    arrived = links.exchange(to_slots(second_normed)).reshape(experts * padded, features)

    router_wide = jnp.pad(router_weight, ((0, 0), (0, 128 - experts)))
    lanes = jnp.arange(128)
    pick_rows = jnp.stack(
        [jnp.where(lanes < experts, 0.0, -1e30), (lanes == links.w).astype(f32)] + [jnp.zeros(128)] * 6
    ).astype(f32)

    grads = []
    for s in range(narrow):
        grad_type = bf16 if s == 1 else f32
        if s == 0:
            slot_grad, made, back, gin, gout = expert_step(
                True, narrow == 1, grad_type, arrived, up_slots, weights_in[0], weights_out[0],
                (router_wide, pick_rows),
            )
        else:
            made, back, gin, gout = expert_step(
                False, s == narrow - 1, grad_type, arrived, slot_grad, weights_in[s], weights_out[s],
                (made, back),
            )
        grads.append((gin, gout))

    def collect(i):
        moving = grads[1][i]
        for s in range(2, narrow):
            moving = (links.shift(moving).astype(f32) + grads[s][i]).astype(bf16)
        return links.shift(moving).astype(f32) + grads[0][i]

    in_sum, out_sum = collect(0), collect(1)
    expert_in_grad = in_sum[None, :features]
    expert_in_bias_grad = in_sum[features : features + 1]
    expert_out_grad = out_sum[None]

    gate_dots = jnp.sum(made.astype(f32) * up_slots.astype(f32), axis=1).reshape(experts, padded)
    dots_high = gate_dots.astype(bf16)
    dots_low = (gate_dots - dots_high.astype(f32)).astype(bf16)
    dot_rows = jnp.pad(jnp.stack([dots_high, dots_low], axis=1), ((0, 0), (0, 0), (0, features - padded)))
    back = back.reshape(experts, padded, features)
    back = jnp.concatenate(
        [back[:, :capacity], dot_rows, jnp.zeros((experts, padded - capacity - 2, features), bf16)], axis=1
    )
    back_tokens = links.exchange(back)
    returned = links.exchange(made.reshape(experts, padded, features)).reshape(
        experts * padded, features
    )

    upstream = upstream_b.astype(f32)
    gate_first = jnp.sum(chance * first_pick, axis=1, keepdims=True)
    gate_second = jnp.sum(chance * second, axis=1, keepdims=True)
    slot_dots = back_tokens[:, capacity, :padded].astype(f32) + back_tokens[
        :, capacity + 1, :padded
    ].astype(f32)
    slot_dots = slot_dots.reshape(1, experts * padded)
    bias_dots = jnp.dot(upstream, expert_out_bias.T, precision=highest)
    gate_first_grad = jnp.sum(spread_first * slot_dots, axis=1, keepdims=True) + jnp.sum(
        first_kept * bias_dots, axis=1, keepdims=True
    )
    gate_second_grad = jnp.sum(spread_second * slot_dots, axis=1, keepdims=True) + jnp.sum(
        second_kept * bias_dots, axis=1, keepdims=True
    )
    out_bias_sum = jnp.dot(
        (gate_first * first_kept + gate_second * second_kept).T, upstream, precision=highest
    )
    chance_grad = first_pick * gate_first_grad + second * gate_second_grad
    logit_grad = chance * (chance_grad - jnp.sum(chance * chance_grad, axis=1, keepdims=True))
    logit_grad = logit_grad.astype(bf16)
    router_sum = jnp.dot(second_normed.T, logit_grad, preferred_element_type=f32)
    second_normed_grad = jnp.dot(logit_grad, router_weight.T, preferred_element_type=f32)
    second_normed_grad = second_normed_grad + jnp.dot(
        spread, back_tokens.reshape(experts * padded, features), preferred_element_type=f32
    )
    unused, second_back = jax.vjp(layer_norm, residual, second_gain, second_shift)
    residual_part, second_gain_grad, second_shift_grad = second_back(second_normed_grad)
    residual_grad = upstream + residual_part
    attended_grad = residual_grad.astype(bf16)
    out_bias_grad = jnp.sum(attended_grad.astype(f32), axis=0)
    out_weight_grad = jnp.dot(mixed_heads.T, attended_grad, preferred_element_type=f32)
    mixed_grad = jnp.dot(attended_grad, out_weight.T, preferred_element_type=f32).astype(bf16)

    out_weight_total = links.sum_all(out_weight_grad)

    query_grad, key_grad, value_grad = attend_backward(
        queries, key_rows, value_rows, live_mask[0], log_total, mixed_grad.reshape(head_shape), scaling
    )
    query_grad = query_grad.reshape(patches_dev, features)
    key_grad = key_grad.reshape(patches_dev, features)
    value_grad = value_grad.reshape(patches_dev, features)
    query_bias_grad = jnp.sum(query_grad.astype(f32), axis=0)
    value_bias_grad = jnp.sum(value_grad.astype(f32), axis=0)
    projection_grads = jnp.concatenate(
        [
            jnp.dot(normed.T, query_grad, preferred_element_type=f32),
            jnp.dot(normed.T, key_grad, preferred_element_type=f32),
            jnp.dot(normed.T, value_grad, preferred_element_type=f32),
        ],
        axis=0,
    )
    projection_total = links.sum_all(projection_grads).reshape(3, features, features)
    normed_grad = dot_nt(query_grad, query_weight)
    normed_grad = normed_grad + dot_nt(key_grad, key_weight)
    normed_grad = normed_grad + dot_nt(value_grad, value_weight)
    unused, first_back = jax.vjp(layer_norm, inputs, first_gain, first_shift)
    input_part, first_gain_grad, first_shift_grad = first_back(normed_grad)
    tokens_grad = (residual_grad + input_part).reshape(sequences, patches, features)

    picked_first = jnp.dot(spread_first, returned, preferred_element_type=f32)
    picked_second = jnp.dot(spread_second, returned, preferred_element_type=f32)
    gated_bias = jnp.dot(
        gate_first * first_kept + gate_second * second_kept, expert_out_bias, precision=highest
    )
    output = residual + gate_first * picked_first + gate_second * picked_second + gated_bias
    output = output.astype(bf16).reshape(sequences, patches, features)

    vectors = jnp.stack(
        [first_gain_grad, first_shift_grad, query_bias_grad, value_bias_grad, out_bias_grad,
         second_gain_grad, second_shift_grad]
    )
    small = jnp.concatenate([vectors, jnp.zeros((1, features), f32), router_sum.T, out_bias_sum], axis=0)
    small = links.sum_small(small)
    return (
        output,
        tokens_grad,
        small[0],
        small[1],
        projection_total[0],
        small[2],
        projection_total[1],
        projection_total[2],
        small[3],
        out_weight_total,
        small[4],
        small[5],
        small[6],
        small[8 : 8 + experts].T,
        expert_in_grad,
        expert_in_bias_grad,
        expert_out_grad,
        small[8 + experts : 8 + 2 * experts],
    )


def solution(mesh):
    return jax.shard_map(
        partial(local, mesh.shape["wide"], mesh.shape["narrow"]),
        mesh=mesh,
        in_specs=(
            P(("wide", "narrow"), None, None),
            P(("wide", "narrow"), None),
            P(("wide", "narrow"), None, None),
            P(("wide", "narrow"), None),
            P(("wide", "narrow"), None, None),
            P(),
            P(),
            P(),
            P(),
            P(),
            P(),
            P(),
            P(),
            P(),
            P(),
            P(),
            P(),
            P("wide", None, "narrow"),
            P("wide", "narrow"),
            P("wide", "narrow", None),
            P(),
        ),
        out_specs=(
            P(("wide", "narrow"), None, None),
            P(("wide", "narrow"), None, None),
            P(),
            P(),
            P(),
            P(),
            P(),
            P(),
            P(),
            P(),
            P(),
            P(),
            P(),
            P(),
            P("wide", None, "narrow"),
            P("wide", "narrow"),
            P("wide", "narrow", None),
            P(),
        ),
        check_vma=False,
    )
```

```python
from functools import partial

import jax
import jax.numpy as jnp
from jax import lax
from jax.experimental import pallas as pl
from jax.experimental.pallas import tpu as pltpu
from jax.sharding import PartitionSpec as P

HEADS = 12
HEAD_DIM = 64


epsilon = 1e-06
highest = lax.Precision.HIGHEST


def layer_norm(source, gain_vec, shift_vec):
    average = jnp.mean(source, axis=-1, keepdims=True)
    centred = source - average
    variance = jnp.mean(centred * centred, axis=-1, keepdims=True)
    return centred * lax.rsqrt(variance + epsilon) * gain_vec + shift_vec


f32 = jnp.float32
bf16 = jnp.bfloat16
GELU_SCALE = 0.7978845608028654
GELU_CUBE = 0.044715
BIAS_ROWS = 16


def slot_columns(alive, route_pair, order_key, experts, capacity, padded):
    earlier = (order_key[None, :] < order_key[:, None]).astype(bf16)
    columns = lax.broadcasted_iota(jnp.int32, (1, experts), 1)
    first_pick = ((route_pair[:, 0:1] == columns) & alive[:, None]).astype(f32)
    second = ((route_pair[:, 1:2] == columns) & alive[:, None]).astype(f32)
    both = jnp.concatenate([first_pick, second], axis=1).astype(bf16)
    ahead = jnp.dot(earlier, both, preferred_element_type=f32)
    place_first = jnp.sum(ahead[:, :experts] * first_pick, axis=1)
    already = jnp.sum(first_pick, axis=0, keepdims=True)
    place_second = jnp.sum((ahead[:, experts:] + already) * second, axis=1)
    slots = lax.broadcasted_iota(jnp.int32, (1, experts * padded), 1)

    def one_table(route_col, position, onehot):
        kept_mask = alive & (position < capacity)
        target = jnp.where(kept_mask, route_col * padded + position.astype(jnp.int32), -1)
        spread = (slots == target[:, None]).astype(bf16)
        return (spread, onehot * kept_mask[:, None].astype(f32))

    spread_first, first_kept = one_table(route_pair[:, 0], place_first, first_pick)
    spread_second, second_kept = one_table(route_pair[:, 1], place_second, second)
    return (first_pick, second, spread_first, spread_second, first_kept, second_kept)


def dot_nt(a, b):
    return lax.dot_general(a, b, (((1,), (1,)), ((), ())), preferred_element_type=f32)


def dot_tn(a, b):
    return lax.dot_general(a, b, (((0,), (0,)), ((), ())), preferred_element_type=f32)


def expert_kernel(first, last, block_ref, *refs):
    refs = list(refs)
    x_ref, g_ref, in_ref, out_ref = refs[:4]
    del refs[:4]
    if first:
        router_ref, pick_ref = refs[:2]
        del refs[:2]
    else:
        made_ref, back_ref = refs[:2]
        del refs[:3]
    if first:
        slot_ref = refs.pop(0)
    prod_ref, ig_ref, grad_ref, gin, gout, gbias = refs
    step = pl.program_id(0)
    width = x_ref.shape[1]

    @pl.when(step == 0)
    def _():
        gin[...] = jnp.zeros_like(gin)
        gout[...] = jnp.zeros_like(gout)
        gbias[...] = jnp.zeros_like(gbias)

    x = x_ref[...]
    if first:
        logits = jnp.dot(x, router_ref[...], preferred_element_type=f32) + pick_ref[0:1, :]
        weights = jnp.exp(logits - jnp.max(logits, axis=1, keepdims=True))
        own = jnp.sum(weights * pick_ref[1:2, :], axis=1, keepdims=True)
        gate = own / jnp.sum(weights, axis=1, keepdims=True)
        slot_grad = (gate * g_ref[...].astype(f32)).astype(bf16)
        slot_ref[...] = slot_grad
    else:
        slot_grad = g_ref[...]
    below = width + BIAS_ROWS
    w_in = in_ref[0:width, :]
    bias = in_ref[width:below, :].astype(f32)[0:1, :]
    w_out = out_ref[...]
    v = jnp.dot(x, w_in, preferred_element_type=f32) + bias
    square = v * v
    t = jnp.tanh(GELU_SCALE * v * (1.0 + GELU_CUBE * square))
    half = 0.5 * (1.0 + t)
    hidden = (v * half).astype(bf16)
    slope = half + 0.5 * v * (1.0 - t * t) * (GELU_SCALE * (1.0 + 3.0 * GELU_CUBE * square))
    made = jnp.dot(hidden, w_out, preferred_element_type=f32)
    before_grad = dot_nt(slot_grad, w_out) * slope
    before_grad_b = before_grad.astype(bf16)
    back = dot_nt(before_grad_b, w_in)
    if not first:
        made = made + made_ref[...]
        back = back + back_ref[...]
    prod_ref[...] = made.astype(prod_ref.dtype)
    ig_ref[...] = back.astype(ig_ref.dtype)
    gin[...] += dot_tn(x, before_grad_b)
    gout[...] += dot_tn(hidden, slot_grad)
    gbias[0:1, :] += jnp.sum(before_grad_b.astype(f32), axis=0, keepdims=True)

    @pl.when(step == pl.num_programs(0) - 1)
    def _():
        grad_ref[0, 0:width, :] = gin[...].astype(grad_ref.dtype)
        grad_ref[0, below : below + width, :] = gout[...].astype(grad_ref.dtype)
        grad_ref[0, width:below, :] = jnp.broadcast_to(
            gbias[0:1, :], (BIAS_ROWS, gbias.shape[1])
        ).astype(grad_ref.dtype)


def expert_step(first, last, count, block, x, g, weights, extra):
    rows, width = x.shape
    tile = 256 if rows % 256 == 0 else 128
    steps = rows // tile
    row_spec = pl.BlockSpec((tile, width), lambda i, b: (i, 0))
    whole = lambda a: pl.BlockSpec(a.shape, lambda i, b: (0, 0))
    in_specs = [row_spec, row_spec, whole(weights[0]), whole(weights[1])]
    outs = []
    specs = []
    if first:
        in_specs += [whole(extra[0]), whole(extra[1])]
        outs.append(jax.ShapeDtypeStruct((rows, width), bf16))
        specs.append(row_spec)
        aliases = {}
    else:
        in_specs += [row_spec, row_spec, pl.BlockSpec(memory_space=pl.ANY)]
        aliases = {7: 2}
    acc_type = bf16 if last else f32
    outs += [jax.ShapeDtypeStruct((rows, width), acc_type)] * 2
    height = weights[0].shape[0] + width
    outs.append(jax.ShapeDtypeStruct((count, height, width), bf16))
    specs += [row_spec, row_spec, pl.BlockSpec((1, height, width), lambda i, b: (b[0], 0, 0))]
    return pl.pallas_call(
        partial(expert_kernel, first, last),
        grid_spec=pltpu.PrefetchScalarGridSpec(
            num_scalar_prefetch=1,
            grid=(steps,),
            in_specs=in_specs,
            out_specs=specs,
            scratch_shapes=[
                pltpu.VMEM((width, width), f32),
                pltpu.VMEM((width, width), f32),
                pltpu.VMEM((8, width), f32),
            ],
        ),
        out_shape=outs,
        input_output_aliases=aliases,
        compiler_params=pltpu.CompilerParams(
            vmem_limit_bytes=60 * 1024 * 1024, dimension_semantics=("arbitrary",)
        ),
        cost_estimate=pl.CostEstimate(flops=width, bytes_accessed=width, transcendentals=0),
        name="expert_step",
    )(block, x, g, *weights, *extra)


GROUP = 256


def lane_half(x, h):
    lanes = lax.broadcasted_iota(jnp.int32, (1, x.shape[1]), 1)
    inside = (lanes >= HEAD_DIM) if h else (lanes < HEAD_DIM)
    return jnp.where(inside, x, jnp.zeros_like(x))


def moments(x):
    average = jnp.mean(x, axis=1, keepdims=True)
    centred = x - average
    scale = lax.rsqrt(jnp.mean(centred * centred, axis=1, keepdims=True) + epsilon)
    return centred * scale, scale


def attend_kernel(
    tok_ref, vec_ref, wq_ref, wk_ref, wv_ref, qv_ref, wo_ref, mask_ref,
    n_ref, q_ref, k_ref, v_ref, m_ref, lse_ref, res_ref, sn_ref, acc,
):
    g = pl.program_id(0)

    @pl.when(g == 0)
    def _():
        tok = tok_ref[...].astype(f32)
        hat, _ = moments(tok)
        n_ref[...] = (hat * vec_ref[0:1, :] + vec_ref[1:2, :]).astype(bf16)
        acc[...] = tok + vec_ref[2:3, :]

    normed = n_ref[...]
    q = (jnp.dot(normed, wq_ref[...], preferred_element_type=f32) + qv_ref[0:1, :]).astype(bf16)
    k = jnp.dot(normed, wk_ref[...], preferred_element_type=f32).astype(bf16)
    v = (jnp.dot(normed, wv_ref[...], preferred_element_type=f32) + qv_ref[1:2, :]).astype(bf16)
    q_ref[...] = q
    k_ref[...] = k
    v_ref[...] = v
    rows = q.shape[0]
    lanes = lax.broadcasted_iota(jnp.int32, (1, 128), 1)
    lse_all = jnp.zeros((rows, 128), f32)
    mixed = []
    for p in range(GROUP // 128):
        at = slice(128 * p, 128 * p + 128)
        qp, kp, vp = q[:, at], k[:, at], v[:, at]
        pair = None
        for h in range(2):
            scores = dot_nt(lane_half(qp, h), kp) * HEAD_DIM**-0.5 + mask_ref[0:1, :]
            top = jnp.max(scores, axis=1, keepdims=True)
            weights = jnp.exp(scores - top)
            total = jnp.sum(weights, axis=1, keepdims=True)
            part = jnp.dot(weights.astype(bf16), lane_half(vp, h), preferred_element_type=f32)
            part = part * (1.0 / total)
            pair = part if pair is None else pair + part
            lse_all = jnp.where(lanes == 2 * p + h, top + jnp.log(total), lse_all)
        mixed.append(pair.astype(bf16))
    lse_ref[...] = lse_all.T[0:8, :]
    mixed = jnp.concatenate(mixed, axis=1)
    m_ref[...] = mixed
    acc[...] += jnp.dot(mixed, wo_ref[...], preferred_element_type=f32)

    @pl.when(g == pl.num_programs(0) - 1)
    def _():
        residual = acc[...]
        hat, _ = moments(residual)
        res_ref[...] = residual
        sn_ref[...] = (hat * vec_ref[3:4, :] + vec_ref[4:5, :]).astype(bf16)


def attend_forward(tok, vecs, wq, wk, wv, qv, wo, mask_row):
    rows, width = tok.shape
    groups = width // GROUP
    whole = lambda a: pl.BlockSpec(a.shape, lambda g: (0, 0))
    by_col = lambda r: pl.BlockSpec((r, GROUP), lambda g: (0, g))
    full = pl.BlockSpec((rows, width), lambda g: (0, 0))
    act = jax.ShapeDtypeStruct((rows, width), bf16)
    return pl.pallas_call(
        attend_kernel,
        grid=(groups,),
        in_specs=[
            whole(tok), whole(vecs), by_col(width), by_col(width), by_col(width), by_col(8),
            pl.BlockSpec((GROUP, width), lambda g: (g, 0)), whole(mask_row),
        ],
        out_specs=[
            full, by_col(rows), by_col(rows), by_col(rows), by_col(rows),
            pl.BlockSpec((8, rows), lambda g: (g, 0)), full, full,
        ],
        out_shape=[
            act, act, act, act, act, jax.ShapeDtypeStruct((8 * groups, rows), f32),
            jax.ShapeDtypeStruct((rows, width), f32), act,
        ],
        scratch_shapes=[pltpu.VMEM((rows, width), f32)],
        compiler_params=pltpu.CompilerParams(
            vmem_limit_bytes=60 * 1024 * 1024, dimension_semantics=("arbitrary",)
        ),
        cost_estimate=pl.CostEstimate(
            flops=width, bytes_accessed=width, transcendentals=0
        ),
        name="attend_forward",
    )(tok, vecs, wq, wk, wv, qv, wo, mask_row)


def attend_back_kernel(
    tok_ref, vec_ref, n_ref, q_ref, k_ref, v_ref, lse_ref, mask_ref, ag_ref, rg_ref,
    wq_ref, wk_ref, wv_ref, wo_ref,
    dq_ref, dk_ref, dv_ref, db_ref, tg_ref, ln_ref, acc,
):
    g = pl.program_id(0)
    mixed_grad = dot_nt(ag_ref[...], wo_ref[...]).astype(bf16)
    scale = HEAD_DIM**-0.5
    out = [[], [], []]
    for p in range(GROUP // 128):
        at = slice(128 * p, 128 * p + 128)
        qp, kp, vp, dp = q_ref[:, at], k_ref[:, at], v_ref[:, at], mixed_grad[:, at]
        dq_t = dk = dv = None
        for h in range(2):
            qh, kh, dh = lane_half(qp, h), lane_half(kp, h), lane_half(dp, h)
            row = 2 * p + h
            scores = dot_nt(kp, qh) * scale + mask_ref[...]
            probs = jnp.exp(scores - lse_ref[row : row + 1, :])
            prob_grad = dot_nt(vp, dh)
            across = jnp.sum(probs * prob_grad, axis=0, keepdims=True)
            score_grad = (probs * (prob_grad - across)).astype(bf16)
            dv_h = jnp.dot(probs.astype(bf16), dh, preferred_element_type=f32)
            dk_h = jnp.dot(score_grad, qh, preferred_element_type=f32)
            dq_h = dot_tn(kh, score_grad)
            dv = dv_h if dv is None else dv + dv_h
            dk = dk_h if dk is None else dk + dk_h
            dq_t = dq_h if dq_t is None else dq_t + dq_h
        out[0].append((dq_t.T * scale).astype(bf16))
        out[1].append((dk * scale).astype(bf16))
        out[2].append(dv.astype(bf16))
    normed = n_ref[...]
    total = None
    sums = []
    for i, (w_ref, d_ref) in enumerate(((wq_ref, dq_ref), (wk_ref, dk_ref), (wv_ref, dv_ref))):
        grad = jnp.concatenate(out[i], axis=1)
        d_ref[...] = dot_tn(normed, grad).astype(bf16)
        sums.append(jnp.sum(grad.astype(f32), axis=0, keepdims=True))
        back = dot_nt(grad, w_ref[...])
        total = back if total is None else total + back
    db_ref[0:1, :] = sums[0]
    db_ref[1:2, :] = sums[2]
    db_ref[2:8, :] = jnp.zeros((6, GROUP), f32)

    @pl.when(g == 0)
    def _():
        acc[...] = total

    @pl.when(g > 0)
    def _():
        acc[...] += total

    @pl.when(g == pl.num_programs(0) - 1)
    def _():
        grad = acc[...]
        hat, scale_of = moments(tok_ref[...].astype(f32))
        inner = grad * vec_ref[0:1, :]
        first = jnp.mean(inner, axis=1, keepdims=True)
        other = jnp.mean(inner * hat, axis=1, keepdims=True)
        tg_ref[...] = rg_ref[...] + (inner - first - hat * other) * scale_of
        ln_ref[0:1, :] = jnp.sum(grad * hat, axis=0, keepdims=True)
        ln_ref[1:2, :] = jnp.sum(grad, axis=0, keepdims=True)
        ln_ref[2:8, :] = jnp.zeros((6, grad.shape[1]), f32)


def attend_backward(tok, vecs, n, q, k, v, lse, mask_col, ag, rg, wq, wk, wv, wo):
    rows, width = tok.shape
    groups = width // GROUP
    whole = lambda a: pl.BlockSpec(a.shape, lambda g: (0, 0))
    by_col = lambda r: pl.BlockSpec((r, GROUP), lambda g: (0, g))
    by_row = lambda r, c: pl.BlockSpec((r, c), lambda g: (g, 0))
    full = pl.BlockSpec((rows, width), lambda g: (0, 0))
    return pl.pallas_call(
        attend_back_kernel,
        grid=(groups,),
        in_specs=[
            whole(tok), whole(vecs), whole(n), by_col(rows), by_col(rows), by_col(rows),
            by_row(8, rows), whole(mask_col), whole(ag), whole(rg),
            by_col(width), by_col(width), by_col(width), by_row(GROUP, width),
        ],
        out_specs=[
            by_col(width), by_col(width), by_col(width), by_col(8), full,
            pl.BlockSpec((8, width), lambda g: (0, 0)),
        ],
        out_shape=[
            *[jax.ShapeDtypeStruct((width, width), bf16)] * 3,
            jax.ShapeDtypeStruct((8, width), f32),
            jax.ShapeDtypeStruct((rows, width), f32),
            jax.ShapeDtypeStruct((8, width), f32),
        ],
        scratch_shapes=[pltpu.VMEM((rows, width), f32)],
        compiler_params=pltpu.CompilerParams(
            vmem_limit_bytes=60 * 1024 * 1024, dimension_semantics=("arbitrary",)
        ),
        cost_estimate=pl.CostEstimate(
            flops=width, bytes_accessed=width, transcendentals=0
        ),
        name="attend_backward",
    )(tok, vecs, n, q, k, v, lse, mask_col, ag, rg, wq, wk, wv, wo)


def place_kernel(cuts, order_ref, src_ref, *dst_refs):
    group = dst_refs[0].shape[0]
    base = pl.program_id(0) * group
    for j in range(group):
        piece = src_ref[order_ref[base + j]].astype(f32)
        for dst_ref, (start, stop) in zip(dst_refs, cuts):
            dst_ref[j] = piece[start:stop]


def put_in_place(pieces, order, group, heights):
    count, rows, width = pieces.shape
    cuts = []
    for height in heights:
        start = cuts[-1][1] if cuts else 0
        cuts.append((start, start + height))
    return pl.pallas_call(
        partial(place_kernel, cuts),
        grid_spec=pltpu.PrefetchScalarGridSpec(
            num_scalar_prefetch=1,
            grid=(count // group,),
            in_specs=[pl.BlockSpec((count, rows, width), lambda i, o: (0, 0, 0))],
            out_specs=[pl.BlockSpec((group, h, width), lambda i, o: (i, 0, 0)) for h in heights],
        ),
        out_shape=[jax.ShapeDtypeStruct((count, h, width), f32) for h in heights],
        compiler_params=pltpu.CompilerParams(
            vmem_limit_bytes=60 * 1024 * 1024, dimension_semantics=("arbitrary",)
        ),
        name="put_in_place",
    )(order, pieces)


class Links:
    def __init__(self, wide, narrow):
        self.wide, self.narrow = wide, narrow
        self.chips = wide // 2
        self.w = lax.axis_index("wide")
        self.z = lax.axis_index("narrow")

    def swap(self, x, k):
        return lax.ppermute(x, "wide", [(i, i ^ k) for i in range(self.wide)])

    def shift(self, x, k=1):
        n = self.narrow
        return lax.ppermute(x, "narrow", [(i, (i + k) % n) for i in range(n)])

    def exchange(self, blocks):
        return lax.all_to_all(blocks, "wide", split_axis=0, concat_axis=0, tiled=True)

    def pick(self, a, i):
        return lax.dynamic_index_in_dim(a, i, 0, keepdims=False)

    def scatter_plane(self, x):
        rest = x.shape[1:]
        core, chip = self.w & 1, self.w >> 1
        x = x.reshape((2, -1) + rest)
        y = self.pick(x, core).astype(f32) + self.swap(self.pick(x, 1 - core), 1).astype(f32)
        y = y.astype(bf16).reshape((self.chips, self.narrow) + rest)
        total = self.pick(y, chip).astype(f32)
        for k in range(1, self.chips):
            total = total + self.swap(self.pick(y, chip ^ k), 2 * k).astype(f32)
        return total.astype(bf16)

    def scatter_narrow(self, total):
        n = self.narrow
        part = self.pick(total, self.z).astype(f32)
        for k in range(1, n):
            part = part + self.shift(self.pick(total, (self.z + k) % n), k).astype(f32)
        return part.astype(bf16)

    def gather_narrow(self, part):
        return jnp.stack([part] + [self.shift(part, k) for k in range(1, self.narrow)])

    def gather_plane(self, pieces):
        pieces = jnp.stack([pieces] + [self.swap(pieces, 2 * k) for k in range(1, self.chips)])
        pieces = jnp.stack([pieces, self.swap(pieces, 1)])
        return pieces.reshape((self.wide * self.narrow,) + pieces.shape[3:])

    def order(self):
        n = self.narrow
        core, chip = self.w & 1, self.w >> 1
        place = jnp.arange(self.wide * n, dtype=jnp.int32)
        c, ch, j = place // (self.chips * n), (place // n) % self.chips, place % n
        order = ((c ^ core) * self.chips + (ch ^ chip)) * n + (self.z - j) % n
        return order.astype(jnp.int32)


def after(value, *others):
    return lax.optimization_barrier((value, others))[0]


def local(
    wide,
    narrow,
    tokens,
    live_mask,
    routes,
    priority,
    cotangent,
    first_gain,
    first_shift,
    query_weight,
    query_bias,
    key_weight,
    value_weight,
    value_bias,
    out_weight,
    out_bias,
    second_gain,
    second_shift,
    router_weight,
    expert_in,
    expert_in_bias,
    expert_out,
    expert_out_bias,
):
    links = Links(wide, narrow)
    sequences, patches, features = tokens.shape
    patches_dev = sequences * patches
    experts = expert_out_bias.shape[0]
    capacity = max(2, (210 * patches_dev + 100 * experts - 1) // (100 * experts))
    padded = (capacity + 15) // 16 * 16
    scaling = HEAD_DIM ** (-0.5)
    head_shape = (patches, HEADS, HEAD_DIM)

    bias_rows = jnp.broadcast_to(expert_in_bias, (BIAS_ROWS, expert_in_bias.shape[1]))
    w_in, w_out = expert_in[0], expert_out[0]
    quarter = w_in.shape[1]
    if quarter < features:
        w_in = jnp.pad(w_in, ((0, 0), (0, features - quarter)))
        bias_rows = jnp.pad(bias_rows, ((0, 0), (0, features - quarter)))
        w_out = jnp.pad(w_out, ((0, features - quarter), (0, 0)))
    weights = [(jnp.concatenate([w_in, bias_rows], axis=0), w_out)]
    for _ in range(1, narrow):
        w_in, w_out = weights[-1]
        w_out = links.shift(w_out)
        weights.append((links.shift(w_in), w_out))

    order_key = (
        priority * sequences + lax.broadcasted_iota(jnp.int32, (sequences, patches), 0)
    ).reshape(patches_dev)
    first_pick, second, spread_first, spread_second, first_kept, second_kept = slot_columns(
        live_mask.reshape(patches_dev) > 0,
        routes.reshape(patches_dev, 2),
        order_key,
        experts,
        capacity,
        padded,
    )
    spread = spread_first + spread_second

    def to_slots(rows):
        return dot_tn(spread, rows).astype(bf16).reshape(experts, padded, features)

    upstream_b = cotangent.reshape(patches_dev, features)
    up_sent = to_slots(upstream_b)
    up_slots = links.exchange(up_sent).reshape(experts * padded, features)

    tok = tokens.reshape(patches_dev, features)
    bias = jnp.where(live_mask.reshape(patches_dev) > 0, 0.0, -1e30).astype(f32)
    none = jnp.zeros_like(first_gain)
    vecs = jnp.stack([first_gain, first_shift, out_bias, second_gain, second_shift, none, none, none])
    qv = jnp.stack([query_bias, value_bias] + [none] * 6)
    normed, queries, key_rows, value_rows, mixed_heads, lse, residual, second_normed = attend_forward(
        tok, vecs, query_weight, key_weight, value_weight, qv, out_weight,
        jnp.broadcast_to(bias[None, :], (8, patches_dev)),
    )
    logits = jnp.dot(second_normed, router_weight, preferred_element_type=f32)
    chance = jax.nn.softmax(logits, axis=-1)

    arrived = links.exchange(to_slots(second_normed)).reshape(experts * padded, features)

    router_wide = jnp.pad(router_weight, ((0, 0), (0, 128 - experts)))
    lanes = jnp.arange(128)
    pick_rows = jnp.stack(
        [jnp.where(lanes < experts, 0.0, -1e30), (lanes == links.w).astype(f32)] + [jnp.zeros(128)] * 6
    ).astype(f32)

    for s in range(narrow):
        block = ((links.z - s) % narrow).astype(jnp.int32).reshape(1)
        last = s == narrow - 1
        if s == 0:
            slot_grad, made, back, grads = expert_step(
                True, last, narrow, block, arrived, up_slots, weights[0], (router_wide, pick_rows)
            )
        else:
            made, back, grads = expert_step(
                False, last, narrow, block, arrived, slot_grad, weights[s], (made, back, grads)
            )
    grad_sum = lax.psum_scatter(
        grads.reshape(-1, features), "narrow", scatter_dimension=0, tiled=True
    ).astype(f32)
    below = features + BIAS_ROWS
    expert_in_grad = grad_sum[None, :features, :quarter]
    expert_in_bias_grad = grad_sum[features : features + 1, :quarter]
    expert_out_grad = grad_sum[None, below : below + quarter]

    gate_dots = jnp.sum(made.astype(f32) * up_slots.astype(f32), axis=1).reshape(experts, padded)
    dots_high = gate_dots.astype(bf16)
    dots_low = (gate_dots - dots_high.astype(f32)).astype(bf16)
    dot_rows = jnp.pad(jnp.stack([dots_high, dots_low], axis=1), ((0, 0), (0, 0), (0, features - padded)))
    back = back.reshape(experts, padded, features)
    back = jnp.concatenate(
        [back[:, :capacity], dot_rows, jnp.zeros((experts, padded - capacity - 2, features), bf16)], axis=1
    )
    back_tokens = links.exchange(back)
    returned = links.exchange(made.reshape(experts, padded, features)).reshape(
        experts * padded, features
    )

    upstream = upstream_b.astype(f32)
    gate_first = jnp.sum(chance * first_pick, axis=1, keepdims=True)
    gate_second = jnp.sum(chance * second, axis=1, keepdims=True)
    slot_dots = back_tokens[:, capacity, :padded].astype(f32) + back_tokens[
        :, capacity + 1, :padded
    ].astype(f32)
    slot_dots = slot_dots.reshape(1, experts * padded)
    bias_dots = jnp.dot(upstream, expert_out_bias.T, precision=highest)
    gate_first_grad = jnp.sum(spread_first * slot_dots, axis=1, keepdims=True) + jnp.sum(
        first_kept * bias_dots, axis=1, keepdims=True
    )
    gate_second_grad = jnp.sum(spread_second * slot_dots, axis=1, keepdims=True) + jnp.sum(
        second_kept * bias_dots, axis=1, keepdims=True
    )
    out_bias_sum = jnp.dot(
        (gate_first * first_kept + gate_second * second_kept).T, upstream, precision=highest
    )
    chance_grad = first_pick * gate_first_grad + second * gate_second_grad
    logit_grad = chance * (chance_grad - jnp.sum(chance * chance_grad, axis=1, keepdims=True))
    logit_grad = logit_grad.astype(bf16)
    router_sum = jnp.dot(second_normed.T, logit_grad, preferred_element_type=f32)
    second_normed_grad = jnp.dot(logit_grad, router_weight.T, preferred_element_type=f32)
    second_normed_grad = second_normed_grad + jnp.dot(
        spread, back_tokens.reshape(experts * padded, features), preferred_element_type=f32
    )
    unused, second_back = jax.vjp(layer_norm, residual, second_gain, second_shift)
    residual_part, second_gain_grad, second_shift_grad = second_back(second_normed_grad)
    residual_grad = upstream + residual_part
    attended_grad = residual_grad.astype(bf16)
    out_bias_grad = jnp.sum(attended_grad.astype(f32), axis=0)
    out_weight_grad = jnp.dot(mixed_heads.T, attended_grad, preferred_element_type=f32)
    *projection_grads, bias_grads, tokens_grad, norm_grads = attend_backward(
        tok, vecs, normed, queries, key_rows, value_rows, lse, bias[:, None], attended_grad,
        residual_grad, query_weight, key_weight, value_weight, out_weight,
    )
    parts = wide * narrow
    small = jnp.concatenate(
        [norm_grads[0:2], bias_grads[0:2], out_bias_grad[None], second_gain_grad[None],
         second_shift_grad[None], jnp.zeros((1, features), f32), router_sum.T, out_bias_sum], axis=0
    )
    small_rows = -(-small.shape[0] // (8 * parts)) * 8
    small = jnp.pad(small, ((0, small_rows * parts - small.shape[0]), (0, 0)))
    summands = list(projection_grads) + [out_weight_grad, small]
    summands = [a.astype(bf16).reshape(parts, -1, features) for a in summands]
    heights = [a.shape[1] for a in summands]
    whole = after(jnp.concatenate(summands, axis=1), returned)
    part = links.scatter_narrow(links.scatter_plane(whole))
    pieces = links.gather_plane(links.gather_narrow(part))
    totals = [a.reshape(-1, features) for a in put_in_place(pieces, links.order(), narrow, heights)]
    small = totals[4]
    tokens_grad = tokens_grad.reshape(sequences, patches, features)

    picked_first = jnp.dot(spread_first, returned, preferred_element_type=f32)
    picked_second = jnp.dot(spread_second, returned, preferred_element_type=f32)
    gated_bias = jnp.dot(
        gate_first * first_kept + gate_second * second_kept, expert_out_bias, precision=highest
    )
    output = residual + gate_first * picked_first + gate_second * picked_second + gated_bias
    output = output.astype(bf16).reshape(sequences, patches, features)

    return (
        output,
        tokens_grad,
        small[0],
        small[1],
        totals[0],
        small[2],
        totals[1],
        totals[2],
        small[3],
        totals[3],
        small[4],
        small[5],
        small[6],
        small[8 : 8 + experts].T,
        expert_in_grad,
        expert_in_bias_grad,
        expert_out_grad,
        small[8 + experts : 8 + 2 * experts],
    )


def solution(mesh):
    return jax.shard_map(
        partial(local, mesh.shape["wide"], mesh.shape["narrow"]),
        mesh=mesh,
        in_specs=(
            P(("wide", "narrow"), None, None),
            P(("wide", "narrow"), None),
            P(("wide", "narrow"), None, None),
            P(("wide", "narrow"), None),
            P(("wide", "narrow"), None, None),
            P(),
            P(),
            P(),
            P(),
            P(),
            P(),
            P(),
            P(),
            P(),
            P(),
            P(),
            P(),
            P("wide", None, "narrow"),
            P("wide", "narrow"),
            P("wide", "narrow", None),
            P(),
        ),
        out_specs=(
            P(("wide", "narrow"), None, None),
            P(("wide", "narrow"), None, None),
            P(),
            P(),
            P(),
            P(),
            P(),
            P(),
            P(),
            P(),
            P(),
            P(),
            P(),
            P(),
            P("wide", None, "narrow"),
            P("wide", "narrow"),
            P("wide", "narrow", None),
            P(),
        ),
        check_vma=False,
    )
```

```python
from functools import partial

import jax
import jax.numpy as jnp
from jax import lax
from jax.experimental import pallas as pl
from jax.experimental.pallas import tpu as pltpu
from jax.sharding import PartitionSpec as P

HEADS = 12
HEAD_DIM = 64


epsilon = 1e-06
highest = lax.Precision.HIGHEST


def layer_norm(source, gain_vec, shift_vec):
    average = jnp.mean(source, axis=-1, keepdims=True)
    centred = source - average
    variance = jnp.mean(centred * centred, axis=-1, keepdims=True)
    return centred * lax.rsqrt(variance + epsilon) * gain_vec + shift_vec


f32 = jnp.float32
bf16 = jnp.bfloat16
GELU_SCALE = 0.7978845608028654
GELU_CUBE = 0.044715
BIAS_ROWS = 16


def slot_columns(alive, route_pair, order_key, experts, capacity, padded):
    earlier = (order_key[None, :] < order_key[:, None]).astype(bf16)
    columns = lax.broadcasted_iota(jnp.int32, (1, experts), 1)
    first_pick = ((route_pair[:, 0:1] == columns) & alive[:, None]).astype(f32)
    second = ((route_pair[:, 1:2] == columns) & alive[:, None]).astype(f32)
    both = jnp.concatenate([first_pick, second], axis=1).astype(bf16)
    ahead = jnp.dot(earlier, both, preferred_element_type=f32)
    place_first = jnp.sum(ahead[:, :experts] * first_pick, axis=1)
    already = jnp.sum(first_pick, axis=0, keepdims=True)
    place_second = jnp.sum((ahead[:, experts:] + already) * second, axis=1)
    slots = lax.broadcasted_iota(jnp.int32, (1, experts * padded), 1)

    def one_table(route_col, position, onehot):
        kept_mask = alive & (position < capacity)
        target = jnp.where(kept_mask, route_col * padded + position.astype(jnp.int32), -1)
        spread = (slots == target[:, None]).astype(bf16)
        return (spread, onehot * kept_mask[:, None].astype(f32))

    spread_first, first_kept = one_table(route_pair[:, 0], place_first, first_pick)
    spread_second, second_kept = one_table(route_pair[:, 1], place_second, second)
    return (first_pick, second, spread_first, spread_second, first_kept, second_kept)


def dot_nt(a, b):
    return lax.dot_general(a, b, (((1,), (1,)), ((), ())), preferred_element_type=f32)


def dot_tn(a, b):
    return lax.dot_general(a, b, (((0,), (0,)), ((), ())), preferred_element_type=f32)


def put_dots(padded, made, up_ref, back, ig_ref):
    width = made.shape[1]
    lanes = -(-padded // 128) * 128
    for start in range(0, made.shape[0], padded):
        at = slice(start, start + padded)
        ours = made[at]
        if lanes > padded:
            ours = jnp.concatenate([ours, jnp.zeros((lanes - padded, width), bf16)], axis=0)
        dots = dot_nt(up_ref[at, :], ours)
        row = lax.broadcasted_iota(jnp.int32, dots.shape, 0)
        column = lax.broadcasted_iota(jnp.int32, dots.shape, 1)
        dots = jnp.sum(jnp.where(row == column, dots, 0.0), axis=0, keepdims=True)
        high = dots.astype(bf16).astype(f32)
        blank = jnp.zeros((1, width - lanes), f32)
        place = lax.broadcasted_iota(jnp.int32, (padded, 1), 0)
        rows = jnp.where(place == padded - 2, jnp.concatenate([high, blank], axis=1), back[at])
        rows = jnp.where(place == padded - 1, jnp.concatenate([dots - high, blank], axis=1), rows)
        ig_ref[at, :] = rows.astype(bf16)


def expert_kernel(first, last, padded, block_ref, *refs):
    refs = list(refs)
    x_ref, g_ref, in_ref, out_ref = refs[:4]
    del refs[:4]
    if first:
        router_ref, pick_ref = refs[:2]
        del refs[:2]
    else:
        made_ref, back_ref = refs[:2]
        del refs[:3]
    if last:
        up_ref = g_ref if first else refs.pop(0)
    if first:
        slot_ref = refs.pop(0)
    prod_ref, ig_ref, grad_ref, gin, gout, gbias = refs
    step = pl.program_id(0)
    width = x_ref.shape[1]

    @pl.when(step == 0)
    def _():
        gin[...] = jnp.zeros_like(gin)
        gout[...] = jnp.zeros_like(gout)
        gbias[...] = jnp.zeros_like(gbias)

    x = x_ref[...]
    if first:
        logits = jnp.dot(x, router_ref[...], preferred_element_type=f32) + pick_ref[0:1, :]
        weights = jnp.exp(logits - jnp.max(logits, axis=1, keepdims=True))
        own = jnp.sum(weights * pick_ref[1:2, :], axis=1, keepdims=True)
        gate = own / jnp.sum(weights, axis=1, keepdims=True)
        slot_grad = (gate * g_ref[...].astype(f32)).astype(bf16)
        slot_ref[...] = slot_grad
    else:
        slot_grad = g_ref[...]
    below = width + BIAS_ROWS
    w_in = in_ref[0:width, :]
    bias = in_ref[width:below, :].astype(f32)[0:1, :]
    w_out = out_ref[...]
    v = jnp.dot(x, w_in, preferred_element_type=f32) + bias
    square = v * v
    t = jnp.tanh(GELU_SCALE * v * (1.0 + GELU_CUBE * square))
    half = 0.5 * (1.0 + t)
    hidden = (v * half).astype(bf16)
    slope = half + 0.5 * v * (1.0 - t * t) * (GELU_SCALE * (1.0 + 3.0 * GELU_CUBE * square))
    made = jnp.dot(hidden, w_out, preferred_element_type=f32)
    before_grad = dot_nt(slot_grad, w_out) * slope
    before_grad_b = before_grad.astype(bf16)
    back = dot_nt(before_grad_b, w_in)
    if not first:
        made = made + made_ref[...]
        back = back + back_ref[...]
    made = made.astype(prod_ref.dtype)
    prod_ref[...] = made
    if last:
        put_dots(padded, made, up_ref, back, ig_ref)
    else:
        ig_ref[...] = back
    gin[...] += dot_tn(x, before_grad_b)
    gout[...] += dot_tn(hidden, slot_grad)
    gbias[0:1, :] += jnp.sum(before_grad_b.astype(f32), axis=0, keepdims=True)

    @pl.when(step == pl.num_programs(0) - 1)
    def _():
        grad_ref[0, 0:width, :] = gin[...].astype(grad_ref.dtype)
        grad_ref[0, below : below + width, :] = gout[...].astype(grad_ref.dtype)
        grad_ref[0, width:below, :] = jnp.broadcast_to(
            gbias[0:1, :], (BIAS_ROWS, gbias.shape[1])
        ).astype(grad_ref.dtype)


def expert_step(first, last, padded, count, block, x, g, weights, extra):
    rows, width = x.shape
    tile = rows // 2 if last else 256
    steps = rows // tile
    row_spec = pl.BlockSpec((tile, width), lambda i, b: (i, 0))
    whole = lambda a: pl.BlockSpec(a.shape, lambda i, b: (0, 0))
    in_specs = [row_spec, row_spec, whole(weights[0]), whole(weights[1])]
    outs = []
    specs = []
    if first:
        in_specs += [whole(extra[0]), whole(extra[1])]
        outs.append(jax.ShapeDtypeStruct((rows, width), bf16))
        specs.append(row_spec)
        aliases = {}
    else:
        in_specs += [row_spec, row_spec, pl.BlockSpec(memory_space=pl.ANY)] + [row_spec] * last
        aliases = {7: 2}
    acc_type = bf16 if last else f32
    outs += [jax.ShapeDtypeStruct((rows, width), acc_type)] * 2
    height = weights[0].shape[0] + width
    outs.append(jax.ShapeDtypeStruct((count, height, width), bf16))
    specs += [row_spec, row_spec, pl.BlockSpec((1, height, width), lambda i, b: (b[0], 0, 0))]
    return pl.pallas_call(
        partial(expert_kernel, first, last, padded),
        grid_spec=pltpu.PrefetchScalarGridSpec(
            num_scalar_prefetch=1,
            grid=(steps,),
            in_specs=in_specs,
            out_specs=specs,
            scratch_shapes=[
                pltpu.VMEM((width, width), f32),
                pltpu.VMEM((width, width), f32),
                pltpu.VMEM((8, width), f32),
            ],
        ),
        out_shape=outs,
        input_output_aliases=aliases,
        compiler_params=pltpu.CompilerParams(
            vmem_limit_bytes=60 * 1024 * 1024, dimension_semantics=("arbitrary",)
        ),
        cost_estimate=pl.CostEstimate(flops=width, bytes_accessed=width, transcendentals=0),
        name="expert_step",
    )(block, x, g, *weights, *extra)


GROUP = 256


def lane_half(x, h):
    lanes = lax.broadcasted_iota(jnp.int32, (1, x.shape[1]), 1)
    inside = (lanes >= HEAD_DIM) if h else (lanes < HEAD_DIM)
    return jnp.where(inside, x, jnp.zeros_like(x))


def moments(x):
    average = jnp.mean(x, axis=1, keepdims=True)
    centred = x - average
    scale = lax.rsqrt(jnp.mean(centred * centred, axis=1, keepdims=True) + epsilon)
    return centred * scale, scale


def attend_kernel(
    tok_ref, vec_ref, wq_ref, wk_ref, wv_ref, qv_ref, wo_ref, mask_ref,
    n_ref, q_ref, k_ref, v_ref, m_ref, lse_ref, res_ref, sn_ref, acc,
):
    g = pl.program_id(0)

    @pl.when(g == 0)
    def _():
        tok = tok_ref[...].astype(f32)
        hat, _ = moments(tok)
        n_ref[...] = (hat * vec_ref[0:1, :] + vec_ref[1:2, :]).astype(bf16)
        acc[...] = tok + vec_ref[2:3, :]

    normed = n_ref[...]
    q = (jnp.dot(normed, wq_ref[...], preferred_element_type=f32) + qv_ref[0:1, :]).astype(bf16)
    k = jnp.dot(normed, wk_ref[...], preferred_element_type=f32).astype(bf16)
    v = (jnp.dot(normed, wv_ref[...], preferred_element_type=f32) + qv_ref[1:2, :]).astype(bf16)
    q = q * HEAD_DIM**-0.5
    q_ref[...] = q
    k_ref[...] = k
    v_ref[...] = v
    rows = q.shape[0]
    lanes = lax.broadcasted_iota(jnp.int32, (1, 128), 1)
    lse_all = jnp.zeros((rows, 128), f32)
    mixed = []
    for p in range(GROUP // 128):
        at = slice(128 * p, 128 * p + 128)
        qp, kp, vp = q[:, at], k[:, at], v[:, at]
        pair = None
        for h in range(2):
            scores = dot_nt(lane_half(qp, h), kp) + mask_ref[0:1, :]
            top = jnp.max(scores, axis=1, keepdims=True)
            weights = jnp.exp(scores - top)
            total = jnp.sum(weights, axis=1, keepdims=True)
            part = jnp.dot(weights.astype(bf16), lane_half(vp, h), preferred_element_type=f32)
            part = part * (1.0 / total)
            pair = part if pair is None else pair + part
            lse_all = jnp.where(lanes == 2 * p + h, top + jnp.log(total), lse_all)
        mixed.append(pair.astype(bf16))
    lse_ref[...] = lse_all.T[0:8, :]
    mixed = jnp.concatenate(mixed, axis=1)
    m_ref[...] = mixed
    acc[...] += jnp.dot(mixed, wo_ref[...], preferred_element_type=f32)

    @pl.when(g == pl.num_programs(0) - 1)
    def _():
        residual = acc[...]
        hat, _ = moments(residual)
        res_ref[...] = residual
        sn_ref[...] = (hat * vec_ref[3:4, :] + vec_ref[4:5, :]).astype(bf16)


def attend_forward(tok, vecs, wq, wk, wv, qv, wo, mask_row):
    rows, width = tok.shape
    groups = width // GROUP
    whole = lambda a: pl.BlockSpec(a.shape, lambda g: (0, 0))
    by_col = lambda r: pl.BlockSpec((r, GROUP), lambda g: (0, g))
    full = pl.BlockSpec((rows, width), lambda g: (0, 0))
    act = jax.ShapeDtypeStruct((rows, width), bf16)
    return pl.pallas_call(
        attend_kernel,
        grid=(groups,),
        in_specs=[
            whole(tok), whole(vecs), by_col(width), by_col(width), by_col(width), by_col(8),
            pl.BlockSpec((GROUP, width), lambda g: (g, 0)), whole(mask_row),
        ],
        out_specs=[
            full, by_col(rows), by_col(rows), by_col(rows), by_col(rows),
            pl.BlockSpec((8, rows), lambda g: (g, 0)), full, full,
        ],
        out_shape=[
            act, act, act, act, act, jax.ShapeDtypeStruct((8 * groups, rows), f32),
            jax.ShapeDtypeStruct((rows, width), f32), act,
        ],
        scratch_shapes=[pltpu.VMEM((rows, width), f32)],
        compiler_params=pltpu.CompilerParams(
            vmem_limit_bytes=40 * 1024 * 1024, dimension_semantics=("arbitrary",)
        ),
        cost_estimate=pl.CostEstimate(
            flops=width, bytes_accessed=width, transcendentals=0
        ),
        name="attend_forward",
    )(tok, vecs, wq, wk, wv, qv, wo, mask_row)


def attend_back_kernel(
    first, n_ref, q_ref, k_ref, v_ref, lse_ref, mask_ref, ag_ref,
    wq_ref, wk_ref, wv_ref, wo_ref, *refs,
):
    refs = list(refs)
    if first:
        mix_ref, dw_ref, db_ref, out_ref, wide_ref = refs
        wide_ref[...] = dot_tn(mix_ref[...], ag_ref[...]).astype(bf16)
    else:
        acc_ref, tok_ref, vec_ref, rg_ref, dw_ref, db_ref, tg_ref, ln_ref, acc = refs
    mixed_grad = dot_nt(ag_ref[...], wo_ref[...]).astype(bf16)
    out = [[], [], []]
    for p in range(GROUP // 128):
        at = slice(128 * p, 128 * p + 128)
        qp, kp, vp, dp = q_ref[:, at], k_ref[:, at], v_ref[:, at], mixed_grad[:, at]
        dq_t = dk = dv = None
        for h in range(2):
            qh, kh, dh = lane_half(qp, h), lane_half(kp, h), lane_half(dp, h)
            row = 2 * p + h
            scores = dot_nt(kp, qh) + mask_ref[...]
            probs = jnp.exp(scores - lse_ref[row : row + 1, :])
            prob_grad = dot_nt(vp, dh)
            across = jnp.sum(probs * prob_grad, axis=0, keepdims=True)
            score_grad = (probs * (prob_grad - across)).astype(bf16)
            dv_h = jnp.dot(probs.astype(bf16), dh, preferred_element_type=f32)
            dk_h = jnp.dot(score_grad, qh, preferred_element_type=f32)
            dq_h = dot_tn(kh, score_grad)
            dv = dv_h if dv is None else dv + dv_h
            dk = dk_h if dk is None else dk + dk_h
            dq_t = dq_h if dq_t is None else dq_t + dq_h
        out[0].append((dq_t.T * HEAD_DIM**-0.5).astype(bf16))
        out[1].append(dk.astype(bf16))
        out[2].append(dv.astype(bf16))
    normed = n_ref[...]
    total = None
    sums = []
    for i, w_ref in enumerate((wq_ref, wk_ref, wv_ref)):
        grad = jnp.concatenate(out[i], axis=1)
        dw_ref[:, GROUP * i : GROUP * (i + 1)] = dot_tn(normed, grad).astype(bf16)
        sums.append(jnp.sum(grad.astype(f32), axis=0, keepdims=True))
        back = dot_nt(grad, w_ref[...])
        total = back if total is None else total + back
    db_ref[0:1, :] = sums[0]
    db_ref[1:2, :] = sums[2]
    db_ref[2:8, :] = jnp.zeros((6, GROUP), f32)
    if first:
        out_ref[...] = total
        return
    step = pl.program_id(0)

    @pl.when(step == 0)
    def _():
        acc[...] = acc_ref[...] + total

    @pl.when(step > 0)
    def _():
        acc[...] += total

    @pl.when(step == pl.num_programs(0) - 1)
    def _():
        grad = acc[...]
        hat, scale_of = moments(tok_ref[...].astype(f32))
        inner = grad * vec_ref[0:1, :]
        mean = jnp.mean(inner, axis=1, keepdims=True)
        other = jnp.mean(inner * hat, axis=1, keepdims=True)
        tg_ref[...] = rg_ref[...] + (inner - mean - hat * other) * scale_of
        ln_ref[0:1, :] = jnp.sum(grad * hat, axis=0, keepdims=True)
        ln_ref[1:2, :] = jnp.sum(grad, axis=0, keepdims=True)
        ln_ref[2:8, :] = jnp.zeros((6, grad.shape[1]), f32)


def attend_backward(first, n, q, k, v, lse, mask_col, ag, wq, wk, wv, wo, extra):
    rows, width = n.shape
    count = 1 if first else width // GROUP - 1
    skip = 0 if first else 1
    whole = lambda a: pl.BlockSpec(a.shape, lambda i: (0, 0))
    by_col = lambda r: pl.BlockSpec((r, GROUP), lambda i: (0, i + skip))
    by_row = lambda r, c: pl.BlockSpec((r, c), lambda i: (i + skip, 0))
    full = jax.ShapeDtypeStruct((rows, width), f32)
    outs = [
        jax.ShapeDtypeStruct((count * width, 3 * GROUP), bf16),
        jax.ShapeDtypeStruct((8, count * GROUP), f32),
        full,
        jax.ShapeDtypeStruct((width, width), bf16) if first else jax.ShapeDtypeStruct((8, width), f32),
    ]
    return pl.pallas_call(
        partial(attend_back_kernel, first),
        grid=(count,),
        in_specs=[
            whole(n), by_col(rows), by_col(rows), by_col(rows), by_row(8, rows), whole(mask_col), whole(ag),
            by_col(width), by_col(width), by_col(width), by_row(GROUP, width), *map(whole, extra),
        ],
        out_specs=[
            pl.BlockSpec((width, 3 * GROUP), lambda i: (i, 0)), pl.BlockSpec((8, GROUP), lambda i: (0, i)),
            whole(full), whole(outs[3]),
        ],
        out_shape=outs,
        scratch_shapes=[] if first else [pltpu.VMEM((rows, width), f32)],
        compiler_params=pltpu.CompilerParams(
            vmem_limit_bytes=(40 if first else 60) * 1024 * 1024, dimension_semantics=("arbitrary",)
        ),
        cost_estimate=pl.CostEstimate(flops=width, bytes_accessed=width, transcendentals=0),
        name="attend_backward",
    )(n, q, k, v, lse, mask_col, ag, wq, wk, wv, wo, *extra)


def place_kernel(at_ref, *refs):
    early_refs, late_refs, (q_ref, k_ref, v_ref, o_ref, small_ref) = refs[0:2], refs[2:4], refs[4:]
    count, height = o_ref.shape[0], o_ref.shape[1]
    half = pl.num_programs(0) // 2
    own = (pl.program_id(0) // half) == at_ref[0]

    def put(early_ref, late_ref):
        for j in range(count):
            at = at_ref[2 + j]
            early, late = early_ref[0, at].astype(f32), late_ref[0, at].astype(f32)
            o_ref[j] = early[0:height]
            groups = (early[height : 2 * height], late[0:height], late[height : 2 * height])
            for g, grad in enumerate(groups):
                for i, ref in enumerate((q_ref, k_ref, v_ref)):
                    ref[j, :, GROUP * g : GROUP * (g + 1)] = grad[:, GROUP * i : GROUP * (i + 1)]
            small_ref[j] = late[2 * height :]

    @pl.when(own)
    def _():
        put(early_refs[0], late_refs[0])

    @pl.when(jnp.logical_not(own))
    def _():
        put(early_refs[1], late_refs[1])


def put_in_place(early, late, at, height):
    chips, narrow, _, width = early[0].shape
    heights = [height] * 4 + [late[0].shape[2] - 2 * height]

    def of_chip(received):
        def spot(i, at):
            return (jnp.clip(i - (at[0] ^ received) * chips, 0, chips - 1) ^ at[1], 0, 0, 0)

        return spot

    return pl.pallas_call(
        place_kernel,
        grid_spec=pltpu.PrefetchScalarGridSpec(
            num_scalar_prefetch=1,
            grid=(2 * chips,),
            in_specs=[
                pl.BlockSpec((1,) + a.shape[1:], of_chip(i)) for pair in (early, late) for i, a in enumerate(pair)
            ],
            out_specs=[pl.BlockSpec((narrow, h, width), lambda i, at: (i, 0, 0)) for h in heights],
        ),
        out_shape=[jax.ShapeDtypeStruct((2 * chips * narrow, h, width), f32) for h in heights],
        compiler_params=pltpu.CompilerParams(
            vmem_limit_bytes=60 * 1024 * 1024, dimension_semantics=("arbitrary",)
        ),
        name="put_in_place",
    )(at, *early, *late)


class Links:
    def __init__(self, wide, narrow):
        self.wide, self.narrow = wide, narrow
        self.chips = wide // 2
        self.w = lax.axis_index("wide")
        self.z = lax.axis_index("narrow")

    def swap(self, x, k):
        return lax.ppermute(x, "wide", [(i, i ^ k) for i in range(self.wide)])

    def shift(self, x, k=1):
        n = self.narrow
        return lax.ppermute(x, "narrow", [(i, (i + k) % n) for i in range(n)])

    def exchange(self, blocks):
        return lax.all_to_all(blocks, "wide", split_axis=0, concat_axis=0, tiled=True)

    def pick(self, a, i):
        return lax.dynamic_index_in_dim(a, i, 0, keepdims=False)

    def halve(self, mats):
        core = self.w & 1
        part = lambda i: jnp.concatenate(
            [
                lax.dynamic_slice_in_dim(m, i * (m.shape[0] // 2), m.shape[0] // 2, 0).astype(bf16)
                for m in mats
            ]
        )
        return (part(core), self.swap(part(1 - core), 1), [m.shape[0] // 2 for m in mats])

    def halve_end(self, begun):
        kept, got, rows = begun
        total = (kept.astype(f32) + got.astype(f32)).astype(bf16)
        cuts = [sum(rows[:i]) for i in range(len(rows) + 1)]
        return [total[a:b] for a, b in zip(cuts, cuts[1:])]

    def spread_chips(self, mats):
        chip = self.w >> 1
        part = lambda i: jnp.concatenate(
            [
                lax.dynamic_slice_in_dim(m, i * (m.shape[0] // self.chips), m.shape[0] // self.chips, 0)
                for m in mats
            ]
        )
        got = [self.swap(part(chip ^ k), 2 * k) for k in range(1, self.chips)]
        return (part(chip), got, [m.shape[0] // self.chips for m in mats])

    def spread_end(self, begun):
        kept, got, rows = begun
        total = sum((g.astype(f32) for g in got), kept.astype(f32)).astype(bf16)
        cuts = [sum(rows[:i]) for i in range(len(rows) + 1)]
        return jnp.concatenate(
            [total[a:b].reshape(self.narrow, -1, total.shape[1]) for a, b in zip(cuts, cuts[1:])], axis=1
        )

    def scatter_narrow(self, total):
        n = self.narrow
        part = self.pick(total, self.z).astype(f32)
        for k in range(1, n):
            part = part + self.shift(self.pick(total, (self.z + k) % n), k).astype(f32)
        return part.astype(bf16)

    def gather_narrow(self, part):
        return jnp.stack([part] + [self.shift(part, k) for k in range(1, self.narrow)])

    def gather_chips(self, pieces):
        return jnp.stack([pieces] + [self.swap(pieces, 2 * k) for k in range(1, self.chips)])

    def gather_cores(self, pieces):
        return (pieces, self.swap(pieces, 1))

    def places(self):
        spots = [(self.z - j) % self.narrow for j in range(self.narrow)]
        return jnp.stack([self.w & 1, self.w >> 1] + spots).astype(jnp.int32)


def after(value, *others):
    return lax.optimization_barrier((value, others))[0]


def local(
    wide,
    narrow,
    tokens,
    live_mask,
    routes,
    priority,
    cotangent,
    first_gain,
    first_shift,
    query_weight,
    query_bias,
    key_weight,
    value_weight,
    value_bias,
    out_weight,
    out_bias,
    second_gain,
    second_shift,
    router_weight,
    expert_in,
    expert_in_bias,
    expert_out,
    expert_out_bias,
):
    links = Links(wide, narrow)
    sequences, patches, features = tokens.shape
    patches_dev = sequences * patches
    experts = expert_out_bias.shape[0]
    capacity = max(2, (210 * patches_dev + 100 * experts - 1) // (100 * experts))
    padded = (capacity + 2 + 15) // 16 * 16
    scaling = HEAD_DIM ** (-0.5)
    head_shape = (patches, HEADS, HEAD_DIM)

    bias_rows = jnp.broadcast_to(expert_in_bias, (BIAS_ROWS, expert_in_bias.shape[1]))
    w_in, w_out = expert_in[0], expert_out[0]
    quarter = w_in.shape[1]
    if quarter < features:
        w_in = jnp.pad(w_in, ((0, 0), (0, features - quarter)))
        bias_rows = jnp.pad(bias_rows, ((0, 0), (0, features - quarter)))
        w_out = jnp.pad(w_out, ((0, features - quarter), (0, 0)))
    weights = [(jnp.concatenate([w_in, bias_rows], axis=0), w_out)]
    for _ in range(1, narrow):
        w_in, w_out = weights[-1]
        w_out = links.shift(w_out)
        weights.append((links.shift(w_in), w_out))

    order_key = (
        priority * sequences + lax.broadcasted_iota(jnp.int32, (sequences, patches), 0)
    ).reshape(patches_dev)
    first_pick, second, spread_first, spread_second, first_kept, second_kept = slot_columns(
        live_mask.reshape(patches_dev) > 0,
        routes.reshape(patches_dev, 2),
        order_key,
        experts,
        capacity,
        padded,
    )
    spread = spread_first + spread_second

    def to_slots(rows):
        return dot_tn(spread, rows).astype(bf16).reshape(experts, padded, features)

    upstream_b = cotangent.reshape(patches_dev, features)
    up_sent = to_slots(upstream_b)
    up_slots = links.exchange(up_sent).reshape(experts * padded, features)

    tok = tokens.reshape(patches_dev, features)
    bias = jnp.where(live_mask.reshape(patches_dev) > 0, 0.0, -1e30).astype(f32)
    none = jnp.zeros_like(first_gain)
    vecs = jnp.stack([first_gain, first_shift, out_bias, second_gain, second_shift, none, none, none])
    qv = jnp.stack([query_bias, value_bias] + [none] * 6)
    normed, queries, key_rows, value_rows, mixed_heads, lse, residual, second_normed = attend_forward(
        tok, vecs, query_weight, key_weight, value_weight, qv, out_weight,
        jnp.broadcast_to(bias[None, :], (8, patches_dev)),
    )
    logits = jnp.dot(second_normed, router_weight, preferred_element_type=f32)
    chance = jax.nn.softmax(logits, axis=-1)

    arrived = links.exchange(to_slots(second_normed)).reshape(experts * padded, features)

    router_wide = jnp.pad(router_weight, ((0, 0), (0, 128 - experts)))
    lanes = jnp.arange(128)
    pick_rows = jnp.stack(
        [jnp.where(lanes < experts, 0.0, -1e30), (lanes == links.w).astype(f32)] + [jnp.zeros(128)] * 6
    ).astype(f32)

    for s in range(narrow):
        block = ((links.z - s) % narrow).astype(jnp.int32).reshape(1)
        last = s == narrow - 1
        if s == 0:
            slot_grad, made, back, grads = expert_step(
                True, last, padded, narrow, block, arrived, up_slots, weights[0], (router_wide, pick_rows)
            )
        else:
            made, back, grads = expert_step(
                False, last, padded, narrow, block, arrived, slot_grad, weights[s],
                (made, back, grads) + ((up_slots,) if last else ()),
            )
    grad_sum = lax.psum_scatter(
        grads.reshape(-1, features), "narrow", scatter_dimension=0, tiled=True
    )
    below = features + BIAS_ROWS
    expert_in_grad = grad_sum[None, :features, :quarter].astype(f32)
    expert_in_bias_grad = grad_sum[features : features + 1, :quarter].astype(f32)
    expert_out_grad = grad_sum[None, below : below + quarter].astype(f32)

    back = back.reshape(experts, padded, features)
    back_tokens = links.exchange(back)
    upstream = upstream_b.astype(f32)
    gate_first = jnp.sum(chance * first_pick, axis=1, keepdims=True)
    gate_second = jnp.sum(chance * second, axis=1, keepdims=True)
    slot_dots = back_tokens[:, padded - 2, :padded].astype(f32) + back_tokens[
        :, padded - 1, :padded
    ].astype(f32)
    slot_dots = slot_dots.reshape(1, experts * padded)
    bias_dots = jnp.dot(upstream, expert_out_bias.T, precision=highest)
    gate_first_grad = jnp.sum(spread_first * slot_dots, axis=1, keepdims=True) + jnp.sum(
        first_kept * bias_dots, axis=1, keepdims=True
    )
    gate_second_grad = jnp.sum(spread_second * slot_dots, axis=1, keepdims=True) + jnp.sum(
        second_kept * bias_dots, axis=1, keepdims=True
    )
    out_bias_sum = jnp.dot(
        (gate_first * first_kept + gate_second * second_kept).T, upstream, precision=highest
    )
    chance_grad = first_pick * gate_first_grad + second * gate_second_grad
    logit_grad = chance * (chance_grad - jnp.sum(chance * chance_grad, axis=1, keepdims=True))
    logit_grad = logit_grad.astype(bf16)
    router_sum = jnp.dot(second_normed.T, logit_grad, preferred_element_type=f32)
    second_normed_grad = jnp.dot(logit_grad, router_weight.T, preferred_element_type=f32)
    second_normed_grad = second_normed_grad + jnp.dot(
        spread, back_tokens.reshape(experts * padded, features), preferred_element_type=f32
    )
    unused, second_back = jax.vjp(layer_norm, residual, second_gain, second_shift)
    residual_part, second_gain_grad, second_shift_grad = second_back(second_normed_grad)
    residual_grad = upstream + residual_part
    attended_grad = residual_grad.astype(bf16)
    out_bias_grad = jnp.sum(attended_grad.astype(f32), axis=0)
    shared = (normed, queries, key_rows, value_rows, lse, bias[:, None], attended_grad)
    shared += (query_weight, key_weight, value_weight, out_weight)
    head_grads, bias_first, running, out_weight_grad = attend_backward(True, *shared, (mixed_heads,))
    begun = links.halve([out_weight_grad, head_grads])
    returned = links.exchange(
        after(made, head_grads).reshape(experts, padded, features)
    ).reshape(experts * padded, features)
    other_grads, bias_rest, tokens_grad, norm_grads = attend_backward(
        False, *shared, (running, tok, vecs, residual_grad)
    )
    begun = links.spread_chips(links.halve_end(begun))
    bias_grads = jnp.concatenate([bias_first, bias_rest], axis=1)

    parts = wide * narrow
    small = jnp.concatenate(
        [norm_grads[0:2], bias_grads[0:2], out_bias_grad[None], second_gain_grad[None],
         second_shift_grad[None], jnp.zeros((1, features), f32), router_sum.T, out_bias_sum], axis=0
    )
    small_rows = -(-small.shape[0] // (8 * parts)) * 8
    small = jnp.pad(small, ((0, small_rows * parts - small.shape[0]), (0, 0)))
    late = links.halve_end(links.halve([*after(other_grads, returned).reshape(2, features, features), small]))
    early = links.scatter_narrow(after(links.spread_end(begun), late))
    late = links.spread_end(links.spread_chips(late))
    early = links.gather_narrow(early)
    early_pieces = links.gather_chips(early)
    picked_first = jnp.dot(spread_first, returned, preferred_element_type=f32)
    picked_second = jnp.dot(spread_second, returned, preferred_element_type=f32)
    gated_bias = jnp.dot(
        gate_first * first_kept + gate_second * second_kept, expert_out_bias, precision=highest
    )
    output = residual + gate_first * picked_first + gate_second * picked_second + gated_bias
    output = output.astype(bf16).reshape(sequences, patches, features)
    late = links.scatter_narrow(after(late, output))
    late = links.gather_narrow(after(late, early))
    late_pieces = links.gather_chips(after(late, early_pieces))
    totals = put_in_place(
        links.gather_cores(after(early_pieces, expert_in_grad, expert_in_bias_grad, expert_out_grad)),
        links.gather_cores(late_pieces),
        links.places(), features // parts)
    totals = [a.reshape(-1, features) for a in totals]
    small = totals[4]
    tokens_grad = tokens_grad.reshape(sequences, patches, features)

    return (
        output,
        tokens_grad,
        small[0],
        small[1],
        totals[0],
        small[2],
        totals[1],
        totals[2],
        small[3],
        totals[3],
        small[4],
        small[5],
        small[6],
        small[8 : 8 + experts].T,
        expert_in_grad,
        expert_in_bias_grad,
        expert_out_grad,
        small[8 + experts : 8 + 2 * experts],
    )


def solution(mesh):
    return jax.shard_map(
        partial(local, mesh.shape["wide"], mesh.shape["narrow"]),
        mesh=mesh,
        in_specs=(
            P(("wide", "narrow"), None, None),
            P(("wide", "narrow"), None),
            P(("wide", "narrow"), None, None),
            P(("wide", "narrow"), None),
            P(("wide", "narrow"), None, None),
            P(),
            P(),
            P(),
            P(),
            P(),
            P(),
            P(),
            P(),
            P(),
            P(),
            P(),
            P(),
            P("wide", None, "narrow"),
            P("wide", "narrow"),
            P("wide", "narrow", None),
            P(),
        ),
        out_specs=(
            P(("wide", "narrow"), None, None),
            P(("wide", "narrow"), None, None),
            P(),
            P(),
            P(),
            P(),
            P(),
            P(),
            P(),
            P(),
            P(),
            P(),
            P(),
            P(),
            P("wide", None, "narrow"),
            P("wide", "narrow"),
            P("wide", "narrow", None),
            P(),
        ),
        check_vma=False,
    )
```

```python
from functools import partial

import jax
import jax.numpy as jnp
from jax import lax
from jax.experimental import pallas as pl
from jax.experimental.pallas import tpu as pltpu
from jax.sharding import PartitionSpec as P

HEADS = 12
HEAD_DIM = 64


epsilon = 1e-06
highest = lax.Precision.HIGHEST


def layer_norm(source, gain_vec, shift_vec):
    average = jnp.mean(source, axis=-1, keepdims=True)
    centred = source - average
    variance = jnp.mean(centred * centred, axis=-1, keepdims=True)
    return centred * lax.rsqrt(variance + epsilon) * gain_vec + shift_vec


f32 = jnp.float32
bf16 = jnp.bfloat16
GELU_SCALE = 0.7978845608028654
GELU_CUBE = 0.044715
BIAS_ROWS = 16


def slot_columns(alive, route_pair, order_key, experts, capacity, padded):
    earlier = (order_key[None, :] < order_key[:, None]).astype(bf16)
    columns = lax.broadcasted_iota(jnp.int32, (1, experts), 1)
    first_pick = ((route_pair[:, 0:1] == columns) & alive[:, None]).astype(f32)
    second = ((route_pair[:, 1:2] == columns) & alive[:, None]).astype(f32)
    both = jnp.concatenate([first_pick, second], axis=1).astype(bf16)
    ahead = jnp.dot(earlier, both, preferred_element_type=f32)
    place_first = jnp.sum(ahead[:, :experts] * first_pick, axis=1)
    already = jnp.sum(first_pick, axis=0, keepdims=True)
    place_second = jnp.sum((ahead[:, experts:] + already) * second, axis=1)
    slots = lax.broadcasted_iota(jnp.int32, (1, experts * padded), 1)

    def one_table(route_col, position, onehot):
        kept_mask = alive & (position < capacity)
        target = jnp.where(kept_mask, route_col * padded + position.astype(jnp.int32), -1)
        spread = (slots == target[:, None]).astype(bf16)
        return (spread, onehot * kept_mask[:, None].astype(f32))

    spread_first, first_kept = one_table(route_pair[:, 0], place_first, first_pick)
    spread_second, second_kept = one_table(route_pair[:, 1], place_second, second)
    return (first_pick, second, spread_first, spread_second, first_kept, second_kept)


def dot_nt(a, b):
    return lax.dot_general(a, b, (((1,), (1,)), ((), ())), preferred_element_type=f32)


def dot_tn(a, b):
    return lax.dot_general(a, b, (((0,), (0,)), ((), ())), preferred_element_type=f32)


def put_dots(padded, made, up_ref, back, ig_ref):
    width = made.shape[1]
    lanes = -(-padded // 128) * 128
    for start in range(0, made.shape[0], padded):
        at = slice(start, start + padded)
        ours = made[at]
        if lanes > padded:
            ours = jnp.concatenate([ours, jnp.zeros((lanes - padded, width), bf16)], axis=0)
        dots = dot_nt(up_ref[at, :], ours)
        row = lax.broadcasted_iota(jnp.int32, dots.shape, 0)
        column = lax.broadcasted_iota(jnp.int32, dots.shape, 1)
        dots = jnp.sum(jnp.where(row == column, dots, 0.0), axis=0, keepdims=True)
        high = dots.astype(bf16).astype(f32)
        blank = jnp.zeros((1, width - lanes), f32)
        place = lax.broadcasted_iota(jnp.int32, (padded, 1), 0)
        rows = jnp.where(place == padded - 2, jnp.concatenate([high, blank], axis=1), back[at])
        rows = jnp.where(place == padded - 1, jnp.concatenate([dots - high, blank], axis=1), rows)
        ig_ref[at, :] = rows.astype(bf16)


def expert_kernel(first, last, padded, block_ref, *refs):
    refs = list(refs)
    x_ref, g_ref, in_ref, out_ref = refs[:4]
    del refs[:4]
    if first:
        router_ref, pick_ref = refs[:2]
        del refs[:2]
    else:
        made_ref, back_ref = refs[:2]
        del refs[:4]
    if last:
        up_ref = g_ref if first else refs.pop(0)
    if first:
        slot_ref = refs.pop(0)
    prod_ref, ig_ref, grad_ref, rest_ref, gin, gout, gbias = refs
    step = pl.program_id(0)
    width = x_ref.shape[1]

    @pl.when(step == 0)
    def _():
        gin[...] = jnp.zeros_like(gin)
        gout[...] = jnp.zeros_like(gout)
        gbias[...] = jnp.zeros_like(gbias)

    x = x_ref[...]
    if first:
        logits = jnp.dot(x, router_ref[...], preferred_element_type=f32) + pick_ref[0:1, :]
        weights = jnp.exp(logits - jnp.max(logits, axis=1, keepdims=True))
        own = jnp.sum(weights * pick_ref[1:2, :], axis=1, keepdims=True)
        gate = own / jnp.sum(weights, axis=1, keepdims=True)
        slot_grad = (gate * g_ref[...].astype(f32)).astype(bf16)
        slot_ref[...] = slot_grad
    else:
        slot_grad = g_ref[...]
    below = width + BIAS_ROWS
    w_in = in_ref[0:width, :]
    bias = in_ref[width:below, :].astype(f32)[0:1, :]
    w_out = out_ref[...]
    v = jnp.dot(x, w_in, preferred_element_type=f32) + bias
    square = v * v
    t = jnp.tanh(GELU_SCALE * v * (1.0 + GELU_CUBE * square))
    half = 0.5 * (1.0 + t)
    hidden = (v * half).astype(bf16)
    slope = half + 0.5 * v * (1.0 - t * t) * (GELU_SCALE * (1.0 + 3.0 * GELU_CUBE * square))
    made = jnp.dot(hidden, w_out, preferred_element_type=f32)
    before_grad = dot_nt(slot_grad, w_out) * slope
    before_grad_b = before_grad.astype(bf16)
    back = dot_nt(before_grad_b, w_in)
    if not first:
        made = made + made_ref[...]
        back = back + back_ref[...]
    made = made.astype(prod_ref.dtype)
    prod_ref[...] = made
    if last:
        put_dots(padded, made, up_ref, back, ig_ref)
    else:
        ig_ref[...] = back
    gin[...] += dot_tn(x, before_grad_b)
    gout[...] += dot_tn(hidden, slot_grad)
    gbias[0:1, :] += jnp.sum(before_grad_b.astype(f32), axis=0, keepdims=True)

    @pl.when(step == pl.num_programs(0) - 1)
    def _():
        grad_ref[0, 0:width, :] = gin[...].astype(grad_ref.dtype)
        cut = width - rest_ref.shape[1]
        grad_ref[0, below : below + cut, :] = gout[0:cut, :].astype(bf16)
        rest_ref[0] = gout[cut:, :].astype(bf16)
        grad_ref[0, width:below, :] = jnp.broadcast_to(
            gbias[0:1, :], (BIAS_ROWS, gbias.shape[1])
        ).astype(grad_ref.dtype)


def expert_step(first, last, padded, count, block, x, g, weights, extra):
    rows, width = x.shape
    tile = rows // 2 if last else 256
    steps = rows // tile
    row_spec = pl.BlockSpec((tile, width), lambda i, b: (i, 0))
    whole = lambda a: pl.BlockSpec(a.shape, lambda i, b: (0, 0))
    in_specs = [row_spec, row_spec, whole(weights[0]), whole(weights[1])]
    outs = []
    specs = []
    if first:
        in_specs += [whole(extra[0]), whole(extra[1])]
        outs.append(jax.ShapeDtypeStruct((rows, width), bf16))
        specs.append(row_spec)
        aliases = {}
    else:
        in_specs += [row_spec, row_spec] + [pl.BlockSpec(memory_space=pl.ANY)] * 2 + [row_spec] * last
        aliases = {7: 2, 8: 3}
    acc_type = bf16 if last else f32
    outs += [jax.ShapeDtypeStruct((rows, width), acc_type)] * 2
    rest = width * 3 // 8 // 16 * 16
    heights = (weights[0].shape[0] + width - rest, rest)
    outs += [jax.ShapeDtypeStruct((count, h, width), bf16) for h in heights]
    specs += [row_spec, row_spec]
    specs += [pl.BlockSpec((1, h, width), lambda i, b: (b[0], 0, 0)) for h in heights]
    return pl.pallas_call(
        partial(expert_kernel, first, last, padded),
        grid_spec=pltpu.PrefetchScalarGridSpec(
            num_scalar_prefetch=1,
            grid=(steps,),
            in_specs=in_specs,
            out_specs=specs,
            scratch_shapes=[
                pltpu.VMEM((width, width), f32),
                pltpu.VMEM((width, width), f32),
                pltpu.VMEM((8, width), f32),
            ],
        ),
        out_shape=outs,
        input_output_aliases=aliases,
        compiler_params=pltpu.CompilerParams(
            vmem_limit_bytes=60 * 1024 * 1024, dimension_semantics=("arbitrary",)
        ),
        cost_estimate=pl.CostEstimate(flops=width, bytes_accessed=width, transcendentals=0),
        name="expert_step",
    )(block, x, g, *weights, *extra)


GROUP = 256


def lane_half(x, h):
    lanes = lax.broadcasted_iota(jnp.int32, (1, x.shape[1]), 1)
    inside = (lanes >= HEAD_DIM) if h else (lanes < HEAD_DIM)
    return jnp.where(inside, x, jnp.zeros_like(x))


def moments(x):
    average = jnp.mean(x, axis=1, keepdims=True)
    centred = x - average
    scale = lax.rsqrt(jnp.mean(centred * centred, axis=1, keepdims=True) + epsilon)
    return centred * scale, scale


def attend_kernel(
    tok_ref, vec_ref, wq_ref, wk_ref, wv_ref, qv_ref, wo_ref, mask_ref,
    n_ref, q_ref, k_ref, v_ref, m_ref, lse_ref, res_ref, sn_ref, acc,
):
    g = pl.program_id(0)

    @pl.when(g == 0)
    def _():
        tok = tok_ref[...].astype(f32)
        hat, _ = moments(tok)
        n_ref[...] = (hat * vec_ref[0:1, :] + vec_ref[1:2, :]).astype(bf16)
        acc[...] = tok + vec_ref[2:3, :]

    normed = n_ref[...]
    q = (jnp.dot(normed, wq_ref[...], preferred_element_type=f32) + qv_ref[0:1, :]).astype(bf16)
    k = jnp.dot(normed, wk_ref[...], preferred_element_type=f32).astype(bf16)
    v = (jnp.dot(normed, wv_ref[...], preferred_element_type=f32) + qv_ref[1:2, :]).astype(bf16)
    q = q * HEAD_DIM**-0.5
    q_ref[...] = q
    k_ref[...] = k
    v_ref[...] = v
    rows = q.shape[0]
    lanes = lax.broadcasted_iota(jnp.int32, (1, 128), 1)
    lse_all = jnp.zeros((rows, 128), f32)
    mixed = []
    for p in range(GROUP // 128):
        at = slice(128 * p, 128 * p + 128)
        qp, kp, vp = q[:, at], k[:, at], v[:, at]
        pair = None
        for h in range(2):
            scores = dot_nt(lane_half(qp, h), kp) + mask_ref[0:1, :]
            top = jnp.max(scores, axis=1, keepdims=True)
            weights = jnp.exp(scores - top)
            total = jnp.sum(weights, axis=1, keepdims=True)
            part = jnp.dot(weights.astype(bf16), lane_half(vp, h), preferred_element_type=f32)
            part = part * (1.0 / total)
            pair = part if pair is None else pair + part
            lse_all = jnp.where(lanes == 2 * p + h, top + jnp.log(total), lse_all)
        mixed.append(pair.astype(bf16))
    lse_ref[...] = lse_all.T[0:8, :]
    mixed = jnp.concatenate(mixed, axis=1)
    m_ref[...] = mixed
    acc[...] += jnp.dot(mixed, wo_ref[...], preferred_element_type=f32)

    @pl.when(g == pl.num_programs(0) - 1)
    def _():
        residual = acc[...]
        hat, _ = moments(residual)
        res_ref[...] = residual
        sn_ref[...] = (hat * vec_ref[3:4, :] + vec_ref[4:5, :]).astype(bf16)


def attend_forward(tok, vecs, wq, wk, wv, qv, wo, mask_row):
    rows, width = tok.shape
    groups = width // GROUP
    whole = lambda a: pl.BlockSpec(a.shape, lambda g: (0, 0))
    by_col = lambda r: pl.BlockSpec((r, GROUP), lambda g: (0, g))
    full = pl.BlockSpec((rows, width), lambda g: (0, 0))
    act = jax.ShapeDtypeStruct((rows, width), bf16)
    return pl.pallas_call(
        attend_kernel,
        grid=(groups,),
        in_specs=[
            whole(tok), whole(vecs), by_col(width), by_col(width), by_col(width), by_col(8),
            pl.BlockSpec((GROUP, width), lambda g: (g, 0)), whole(mask_row),
        ],
        out_specs=[
            full, by_col(rows), by_col(rows), by_col(rows), by_col(rows),
            pl.BlockSpec((8, rows), lambda g: (g, 0)), full, full,
        ],
        out_shape=[
            act, act, act, act, act, jax.ShapeDtypeStruct((8 * groups, rows), f32),
            jax.ShapeDtypeStruct((rows, width), f32), act,
        ],
        scratch_shapes=[pltpu.VMEM((rows, width), f32)],
        compiler_params=pltpu.CompilerParams(
            vmem_limit_bytes=40 * 1024 * 1024, dimension_semantics=("arbitrary",)
        ),
        cost_estimate=pl.CostEstimate(
            flops=width, bytes_accessed=width, transcendentals=0
        ),
        name="attend_forward",
    )(tok, vecs, wq, wk, wv, qv, wo, mask_row)


def attend_back_kernel(
    first, n_ref, q_ref, k_ref, v_ref, lse_ref, mask_ref, ag_ref,
    wq_ref, wk_ref, wv_ref, wo_ref, *refs,
):
    refs = list(refs)
    if first:
        mix_ref, dw_ref, db_ref, out_ref, wide_ref = refs
        wide_ref[...] = dot_tn(mix_ref[...], ag_ref[...]).astype(bf16)
    else:
        acc_ref, tok_ref, vec_ref, rg_ref, dw_ref, db_ref, tg_ref, ln_ref, acc = refs
    mixed_grad = dot_nt(ag_ref[...], wo_ref[...]).astype(bf16)
    out = [[], [], []]
    for p in range(GROUP // 128):
        at = slice(128 * p, 128 * p + 128)
        qp, kp, vp, dp = q_ref[:, at], k_ref[:, at], v_ref[:, at], mixed_grad[:, at]
        dq_t = dk = dv = None
        for h in range(2):
            qh, kh, dh = lane_half(qp, h), lane_half(kp, h), lane_half(dp, h)
            row = 2 * p + h
            scores = dot_nt(kp, qh) + mask_ref[...]
            probs = jnp.exp(scores - lse_ref[row : row + 1, :])
            prob_grad = dot_nt(vp, dh)
            across = jnp.sum(probs * prob_grad, axis=0, keepdims=True)
            score_grad = (probs * (prob_grad - across)).astype(bf16)
            dv_h = jnp.dot(probs.astype(bf16), dh, preferred_element_type=f32)
            dk_h = jnp.dot(score_grad, qh, preferred_element_type=f32)
            dq_h = dot_tn(kh, score_grad)
            dv = dv_h if dv is None else dv + dv_h
            dk = dk_h if dk is None else dk + dk_h
            dq_t = dq_h if dq_t is None else dq_t + dq_h
        out[0].append((dq_t.T * HEAD_DIM**-0.5).astype(bf16))
        out[1].append(dk.astype(bf16))
        out[2].append(dv.astype(bf16))
    normed = n_ref[...]
    total = None
    sums = []
    for i, w_ref in enumerate((wq_ref, wk_ref, wv_ref)):
        grad = jnp.concatenate(out[i], axis=1)
        dw_ref[:, GROUP * i : GROUP * (i + 1)] = dot_tn(normed, grad).astype(bf16)
        sums.append(jnp.sum(grad.astype(f32), axis=0, keepdims=True))
        back = dot_nt(grad, w_ref[...])
        total = back if total is None else total + back
    db_ref[0:1, :] = sums[0]
    db_ref[1:2, :] = sums[2]
    db_ref[2:8, :] = jnp.zeros((6, GROUP), f32)
    if first:
        out_ref[...] = total
        return
    step = pl.program_id(0)

    @pl.when(step == 0)
    def _():
        acc[...] = acc_ref[...] + total

    @pl.when(step > 0)
    def _():
        acc[...] += total

    @pl.when(step == pl.num_programs(0) - 1)
    def _():
        grad = acc[...]
        hat, scale_of = moments(tok_ref[...].astype(f32))
        inner = grad * vec_ref[0:1, :]
        mean = jnp.mean(inner, axis=1, keepdims=True)
        other = jnp.mean(inner * hat, axis=1, keepdims=True)
        tg_ref[...] = rg_ref[...] + (inner - mean - hat * other) * scale_of
        ln_ref[0:1, :] = jnp.sum(grad * hat, axis=0, keepdims=True)
        ln_ref[1:2, :] = jnp.sum(grad, axis=0, keepdims=True)
        ln_ref[2:8, :] = jnp.zeros((6, grad.shape[1]), f32)


def attend_backward(first, n, q, k, v, lse, mask_col, ag, wq, wk, wv, wo, extra):
    rows, width = n.shape
    count = 1 if first else width // GROUP - 1
    skip = 0 if first else 1
    whole = lambda a: pl.BlockSpec(a.shape, lambda i: (0, 0))
    by_col = lambda r: pl.BlockSpec((r, GROUP), lambda i: (0, i + skip))
    by_row = lambda r, c: pl.BlockSpec((r, c), lambda i: (i + skip, 0))
    full = jax.ShapeDtypeStruct((rows, width), f32)
    outs = [
        jax.ShapeDtypeStruct((count * width, 3 * GROUP), bf16),
        jax.ShapeDtypeStruct((8, count * GROUP), f32),
        full,
        jax.ShapeDtypeStruct((width, width), bf16) if first else jax.ShapeDtypeStruct((8, width), f32),
    ]
    return pl.pallas_call(
        partial(attend_back_kernel, first),
        grid=(count,),
        in_specs=[
            whole(n), by_col(rows), by_col(rows), by_col(rows), by_row(8, rows), whole(mask_col), whole(ag),
            by_col(width), by_col(width), by_col(width), by_row(GROUP, width), *map(whole, extra),
        ],
        out_specs=[
            pl.BlockSpec((width, 3 * GROUP), lambda i: (i, 0)), pl.BlockSpec((8, GROUP), lambda i: (0, i)),
            whole(full), whole(outs[3]),
        ],
        out_shape=outs,
        scratch_shapes=[] if first else [pltpu.VMEM((rows, width), f32)],
        compiler_params=pltpu.CompilerParams(
            vmem_limit_bytes=(40 if first else 60) * 1024 * 1024, dimension_semantics=("arbitrary",)
        ),
        cost_estimate=pl.CostEstimate(flops=width, bytes_accessed=width, transcendentals=0),
        name="attend_backward",
    )(n, q, k, v, lse, mask_col, ag, wq, wk, wv, wo, *extra)


def place_kernel(at_ref, *refs):
    early_refs, late_refs, (q_ref, k_ref, v_ref, o_ref, small_ref) = refs[0:2], refs[2:4], refs[4:]
    count, height = o_ref.shape[0], o_ref.shape[1]
    half = pl.num_programs(0) // 2
    own = (pl.program_id(0) // half) == at_ref[0]

    def put(early_ref, late_ref):
        for j in range(count):
            at = at_ref[2 + j]
            early, late = early_ref[0, at].astype(f32), late_ref[0, at].astype(f32)
            o_ref[j] = early[0:height]
            groups = (early[height : 2 * height], late[0:height], late[height : 2 * height])
            for g, grad in enumerate(groups):
                for i, ref in enumerate((q_ref, k_ref, v_ref)):
                    ref[j, :, GROUP * g : GROUP * (g + 1)] = grad[:, GROUP * i : GROUP * (i + 1)]
            small_ref[j] = late[2 * height :]

    @pl.when(own)
    def _():
        put(early_refs[0], late_refs[0])

    @pl.when(jnp.logical_not(own))
    def _():
        put(early_refs[1], late_refs[1])


def put_in_place(early, late, at, height):
    chips, narrow, _, width = early[0].shape
    heights = [height] * 4 + [late[0].shape[2] - 2 * height]

    def of_chip(received):
        def spot(i, at):
            return (jnp.clip(i - (at[0] ^ received) * chips, 0, chips - 1) ^ at[1], 0, 0, 0)

        return spot

    return pl.pallas_call(
        place_kernel,
        grid_spec=pltpu.PrefetchScalarGridSpec(
            num_scalar_prefetch=1,
            grid=(2 * chips,),
            in_specs=[
                pl.BlockSpec((1,) + a.shape[1:], of_chip(i)) for pair in (early, late) for i, a in enumerate(pair)
            ],
            out_specs=[pl.BlockSpec((narrow, h, width), lambda i, at: (i, 0, 0)) for h in heights],
        ),
        out_shape=[jax.ShapeDtypeStruct((2 * chips * narrow, h, width), f32) for h in heights],
        compiler_params=pltpu.CompilerParams(
            vmem_limit_bytes=60 * 1024 * 1024, dimension_semantics=("arbitrary",)
        ),
        name="put_in_place",
    )(at, *early, *late)


class Links:
    def __init__(self, wide, narrow):
        self.wide, self.narrow = wide, narrow
        self.chips = wide // 2
        self.w = lax.axis_index("wide")
        self.z = lax.axis_index("narrow")

    def swap(self, x, k):
        return lax.ppermute(x, "wide", [(i, i ^ k) for i in range(self.wide)])

    def shift(self, x, k=1):
        n = self.narrow
        return lax.ppermute(x, "narrow", [(i, (i + k) % n) for i in range(n)])

    def exchange(self, blocks):
        return lax.all_to_all(blocks, "wide", split_axis=0, concat_axis=0, tiled=True)

    def pick(self, a, i):
        return lax.dynamic_index_in_dim(a, i, 0, keepdims=False)

    def halve(self, mats):
        core = self.w & 1
        part = lambda i: jnp.concatenate(
            [
                lax.dynamic_slice_in_dim(m, i * (m.shape[0] // 2), m.shape[0] // 2, 0).astype(bf16)
                for m in mats
            ]
        )
        return (part(core), self.swap(part(1 - core), 1), [m.shape[0] // 2 for m in mats])

    def halve_end(self, begun):
        kept, got, rows = begun
        total = (kept.astype(f32) + got.astype(f32)).astype(bf16)
        cuts = [sum(rows[:i]) for i in range(len(rows) + 1)]
        return [total[a:b] for a, b in zip(cuts, cuts[1:])]

    def spread_chips(self, mats):
        chip = self.w >> 1
        part = lambda i: jnp.concatenate(
            [
                lax.dynamic_slice_in_dim(m, i * (m.shape[0] // self.chips), m.shape[0] // self.chips, 0)
                for m in mats
            ]
        )
        got = [self.swap(part(chip ^ k), 2 * k) for k in range(1, self.chips)]
        return (part(chip), got, [m.shape[0] // self.chips for m in mats])

    def spread_end(self, begun):
        kept, got, rows = begun
        total = sum((g.astype(f32) for g in got), kept.astype(f32)).astype(bf16)
        cuts = [sum(rows[:i]) for i in range(len(rows) + 1)]
        return jnp.concatenate(
            [total[a:b].reshape(self.narrow, -1, total.shape[1]) for a, b in zip(cuts, cuts[1:])], axis=1
        )

    def scatter_narrow(self, total):
        n = self.narrow
        part = self.pick(total, self.z).astype(f32)
        for k in range(1, n):
            part = part + self.shift(self.pick(total, (self.z + k) % n), k).astype(f32)
        return part.astype(bf16)

    def gather_narrow(self, part):
        return jnp.stack([part] + [self.shift(part, k) for k in range(1, self.narrow)])

    def gather_chips(self, pieces, *first):
        got = [self.swap(pieces, 2 * k) for k in range(1, self.chips - 1)]
        got.append(self.swap(after(pieces, first) if first else pieces, 2 * self.chips - 2))
        return jnp.stack([pieces] + got)

    def gather_cores(self, pieces):
        return (pieces, self.swap(pieces, 1))

    def places(self):
        spots = [(self.z - j) % self.narrow for j in range(self.narrow)]
        return jnp.stack([self.w & 1, self.w >> 1] + spots).astype(jnp.int32)


def after(value, *others):
    return lax.optimization_barrier((value, others))[0]


def local(
    wide,
    narrow,
    tokens,
    live_mask,
    routes,
    priority,
    cotangent,
    first_gain,
    first_shift,
    query_weight,
    query_bias,
    key_weight,
    value_weight,
    value_bias,
    out_weight,
    out_bias,
    second_gain,
    second_shift,
    router_weight,
    expert_in,
    expert_in_bias,
    expert_out,
    expert_out_bias,
):
    links = Links(wide, narrow)
    sequences, patches, features = tokens.shape
    patches_dev = sequences * patches
    experts = expert_out_bias.shape[0]
    capacity = max(2, (210 * patches_dev + 100 * experts - 1) // (100 * experts))
    padded = (capacity + 2 + 15) // 16 * 16
    scaling = HEAD_DIM ** (-0.5)
    head_shape = (patches, HEADS, HEAD_DIM)

    bias_rows = jnp.broadcast_to(expert_in_bias, (BIAS_ROWS, expert_in_bias.shape[1]))
    w_in, w_out = expert_in[0], expert_out[0]
    quarter = w_in.shape[1]
    if quarter < features:
        w_in = jnp.pad(w_in, ((0, 0), (0, features - quarter)))
        bias_rows = jnp.pad(bias_rows, ((0, 0), (0, features - quarter)))
        w_out = jnp.pad(w_out, ((0, features - quarter), (0, 0)))
    weights = [(jnp.concatenate([w_in, bias_rows], axis=0), w_out)]
    for _ in range(1, narrow):
        w_in, w_out = weights[-1]
        w_out = links.shift(w_out)
        weights.append((links.shift(w_in), w_out))

    order_key = (
        priority * sequences + lax.broadcasted_iota(jnp.int32, (sequences, patches), 0)
    ).reshape(patches_dev)
    first_pick, second, spread_first, spread_second, first_kept, second_kept = slot_columns(
        live_mask.reshape(patches_dev) > 0,
        routes.reshape(patches_dev, 2),
        order_key,
        experts,
        capacity,
        padded,
    )
    spread = spread_first + spread_second

    def to_slots(rows):
        return dot_tn(spread, rows).astype(bf16).reshape(experts, padded, features)

    upstream_b = cotangent.reshape(patches_dev, features)
    up_sent = to_slots(upstream_b)
    up_slots = links.exchange(up_sent).reshape(experts * padded, features)

    tok = tokens.reshape(patches_dev, features)
    bias = jnp.where(live_mask.reshape(patches_dev) > 0, 0.0, -1e30).astype(f32)
    none = jnp.zeros_like(first_gain)
    vecs = jnp.stack([first_gain, first_shift, out_bias, second_gain, second_shift, none, none, none])
    qv = jnp.stack([query_bias, value_bias] + [none] * 6)
    normed, queries, key_rows, value_rows, mixed_heads, lse, residual, second_normed = attend_forward(
        tok, vecs, query_weight, key_weight, value_weight, qv, out_weight,
        jnp.broadcast_to(bias[None, :], (8, patches_dev)),
    )
    logits = jnp.dot(second_normed, router_weight, preferred_element_type=f32)
    chance = jax.nn.softmax(logits, axis=-1)

    arrived = links.exchange(to_slots(second_normed)).reshape(experts * padded, features)

    router_wide = jnp.pad(router_weight, ((0, 0), (0, 128 - experts)))
    lanes = jnp.arange(128)
    pick_rows = jnp.stack(
        [jnp.where(lanes < experts, 0.0, -1e30), (lanes == links.w).astype(f32)] + [jnp.zeros(128)] * 6
    ).astype(f32)

    for s in range(narrow):
        block = ((links.z - s) % narrow).astype(jnp.int32).reshape(1)
        last = s == narrow - 1
        if s == 0:
            slot_grad, made, back, *grads = expert_step(
                True, last, padded, narrow, block, arrived, up_slots, weights[0], (router_wide, pick_rows)
            )
        else:
            made, back, *grads = expert_step(
                False, last, padded, narrow, block, arrived, slot_grad, weights[s],
                (made, back, *grads) + ((up_slots,) if last else ()),
            )
    def sum_owned(stacked):
        return lax.psum_scatter(stacked.reshape(-1, features), "narrow", scatter_dimension=0, tiled=True)

    grad_sum = sum_owned(grads[0])
    below = features + BIAS_ROWS
    expert_in_grad = grad_sum[None, :features, :quarter].astype(f32)
    expert_in_bias_grad = grad_sum[features : features + 1, :quarter].astype(f32)

    back = back.reshape(experts, padded, features)
    back_tokens = links.exchange(back)
    upstream = upstream_b.astype(f32)
    gate_first = jnp.sum(chance * first_pick, axis=1, keepdims=True)
    gate_second = jnp.sum(chance * second, axis=1, keepdims=True)
    slot_dots = back_tokens[:, padded - 2, :padded].astype(f32) + back_tokens[
        :, padded - 1, :padded
    ].astype(f32)
    slot_dots = slot_dots.reshape(1, experts * padded)
    bias_dots = jnp.dot(upstream, expert_out_bias.T, precision=highest)
    gate_first_grad = jnp.sum(spread_first * slot_dots, axis=1, keepdims=True) + jnp.sum(
        first_kept * bias_dots, axis=1, keepdims=True
    )
    gate_second_grad = jnp.sum(spread_second * slot_dots, axis=1, keepdims=True) + jnp.sum(
        second_kept * bias_dots, axis=1, keepdims=True
    )
    out_bias_sum = jnp.dot(
        (gate_first * first_kept + gate_second * second_kept).T, upstream, precision=highest
    )
    chance_grad = first_pick * gate_first_grad + second * gate_second_grad
    logit_grad = chance * (chance_grad - jnp.sum(chance * chance_grad, axis=1, keepdims=True))
    logit_grad = logit_grad.astype(bf16)
    router_sum = jnp.dot(second_normed.T, logit_grad, preferred_element_type=f32)
    second_normed_grad = jnp.dot(logit_grad, router_weight.T, preferred_element_type=f32)
    second_normed_grad = second_normed_grad + jnp.dot(
        spread, back_tokens.reshape(experts * padded, features), preferred_element_type=f32
    )
    unused, second_back = jax.vjp(layer_norm, residual, second_gain, second_shift)
    residual_part, second_gain_grad, second_shift_grad = second_back(second_normed_grad)
    residual_grad = upstream + residual_part
    attended_grad = residual_grad.astype(bf16)
    out_bias_grad = jnp.sum(attended_grad.astype(f32), axis=0)
    shared = (normed, queries, key_rows, value_rows, lse, bias[:, None], attended_grad)
    shared += (query_weight, key_weight, value_weight, out_weight)
    head_grads, bias_first, running, out_weight_grad = attend_backward(True, *shared, (mixed_heads,))
    begun = links.halve([out_weight_grad, head_grads])
    returned = links.exchange(
        after(made, head_grads).reshape(experts, padded, features)
    ).reshape(experts * padded, features)
    other_grads, bias_rest, tokens_grad, norm_grads = attend_backward(
        False, *shared, (running, tok, vecs, residual_grad)
    )
    begun = links.spread_chips(links.halve_end(begun))
    bias_grads = jnp.concatenate([bias_first, bias_rest], axis=1)

    parts = wide * narrow
    small = jnp.concatenate(
        [norm_grads[0:2], bias_grads[0:2], out_bias_grad[None], second_gain_grad[None],
         second_shift_grad[None], jnp.zeros((1, features), f32), router_sum.T, out_bias_sum], axis=0
    )
    small_rows = -(-small.shape[0] // (8 * parts)) * 8
    small = jnp.pad(small, ((0, small_rows * parts - small.shape[0]), (0, 0)))
    late = links.halve_end(links.halve([*after(other_grads, returned).reshape(2, features, features), small]))
    early = links.scatter_narrow(after(links.spread_end(begun), late))
    late = links.spread_end(links.spread_chips(late))
    early = links.gather_narrow(early)
    early_pieces = links.gather_chips(early)
    picked_first = jnp.dot(spread_first, returned, preferred_element_type=f32)
    picked_second = jnp.dot(spread_second, returned, preferred_element_type=f32)
    gated_bias = jnp.dot(
        gate_first * first_kept + gate_second * second_kept, expert_out_bias, precision=highest
    )
    output = residual + gate_first * picked_first + gate_second * picked_second + gated_bias
    output = output.astype(bf16).reshape(sequences, patches, features)
    late = links.scatter_narrow(after(late, output))
    late = links.gather_narrow(after(late, early))
    late_pieces = links.gather_chips(
        after(late, early_pieces), expert_in_grad, expert_in_bias_grad
    )
    rest_sum = sum_owned(after(grads[1], late, early_pieces))
    totals = put_in_place(
        links.gather_cores(early_pieces),
        links.gather_cores(late_pieces),
        links.places(), features // parts)
    rest_sum = after(rest_sum, totals)
    expert_out_grad = jnp.concatenate([grad_sum[below:], rest_sum])[None, :quarter].astype(f32)
    totals = [a.reshape(-1, features) for a in totals]
    small = totals[4]
    tokens_grad = tokens_grad.reshape(sequences, patches, features)

    return (
        output,
        tokens_grad,
        small[0],
        small[1],
        totals[0],
        small[2],
        totals[1],
        totals[2],
        small[3],
        totals[3],
        small[4],
        small[5],
        small[6],
        small[8 : 8 + experts].T,
        expert_in_grad,
        expert_in_bias_grad,
        expert_out_grad,
        small[8 + experts : 8 + 2 * experts],
    )


def solution(mesh):
    return jax.shard_map(
        partial(local, mesh.shape["wide"], mesh.shape["narrow"]),
        mesh=mesh,
        in_specs=(
            P(("wide", "narrow"), None, None),
            P(("wide", "narrow"), None),
            P(("wide", "narrow"), None, None),
            P(("wide", "narrow"), None),
            P(("wide", "narrow"), None, None),
            P(),
            P(),
            P(),
            P(),
            P(),
            P(),
            P(),
            P(),
            P(),
            P(),
            P(),
            P(),
            P("wide", None, "narrow"),
            P("wide", "narrow"),
            P("wide", "narrow", None),
            P(),
        ),
        out_specs=(
            P(("wide", "narrow"), None, None),
            P(("wide", "narrow"), None, None),
            P(),
            P(),
            P(),
            P(),
            P(),
            P(),
            P(),
            P(),
            P(),
            P(),
            P(),
            P(),
            P("wide", None, "narrow"),
            P("wide", "narrow"),
            P("wide", "narrow", None),
            P(),
        ),
        check_vma=False,
    )
```

```python
from functools import partial

import jax
import jax.numpy as jnp
from jax import lax
from jax.experimental import pallas as pl
from jax.experimental.pallas import tpu as pltpu
from jax.sharding import PartitionSpec as P

HEADS = 12
HEAD_DIM = 64


epsilon = 1e-06
highest = lax.Precision.HIGHEST


def layer_norm(source, gain_vec, shift_vec):
    average = jnp.mean(source, axis=-1, keepdims=True)
    centred = source - average
    variance = jnp.mean(centred * centred, axis=-1, keepdims=True)
    return centred * lax.rsqrt(variance + epsilon) * gain_vec + shift_vec


f32 = jnp.float32
bf16 = jnp.bfloat16
GELU_SCALE = 0.7978845608028654
GELU_CUBE = 0.044715
BIAS_ROWS = 16


def slot_columns(alive, route_pair, order_key, experts, capacity, padded):
    earlier = (order_key[None, :] < order_key[:, None]).astype(bf16)
    columns = lax.broadcasted_iota(jnp.int32, (1, experts), 1)
    first_pick = ((route_pair[:, 0:1] == columns) & alive[:, None]).astype(f32)
    second = ((route_pair[:, 1:2] == columns) & alive[:, None]).astype(f32)
    both = jnp.concatenate([first_pick, second], axis=1).astype(bf16)
    ahead = jnp.dot(earlier, both, preferred_element_type=f32)
    place_first = jnp.sum(ahead[:, :experts] * first_pick, axis=1)
    already = jnp.sum(first_pick, axis=0, keepdims=True)
    place_second = jnp.sum((ahead[:, experts:] + already) * second, axis=1)
    slots = lax.broadcasted_iota(jnp.int32, (1, experts * padded), 1)

    def one_table(route_col, position, onehot):
        kept_mask = alive & (position < capacity)
        target = jnp.where(kept_mask, route_col * padded + position.astype(jnp.int32), -1)
        spread = (slots == target[:, None]).astype(bf16)
        return (spread, onehot * kept_mask[:, None].astype(f32))

    spread_first, first_kept = one_table(route_pair[:, 0], place_first, first_pick)
    spread_second, second_kept = one_table(route_pair[:, 1], place_second, second)
    return (first_pick, second, spread_first, spread_second, first_kept, second_kept)


def dot_nt(a, b):
    return lax.dot_general(a, b, (((1,), (1,)), ((), ())), preferred_element_type=f32)


def dot_tn(a, b):
    return lax.dot_general(a, b, (((0,), (0,)), ((), ())), preferred_element_type=f32)


def put_dots(padded, made, up_ref, back, ig_ref):
    width = made.shape[1]
    lanes = -(-padded // 128) * 128
    for start in range(0, made.shape[0], padded):
        at = slice(start, start + padded)
        ours = made[at]
        if lanes > padded:
            ours = jnp.concatenate([ours, jnp.zeros((lanes - padded, width), bf16)], axis=0)
        dots = dot_nt(up_ref[at, :], ours)
        row = lax.broadcasted_iota(jnp.int32, dots.shape, 0)
        column = lax.broadcasted_iota(jnp.int32, dots.shape, 1)
        dots = jnp.sum(jnp.where(row == column, dots, 0.0), axis=0, keepdims=True)
        high = dots.astype(bf16).astype(f32)
        blank = jnp.zeros((1, width - lanes), f32)
        place = lax.broadcasted_iota(jnp.int32, (padded, 1), 0)
        rows = jnp.where(place == padded - 2, jnp.concatenate([high, blank], axis=1), back[at])
        rows = jnp.where(place == padded - 1, jnp.concatenate([dots - high, blank], axis=1), rows)
        ig_ref[at, :] = rows.astype(bf16)


def expert_kernel(first, last, padded, block_ref, *refs):
    refs = list(refs)
    x_ref, g_ref, in_ref, out_ref = refs[:4]
    del refs[:4]
    if first:
        router_ref, pick_ref = refs[:2]
        del refs[:2]
    else:
        made_ref, back_ref = refs[:2]
        del refs[:4]
    if last:
        up_ref = g_ref if first else refs.pop(0)
    if first:
        slot_ref = refs.pop(0)
    prod_ref, ig_ref, grad_ref, rest_ref, gin, gout, gbias = refs
    step = pl.program_id(0)
    width = x_ref.shape[1]

    @pl.when(step == 0)
    def _():
        gin[...] = jnp.zeros_like(gin)
        gout[...] = jnp.zeros_like(gout)
        gbias[...] = jnp.zeros_like(gbias)

    x = x_ref[...]
    if first:
        logits = jnp.dot(x, router_ref[...], preferred_element_type=f32) + pick_ref[0:1, :]
        weights = jnp.exp(logits - jnp.max(logits, axis=1, keepdims=True))
        own = jnp.sum(weights * pick_ref[1:2, :], axis=1, keepdims=True)
        gate = own / jnp.sum(weights, axis=1, keepdims=True)
        slot_grad = (gate * g_ref[...].astype(f32)).astype(bf16)
        slot_ref[...] = slot_grad
    else:
        slot_grad = g_ref[...]
    below = width + BIAS_ROWS
    w_in = in_ref[0:width, :]
    bias = in_ref[width:below, :].astype(f32)[0:1, :]
    w_out = out_ref[...]
    v = jnp.dot(x, w_in, preferred_element_type=f32) + bias
    square = v * v
    t = jnp.tanh(GELU_SCALE * v * (1.0 + GELU_CUBE * square))
    half = 0.5 * (1.0 + t)
    hidden = (v * half).astype(bf16)
    slope = half + 0.5 * v * (1.0 - t * t) * (GELU_SCALE * (1.0 + 3.0 * GELU_CUBE * square))
    made = jnp.dot(hidden, w_out, preferred_element_type=f32)
    before_grad = dot_nt(slot_grad, w_out) * slope
    before_grad_b = before_grad.astype(bf16)
    back = dot_nt(before_grad_b, w_in)
    if not first:
        made = made + made_ref[...]
        back = back + back_ref[...]
    made = made.astype(prod_ref.dtype)
    prod_ref[...] = made
    if last:
        put_dots(padded, made, up_ref, back, ig_ref)
    else:
        ig_ref[...] = back
    gin[...] += dot_tn(x, before_grad_b)
    gout[...] += dot_tn(hidden, slot_grad)
    gbias[0:1, :] += jnp.sum(before_grad_b.astype(f32), axis=0, keepdims=True)

    @pl.when(step == pl.num_programs(0) - 1)
    def _():
        grad_ref[0, 0:width, :] = gin[...].astype(grad_ref.dtype)
        cut = width - rest_ref.shape[1]
        grad_ref[0, below : below + cut, :] = gout[0:cut, :].astype(bf16)
        rest_ref[0] = gout[cut:, :].astype(bf16)
        grad_ref[0, width:below, :] = jnp.broadcast_to(
            gbias[0:1, :], (BIAS_ROWS, gbias.shape[1])
        ).astype(grad_ref.dtype)


def expert_step(first, last, padded, count, block, x, g, weights, extra):
    rows, width = x.shape
    tile = rows // 2 if last else 256
    steps = rows // tile
    row_spec = pl.BlockSpec((tile, width), lambda i, b: (i, 0))
    whole = lambda a: pl.BlockSpec(a.shape, lambda i, b: (0, 0))
    in_specs = [row_spec, row_spec, whole(weights[0]), whole(weights[1])]
    outs = []
    specs = []
    if first:
        in_specs += [whole(extra[0]), whole(extra[1])]
        outs.append(jax.ShapeDtypeStruct((rows, width), bf16))
        specs.append(row_spec)
        aliases = {}
    else:
        in_specs += [row_spec, row_spec] + [pl.BlockSpec(memory_space=pl.ANY)] * 2 + [row_spec] * last
        aliases = {7: 2, 8: 3}
    acc_type = bf16 if last else f32
    outs += [jax.ShapeDtypeStruct((rows, width), acc_type)] * 2
    rest = width // 3 // 16 * 16
    heights = (weights[0].shape[0] + width - rest, rest)
    outs += [jax.ShapeDtypeStruct((count, h, width), bf16) for h in heights]
    specs += [row_spec, row_spec]
    specs += [pl.BlockSpec((1, h, width), lambda i, b: (b[0], 0, 0)) for h in heights]
    return pl.pallas_call(
        partial(expert_kernel, first, last, padded),
        grid_spec=pltpu.PrefetchScalarGridSpec(
            num_scalar_prefetch=1,
            grid=(steps,),
            in_specs=in_specs,
            out_specs=specs,
            scratch_shapes=[
                pltpu.VMEM((width, width), f32),
                pltpu.VMEM((width, width), f32),
                pltpu.VMEM((8, width), f32),
            ],
        ),
        out_shape=outs,
        input_output_aliases=aliases,
        compiler_params=pltpu.CompilerParams(
            vmem_limit_bytes=60 * 1024 * 1024, dimension_semantics=("arbitrary",)
        ),
        cost_estimate=pl.CostEstimate(flops=width, bytes_accessed=width, transcendentals=0),
        name="expert_step",
    )(block, x, g, *weights, *extra)


GROUP = 256


def lane_half(x, h):
    lanes = lax.broadcasted_iota(jnp.int32, (1, x.shape[1]), 1)
    inside = (lanes >= HEAD_DIM) if h else (lanes < HEAD_DIM)
    return jnp.where(inside, x, jnp.zeros_like(x))


def moments(x):
    average = jnp.mean(x, axis=1, keepdims=True)
    centred = x - average
    scale = lax.rsqrt(jnp.mean(centred * centred, axis=1, keepdims=True) + epsilon)
    return centred * scale, scale


def attend_kernel(
    tok_ref, vec_ref, wq_ref, wk_ref, wv_ref, qv_ref, wo_ref, mask_ref,
    n_ref, q_ref, k_ref, v_ref, m_ref, lse_ref, res_ref, sn_ref, acc,
):
    g = pl.program_id(0)

    @pl.when(g == 0)
    def _():
        tok = tok_ref[...].astype(f32)
        hat, _ = moments(tok)
        n_ref[...] = (hat * vec_ref[0:1, :] + vec_ref[1:2, :]).astype(bf16)
        acc[...] = tok + vec_ref[2:3, :]

    normed = n_ref[...]
    q = (jnp.dot(normed, wq_ref[...], preferred_element_type=f32) + qv_ref[0:1, :]).astype(bf16)
    k = jnp.dot(normed, wk_ref[...], preferred_element_type=f32).astype(bf16)
    v = (jnp.dot(normed, wv_ref[...], preferred_element_type=f32) + qv_ref[1:2, :]).astype(bf16)
    q = q * HEAD_DIM**-0.5
    q_ref[...] = q
    k_ref[...] = k
    v_ref[...] = v
    rows = q.shape[0]
    lanes = lax.broadcasted_iota(jnp.int32, (1, 128), 1)
    lse_all = jnp.zeros((rows, 128), f32)
    mixed = []
    for p in range(GROUP // 128):
        at = slice(128 * p, 128 * p + 128)
        qp, kp, vp = q[:, at], k[:, at], v[:, at]
        pair = None
        for h in range(2):
            scores = dot_nt(lane_half(qp, h), kp) + mask_ref[0:1, :]
            top = jnp.max(scores, axis=1, keepdims=True)
            weights = jnp.exp(scores - top)
            total = jnp.sum(weights, axis=1, keepdims=True)
            part = jnp.dot(weights.astype(bf16), lane_half(vp, h), preferred_element_type=f32)
            part = part * (1.0 / total)
            pair = part if pair is None else pair + part
            lse_all = jnp.where(lanes == 2 * p + h, top + jnp.log(total), lse_all)
        mixed.append(pair.astype(bf16))
    lse_ref[...] = lse_all.T[0:8, :]
    mixed = jnp.concatenate(mixed, axis=1)
    m_ref[...] = mixed
    acc[...] += jnp.dot(mixed, wo_ref[...], preferred_element_type=f32)

    @pl.when(g == pl.num_programs(0) - 1)
    def _():
        residual = acc[...]
        hat, _ = moments(residual)
        res_ref[...] = residual
        sn_ref[...] = (hat * vec_ref[3:4, :] + vec_ref[4:5, :]).astype(bf16)


def attend_forward(tok, vecs, wq, wk, wv, qv, wo, mask_row):
    rows, width = tok.shape
    groups = width // GROUP
    whole = lambda a: pl.BlockSpec(a.shape, lambda g: (0, 0))
    by_col = lambda r: pl.BlockSpec((r, GROUP), lambda g: (0, g))
    full = pl.BlockSpec((rows, width), lambda g: (0, 0))
    act = jax.ShapeDtypeStruct((rows, width), bf16)
    return pl.pallas_call(
        attend_kernel,
        grid=(groups,),
        in_specs=[
            whole(tok), whole(vecs), by_col(width), by_col(width), by_col(width), by_col(8),
            pl.BlockSpec((GROUP, width), lambda g: (g, 0)), whole(mask_row),
        ],
        out_specs=[
            full, by_col(rows), by_col(rows), by_col(rows), by_col(rows),
            pl.BlockSpec((8, rows), lambda g: (g, 0)), full, full,
        ],
        out_shape=[
            act, act, act, act, act, jax.ShapeDtypeStruct((8 * groups, rows), f32),
            jax.ShapeDtypeStruct((rows, width), f32), act,
        ],
        scratch_shapes=[pltpu.VMEM((rows, width), f32)],
        compiler_params=pltpu.CompilerParams(
            vmem_limit_bytes=40 * 1024 * 1024, dimension_semantics=("arbitrary",)
        ),
        cost_estimate=pl.CostEstimate(
            flops=width, bytes_accessed=width, transcendentals=0
        ),
        name="attend_forward",
    )(tok, vecs, wq, wk, wv, qv, wo, mask_row)


def put_halves(core, keep_ref, send_ref, start, columns, value):
    half = value.shape[0] // 2
    low, high = value[:half], value[half:]
    at = pl.ds(start, half)
    keep_ref[at, columns] = jnp.where(core == 0, low, high).astype(bf16)
    send_ref[at, columns] = jnp.where(core == 0, high, low).astype(bf16)


def attend_back_kernel(
    first, core_ref, n_ref, q_ref, k_ref, v_ref, lse_ref, mask_ref, ag_ref,
    wq_ref, wk_ref, wv_ref, wo_ref, *refs,
):
    refs = list(refs)
    if first:
        mix_ref, keep_ref, send_ref, db_ref, out_ref = refs
        start = n_ref.shape[1] // 2
        wide_grad = dot_tn(mix_ref[...], ag_ref[...])
        put_halves(core_ref[0], keep_ref, send_ref, 0, slice(None), wide_grad)
    else:
        acc_ref, tok_ref, vec_ref, rg_ref, keep_ref, send_ref, db_ref, tg_ref, ln_ref, acc = refs
        start = pl.multiple_of(pl.program_id(0) * (n_ref.shape[1] // 2), 16)
    mixed_grad = dot_nt(ag_ref[...], wo_ref[...]).astype(bf16)
    out = [[], [], []]
    for p in range(GROUP // 128):
        at = slice(128 * p, 128 * p + 128)
        qp, kp, vp, dp = q_ref[:, at], k_ref[:, at], v_ref[:, at], mixed_grad[:, at]
        dq_t = dk = dv = None
        for h in range(2):
            qh, kh, dh = lane_half(qp, h), lane_half(kp, h), lane_half(dp, h)
            row = 2 * p + h
            scores = dot_nt(kp, qh) + mask_ref[...]
            probs = jnp.exp(scores - lse_ref[row : row + 1, :])
            prob_grad = dot_nt(vp, dh)
            across = jnp.sum(probs * prob_grad, axis=0, keepdims=True)
            score_grad = (probs * (prob_grad - across)).astype(bf16)
            dv_h = jnp.dot(probs.astype(bf16), dh, preferred_element_type=f32)
            dk_h = jnp.dot(score_grad, qh, preferred_element_type=f32)
            dq_h = dot_tn(kh, score_grad)
            dv = dv_h if dv is None else dv + dv_h
            dk = dk_h if dk is None else dk + dk_h
            dq_t = dq_h if dq_t is None else dq_t + dq_h
        out[0].append((dq_t.T * HEAD_DIM**-0.5).astype(bf16))
        out[1].append(dk.astype(bf16))
        out[2].append(dv.astype(bf16))
    normed = n_ref[...]
    total = None
    sums = []
    for i, w_ref in enumerate((wq_ref, wk_ref, wv_ref)):
        grad = jnp.concatenate(out[i], axis=1)
        columns = slice(GROUP * i, GROUP * (i + 1))
        put_halves(core_ref[0], keep_ref, send_ref, start, columns, dot_tn(normed, grad))
        sums.append(jnp.sum(grad.astype(f32), axis=0, keepdims=True))
        back = dot_nt(grad, w_ref[...])
        total = back if total is None else total + back
    db_ref[0:1, :] = sums[0]
    db_ref[1:2, :] = sums[2]
    db_ref[2:8, :] = jnp.zeros((6, GROUP), f32)
    if first:
        out_ref[...] = total
        return
    step = pl.program_id(0)

    @pl.when(step == 0)
    def _():
        acc[...] = acc_ref[...] + total

    @pl.when(step > 0)
    def _():
        acc[...] += total

    @pl.when(step == pl.num_programs(0) - 1)
    def _():
        grad = acc[...]
        hat, scale_of = moments(tok_ref[...].astype(f32))
        inner = grad * vec_ref[0:1, :]
        mean = jnp.mean(inner, axis=1, keepdims=True)
        other = jnp.mean(inner * hat, axis=1, keepdims=True)
        tg_ref[...] = rg_ref[...] + (inner - mean - hat * other) * scale_of
        ln_ref[0:1, :] = jnp.sum(grad * hat, axis=0, keepdims=True)
        ln_ref[1:2, :] = jnp.sum(grad, axis=0, keepdims=True)
        ln_ref[2:8, :] = jnp.zeros((6, grad.shape[1]), f32)


def attend_backward(first, core, spare, n, q, k, v, lse, mask_col, ag, wq, wk, wv, wo, extra):
    rows, width = n.shape
    count = 1 if first else width // GROUP - 1
    skip = 0 if first else 1
    whole = lambda a: pl.BlockSpec(a.shape, lambda i, c: (0, 0))
    by_col = lambda r: pl.BlockSpec((r, GROUP), lambda i, c: (0, i + skip))
    by_row = lambda r, w: pl.BlockSpec((r, w), lambda i, c: (i + skip, 0))
    full = jax.ShapeDtypeStruct((rows, width), f32)
    half = jax.ShapeDtypeStruct(((count + first) * width // 2 + spare, width), bf16)
    outs = [half, half, jax.ShapeDtypeStruct((8, count * GROUP), f32), full]
    specs = [whole(half), whole(half), pl.BlockSpec((8, GROUP), lambda i, c: (0, i)), whole(full)]
    if not first:
        outs.append(jax.ShapeDtypeStruct((8, width), f32))
        specs.append(whole(outs[-1]))
    return pl.pallas_call(
        partial(attend_back_kernel, first),
        grid_spec=pltpu.PrefetchScalarGridSpec(
            num_scalar_prefetch=1,
            grid=(count,),
            in_specs=[
                whole(n), by_col(rows), by_col(rows), by_col(rows), by_row(8, rows), whole(mask_col), whole(ag),
                by_col(width), by_col(width), by_col(width), by_row(GROUP, width), *map(whole, extra),
            ],
            out_specs=specs,
            scratch_shapes=[] if first else [pltpu.VMEM((rows, width), f32)],
        ),
        out_shape=outs,
        compiler_params=pltpu.CompilerParams(
            vmem_limit_bytes=(40 if first else 60) * 1024 * 1024, dimension_semantics=("arbitrary",)
        ),
        cost_estimate=pl.CostEstimate(flops=width, bytes_accessed=width, transcendentals=0),
        name="attend_backward",
    )(core, n, q, k, v, lse, mask_col, ag, wq, wk, wv, wo, *extra)


def place_kernel(at_ref, *refs):
    early_refs, late_refs, (q_ref, k_ref, v_ref, o_ref, small_ref) = refs[0:2], refs[2:4], refs[4:]
    count, height = o_ref.shape[0], o_ref.shape[1]
    half = pl.num_programs(0) // 2
    own = (pl.program_id(0) // half) == at_ref[0]

    def put(early_ref, late_ref):
        for j in range(count):
            at = at_ref[2 + j]
            early, late = early_ref[0, at].astype(f32), late_ref[0, at].astype(f32)
            o_ref[j] = early[0:height]
            groups = (early[height : 2 * height], late[0:height], late[height : 2 * height])
            for g, grad in enumerate(groups):
                for i, ref in enumerate((q_ref, k_ref, v_ref)):
                    ref[j, :, GROUP * g : GROUP * (g + 1)] = grad[:, GROUP * i : GROUP * (i + 1)]
            small_ref[j] = late[2 * height :]

    @pl.when(own)
    def _():
        put(early_refs[0], late_refs[0])

    @pl.when(jnp.logical_not(own))
    def _():
        put(early_refs[1], late_refs[1])


def put_in_place(early, late, at, height):
    chips, narrow, _, width = early[0].shape
    heights = [height] * 4 + [late[0].shape[2] - 2 * height]

    def of_chip(received):
        def spot(i, at):
            return (jnp.clip(i - (at[0] ^ received) * chips, 0, chips - 1) ^ at[1], 0, 0, 0)

        return spot

    return pl.pallas_call(
        place_kernel,
        grid_spec=pltpu.PrefetchScalarGridSpec(
            num_scalar_prefetch=1,
            grid=(2 * chips,),
            in_specs=[
                pl.BlockSpec((1,) + a.shape[1:], of_chip(i)) for pair in (early, late) for i, a in enumerate(pair)
            ],
            out_specs=[pl.BlockSpec((narrow, h, width), lambda i, at: (i, 0, 0)) for h in heights],
        ),
        out_shape=[jax.ShapeDtypeStruct((2 * chips * narrow, h, width), f32) for h in heights],
        compiler_params=pltpu.CompilerParams(
            vmem_limit_bytes=60 * 1024 * 1024, dimension_semantics=("arbitrary",)
        ),
        name="put_in_place",
    )(at, *early, *late)


class Links:
    def __init__(self, wide, narrow):
        self.wide, self.narrow = wide, narrow
        self.chips = wide // 2
        self.w = lax.axis_index("wide")
        self.z = lax.axis_index("narrow")

    def swap(self, x, k):
        return lax.ppermute(x, "wide", [(i, i ^ k) for i in range(self.wide)])

    def shift(self, x, k=1):
        n = self.narrow
        return lax.ppermute(x, "narrow", [(i, (i + k) % n) for i in range(n)])

    def exchange(self, blocks):
        return lax.all_to_all(blocks, "wide", split_axis=0, concat_axis=0, tiled=True)

    def pick(self, a, i):
        return lax.dynamic_index_in_dim(a, i, 0, keepdims=False)

    def halve_end(self, begun):
        kept, got, rows = begun
        total = (kept.astype(f32) + got.astype(f32)).astype(bf16)
        cuts = [sum(rows[:i]) for i in range(len(rows) + 1)]
        return [total[a:b] for a, b in zip(cuts, cuts[1:])]

    def spread_chips(self, mats):
        chip = self.w >> 1
        part = lambda i: jnp.concatenate(
            [
                lax.dynamic_slice_in_dim(m, i * (m.shape[0] // self.chips), m.shape[0] // self.chips, 0)
                for m in mats
            ]
        )
        got = [self.swap(part(chip ^ k), 2 * k) for k in range(1, self.chips)]
        return (part(chip), got, [m.shape[0] // self.chips for m in mats])

    def spread_end(self, begun):
        kept, got, rows = begun
        total = sum((g.astype(f32) for g in got), kept.astype(f32)).astype(bf16)
        cuts = [sum(rows[:i]) for i in range(len(rows) + 1)]
        return jnp.concatenate(
            [total[a:b].reshape(self.narrow, -1, total.shape[1]) for a, b in zip(cuts, cuts[1:])], axis=1
        )

    def scatter_narrow(self, total):
        n = self.narrow
        part = self.pick(total, self.z).astype(f32)
        for k in range(1, n):
            part = part + self.shift(self.pick(total, (self.z + k) % n), k).astype(f32)
        return part.astype(bf16)

    def gather_narrow(self, part):
        return jnp.stack([part] + [self.shift(part, k) for k in range(1, self.narrow)])

    def gather_chips(self, pieces, *first):
        got = [self.swap(pieces, 2 * k) for k in range(1, self.chips - 1)]
        got.append(self.swap(after(pieces, first) if first else pieces, 2 * self.chips - 2))
        return jnp.stack([pieces] + got)

    def gather_cores(self, pieces):
        return (pieces, self.swap(pieces, 1))

    def places(self):
        spots = [(self.z - j) % self.narrow for j in range(self.narrow)]
        return jnp.stack([self.w & 1, self.w >> 1] + spots).astype(jnp.int32)


def after(value, *others):
    return lax.optimization_barrier((value, others))[0]


def local(
    wide,
    narrow,
    tokens,
    live_mask,
    routes,
    priority,
    cotangent,
    first_gain,
    first_shift,
    query_weight,
    query_bias,
    key_weight,
    value_weight,
    value_bias,
    out_weight,
    out_bias,
    second_gain,
    second_shift,
    router_weight,
    expert_in,
    expert_in_bias,
    expert_out,
    expert_out_bias,
):
    links = Links(wide, narrow)
    sequences, patches, features = tokens.shape
    patches_dev = sequences * patches
    experts = expert_out_bias.shape[0]
    capacity = max(2, (210 * patches_dev + 100 * experts - 1) // (100 * experts))
    padded = (capacity + 2 + 15) // 16 * 16
    scaling = HEAD_DIM ** (-0.5)
    head_shape = (patches, HEADS, HEAD_DIM)

    bias_rows = jnp.broadcast_to(expert_in_bias, (BIAS_ROWS, expert_in_bias.shape[1]))
    w_in, w_out = expert_in[0], expert_out[0]
    quarter = w_in.shape[1]
    if quarter < features:
        w_in = jnp.pad(w_in, ((0, 0), (0, features - quarter)))
        bias_rows = jnp.pad(bias_rows, ((0, 0), (0, features - quarter)))
        w_out = jnp.pad(w_out, ((0, features - quarter), (0, 0)))
    weights = [(jnp.concatenate([w_in, bias_rows], axis=0), w_out)]
    for _ in range(1, narrow):
        w_in, w_out = weights[-1]
        w_out = links.shift(w_out)
        weights.append((links.shift(w_in), w_out))

    order_key = (
        priority * sequences + lax.broadcasted_iota(jnp.int32, (sequences, patches), 0)
    ).reshape(patches_dev)
    first_pick, second, spread_first, spread_second, first_kept, second_kept = slot_columns(
        live_mask.reshape(patches_dev) > 0,
        routes.reshape(patches_dev, 2),
        order_key,
        experts,
        capacity,
        padded,
    )
    spread = spread_first + spread_second

    def to_slots(rows):
        return dot_tn(spread, rows).astype(bf16).reshape(experts, padded, features)

    upstream_b = cotangent.reshape(patches_dev, features)
    up_sent = to_slots(upstream_b)
    up_slots = links.exchange(up_sent).reshape(experts * padded, features)

    tok = tokens.reshape(patches_dev, features)
    bias = jnp.where(live_mask.reshape(patches_dev) > 0, 0.0, -1e30).astype(f32)
    none = jnp.zeros_like(first_gain)
    vecs = jnp.stack([first_gain, first_shift, out_bias, second_gain, second_shift, none, none, none])
    qv = jnp.stack([query_bias, value_bias] + [none] * 6)
    normed, queries, key_rows, value_rows, mixed_heads, lse, residual, second_normed = attend_forward(
        tok, vecs, query_weight, key_weight, value_weight, qv, out_weight,
        jnp.broadcast_to(bias[None, :], (8, patches_dev)),
    )
    logits = jnp.dot(second_normed, router_weight, preferred_element_type=f32)
    chance = jax.nn.softmax(logits, axis=-1)

    arrived = links.exchange(to_slots(second_normed)).reshape(experts * padded, features)

    router_wide = jnp.pad(router_weight, ((0, 0), (0, 128 - experts)))
    lanes = jnp.arange(128)
    pick_rows = jnp.stack(
        [jnp.where(lanes < experts, 0.0, -1e30), (lanes == links.w).astype(f32)] + [jnp.zeros(128)] * 6
    ).astype(f32)

    for s in range(narrow):
        block = ((links.z - s) % narrow).astype(jnp.int32).reshape(1)
        last = s == narrow - 1
        if s == 0:
            slot_grad, made, back, *grads = expert_step(
                True, last, padded, narrow, block, arrived, up_slots, weights[0], (router_wide, pick_rows)
            )
        else:
            made, back, *grads = expert_step(
                False, last, padded, narrow, block, arrived, slot_grad, weights[s],
                (made, back, *grads) + ((up_slots,) if last else ()),
            )
    def sum_owned(stacked):
        return lax.psum_scatter(stacked.reshape(-1, features), "narrow", scatter_dimension=0, tiled=True)

    grad_sum = sum_owned(grads[0])
    below = features + BIAS_ROWS
    expert_in_grad = grad_sum[None, :features, :quarter].astype(f32)
    expert_in_bias_grad = grad_sum[features : features + 1, :quarter].astype(f32)

    back = back.reshape(experts, padded, features)
    back_tokens = links.exchange(back)
    upstream = upstream_b.astype(f32)
    gate_first = jnp.sum(chance * first_pick, axis=1, keepdims=True)
    gate_second = jnp.sum(chance * second, axis=1, keepdims=True)
    slot_dots = back_tokens[:, padded - 2, :padded].astype(f32) + back_tokens[
        :, padded - 1, :padded
    ].astype(f32)
    slot_dots = slot_dots.reshape(1, experts * padded)
    bias_dots = jnp.dot(upstream, expert_out_bias.T, precision=highest)
    gate_first_grad = jnp.sum(spread_first * slot_dots, axis=1, keepdims=True) + jnp.sum(
        first_kept * bias_dots, axis=1, keepdims=True
    )
    gate_second_grad = jnp.sum(spread_second * slot_dots, axis=1, keepdims=True) + jnp.sum(
        second_kept * bias_dots, axis=1, keepdims=True
    )
    out_bias_sum = jnp.dot(
        (gate_first * first_kept + gate_second * second_kept).T, upstream, precision=highest
    )
    chance_grad = first_pick * gate_first_grad + second * gate_second_grad
    logit_grad = chance * (chance_grad - jnp.sum(chance * chance_grad, axis=1, keepdims=True))
    logit_grad = logit_grad.astype(bf16)
    router_sum = jnp.dot(second_normed.T, logit_grad, preferred_element_type=f32)
    second_normed_grad = jnp.dot(logit_grad, router_weight.T, preferred_element_type=f32)
    second_normed_grad = second_normed_grad + jnp.dot(
        spread, back_tokens.reshape(experts * padded, features), preferred_element_type=f32
    )
    unused, second_back = jax.vjp(layer_norm, residual, second_gain, second_shift)
    residual_part, second_gain_grad, second_shift_grad = second_back(second_normed_grad)
    residual_grad = upstream + residual_part
    attended_grad = residual_grad.astype(bf16)
    out_bias_grad = jnp.sum(attended_grad.astype(f32), axis=0)
    shared = (normed, queries, key_rows, value_rows, lse, bias[:, None], attended_grad)
    shared += (query_weight, key_weight, value_weight, out_weight)
    parts = wide * narrow
    small_rows = -(-(8 + 2 * experts) // (8 * parts)) * 8
    spare = small_rows * parts // 2
    core = (links.w & 1).astype(jnp.int32)
    kept, sent, bias_first, running = attend_backward(True, core[None], 0, *shared, (mixed_heads,))
    begun = (kept, links.swap(sent, 1), [features // 2] * 2)
    returned = links.exchange(after(made, sent).reshape(experts, padded, features)).reshape(
        experts * padded, features
    )
    kept, sent, bias_rest, tokens_grad, norm_grads = attend_backward(
        False, core[None], spare, *shared, (running, tok, vecs, residual_grad)
    )
    begun = links.spread_chips(links.halve_end(begun))
    bias_grads = jnp.concatenate([bias_first, bias_rest], axis=1)

    small = jnp.concatenate(
        [norm_grads[0:2], bias_grads[0:2], out_bias_grad[None], second_gain_grad[None],
         second_shift_grad[None], jnp.zeros((1, features), f32), router_sum.T, out_bias_sum], axis=0
    )
    small = jnp.pad(small, ((0, 2 * spare - small.shape[0]), (0, 0))).astype(bf16).reshape(2, spare, features)
    filled = kept.shape[0] - spare
    kept = lax.dynamic_update_slice_in_dim(kept, links.pick(small, core), filled, 0)
    sent = lax.dynamic_update_slice_in_dim(sent, links.pick(small, 1 - core), filled, 0)
    late = (kept, links.swap(after(sent, returned), 1), [features // 2] * 2 + [spare])
    late = links.halve_end(late)
    early = links.scatter_narrow(after(links.spread_end(begun), late))
    late = links.spread_end(links.spread_chips(late))
    early = links.gather_narrow(early)
    early_pieces = links.gather_chips(early)
    picked_first = jnp.dot(spread_first, returned, preferred_element_type=f32)
    picked_second = jnp.dot(spread_second, returned, preferred_element_type=f32)
    gated_bias = jnp.dot(
        gate_first * first_kept + gate_second * second_kept, expert_out_bias, precision=highest
    )
    output = residual + gate_first * picked_first + gate_second * picked_second + gated_bias
    output = output.astype(bf16).reshape(sequences, patches, features)
    late = links.scatter_narrow(after(late, output))
    late = links.gather_narrow(after(late, early))
    late_pieces = links.gather_chips(
        after(late, early_pieces), expert_in_grad, expert_in_bias_grad
    )
    rest_sum = sum_owned(after(grads[1], late, early_pieces))
    totals = put_in_place(
        links.gather_cores(early_pieces),
        links.gather_cores(late_pieces),
        links.places(), features // parts)
    rest_sum = after(rest_sum, totals)
    expert_out_grad = jnp.concatenate([grad_sum[below:], rest_sum])[None, :quarter].astype(f32)
    totals = [a.reshape(-1, features) for a in totals]
    small = totals[4]
    tokens_grad = tokens_grad.reshape(sequences, patches, features)

    return (
        output,
        tokens_grad,
        small[0],
        small[1],
        totals[0],
        small[2],
        totals[1],
        totals[2],
        small[3],
        totals[3],
        small[4],
        small[5],
        small[6],
        small[8 : 8 + experts].T,
        expert_in_grad,
        expert_in_bias_grad,
        expert_out_grad,
        small[8 + experts : 8 + 2 * experts],
    )


def solution(mesh):
    return jax.shard_map(
        partial(local, mesh.shape["wide"], mesh.shape["narrow"]),
        mesh=mesh,
        in_specs=(
            P(("wide", "narrow"), None, None),
            P(("wide", "narrow"), None),
            P(("wide", "narrow"), None, None),
            P(("wide", "narrow"), None),
            P(("wide", "narrow"), None, None),
            P(),
            P(),
            P(),
            P(),
            P(),
            P(),
            P(),
            P(),
            P(),
            P(),
            P(),
            P(),
            P("wide", None, "narrow"),
            P("wide", "narrow"),
            P("wide", "narrow", None),
            P(),
        ),
        out_specs=(
            P(("wide", "narrow"), None, None),
            P(("wide", "narrow"), None, None),
            P(),
            P(),
            P(),
            P(),
            P(),
            P(),
            P(),
            P(),
            P(),
            P(),
            P(),
            P(),
            P("wide", None, "narrow"),
            P("wide", "narrow"),
            P("wide", "narrow", None),
            P(),
        ),
        check_vma=False,
    )
```

```python
from functools import partial

import jax
import jax.numpy as jnp
from jax import lax
from jax.experimental import pallas as pl
from jax.experimental.pallas import tpu as pltpu
from jax.sharding import PartitionSpec as P

HEADS = 12
HEAD_DIM = 64


epsilon = 1e-06
highest = lax.Precision.HIGHEST


def layer_norm(source, gain_vec, shift_vec):
    average = jnp.mean(source, axis=-1, keepdims=True)
    centred = source - average
    variance = jnp.mean(centred * centred, axis=-1, keepdims=True)
    return centred * lax.rsqrt(variance + epsilon) * gain_vec + shift_vec


f32 = jnp.float32
bf16 = jnp.bfloat16
GELU_SCALE = 0.7978845608028654
GELU_CUBE = 0.044715
BIAS_ROWS = 16


def slot_columns(alive, route_pair, order_key, experts, capacity, padded):
    earlier = (order_key[None, :] < order_key[:, None]).astype(bf16)
    columns = lax.broadcasted_iota(jnp.int32, (1, experts), 1)
    first_pick = ((route_pair[:, 0:1] == columns) & alive[:, None]).astype(f32)
    second = ((route_pair[:, 1:2] == columns) & alive[:, None]).astype(f32)
    both = jnp.concatenate([first_pick, second], axis=1).astype(bf16)
    ahead = jnp.dot(earlier, both, preferred_element_type=f32)
    place_first = jnp.sum(ahead[:, :experts] * first_pick, axis=1)
    already = jnp.sum(first_pick, axis=0, keepdims=True)
    place_second = jnp.sum((ahead[:, experts:] + already) * second, axis=1)
    slots = lax.broadcasted_iota(jnp.int32, (1, experts * padded), 1)

    def one_table(route_col, position, onehot):
        kept_mask = alive & (position < capacity)
        target = jnp.where(kept_mask, route_col * padded + position.astype(jnp.int32), -1)
        spread = (slots == target[:, None]).astype(bf16)
        return (spread, onehot * kept_mask[:, None].astype(f32))

    spread_first, first_kept = one_table(route_pair[:, 0], place_first, first_pick)
    spread_second, second_kept = one_table(route_pair[:, 1], place_second, second)
    return (first_pick, second, spread_first, spread_second, first_kept, second_kept)


def dot_nt(a, b):
    return lax.dot_general(a, b, (((1,), (1,)), ((), ())), preferred_element_type=f32)


def dot_tn(a, b):
    return lax.dot_general(a, b, (((0,), (0,)), ((), ())), preferred_element_type=f32)


def put_dots(padded, made, up_ref, back, ig_ref):
    width = made.shape[1]
    lanes = -(-padded // 128) * 128
    for start in range(0, made.shape[0], padded):
        at = slice(start, start + padded)
        ours = made[at]
        if lanes > padded:
            ours = jnp.concatenate([ours, jnp.zeros((lanes - padded, width), bf16)], axis=0)
        dots = dot_nt(up_ref[at, :], ours)
        row = lax.broadcasted_iota(jnp.int32, dots.shape, 0)
        column = lax.broadcasted_iota(jnp.int32, dots.shape, 1)
        dots = jnp.sum(jnp.where(row == column, dots, 0.0), axis=0, keepdims=True)
        high = dots.astype(bf16).astype(f32)
        blank = jnp.zeros((1, width - lanes), f32)
        place = lax.broadcasted_iota(jnp.int32, (padded, 1), 0)
        rows = jnp.where(place == padded - 2, jnp.concatenate([high, blank], axis=1), back[at])
        rows = jnp.where(place == padded - 1, jnp.concatenate([dots - high, blank], axis=1), rows)
        ig_ref[at, :] = rows.astype(bf16)


def expert_kernel(first, last, padded, block_ref, *refs):
    refs = list(refs)
    x_ref, g_ref, in_ref, out_ref = refs[:4]
    del refs[:4]
    if first:
        router_ref, pick_ref = refs[:2]
        del refs[:2]
    else:
        made_ref, back_ref = refs[:2]
        del refs[:4]
    if last:
        up_ref = g_ref if first else refs.pop(0)
    if first:
        slot_ref = refs.pop(0)
    prod_ref, ig_ref, grad_ref, rest_ref, gin, gout, gbias = refs
    step = pl.program_id(0)
    width = x_ref.shape[1]

    @pl.when(step == 0)
    def _():
        gin[...] = jnp.zeros_like(gin)
        gout[...] = jnp.zeros_like(gout)
        gbias[...] = jnp.zeros_like(gbias)

    x = x_ref[...]
    if first:
        logits = jnp.dot(x, router_ref[...], preferred_element_type=f32) + pick_ref[0:1, :]
        weights = jnp.exp(logits - jnp.max(logits, axis=1, keepdims=True))
        own = jnp.sum(weights * pick_ref[1:2, :], axis=1, keepdims=True)
        gate = own / jnp.sum(weights, axis=1, keepdims=True)
        slot_grad = (gate * g_ref[...].astype(f32)).astype(bf16)
        slot_ref[...] = slot_grad
    else:
        slot_grad = g_ref[...]
    below = width + BIAS_ROWS
    w_in = in_ref[0:width, :]
    bias = in_ref[width:below, :].astype(f32)[0:1, :]
    w_out = out_ref[...]
    v = jnp.dot(x, w_in, preferred_element_type=f32) + bias
    square = v * v
    t = jnp.tanh(GELU_SCALE * v * (1.0 + GELU_CUBE * square))
    half = 0.5 * (1.0 + t)
    hidden = (v * half).astype(bf16)
    slope = half + 0.5 * v * (1.0 - t * t) * (GELU_SCALE * (1.0 + 3.0 * GELU_CUBE * square))
    made = jnp.dot(hidden, w_out, preferred_element_type=f32)
    before_grad = dot_nt(slot_grad, w_out) * slope
    before_grad_b = before_grad.astype(bf16)
    back = dot_nt(before_grad_b, w_in)
    if not first:
        made = made + made_ref[...]
        back = back + back_ref[...]
    made = made.astype(prod_ref.dtype)
    prod_ref[...] = made
    if last:
        put_dots(padded, made, up_ref, back, ig_ref)
    else:
        ig_ref[...] = back
    gin[...] += dot_tn(x, before_grad_b)
    gout[...] += dot_tn(hidden, slot_grad)
    gbias[0:1, :] += jnp.sum(before_grad_b.astype(f32), axis=0, keepdims=True)

    @pl.when(step == pl.num_programs(0) - 1)
    def _():
        grad_ref[0, 0:width, :] = gin[...].astype(grad_ref.dtype)
        cut = width - rest_ref.shape[1]
        grad_ref[0, below : below + cut, :] = gout[0:cut, :].astype(bf16)
        rest_ref[0] = gout[cut:, :].astype(bf16)
        grad_ref[0, width:below, :] = jnp.broadcast_to(
            gbias[0:1, :], (BIAS_ROWS, gbias.shape[1])
        ).astype(grad_ref.dtype)


def expert_step(first, last, padded, count, block, x, g, weights, extra):
    rows, width = x.shape
    tile = rows // 2 if last else 256
    steps = rows // tile
    row_spec = pl.BlockSpec((tile, width), lambda i, b: (i, 0))
    whole = lambda a: pl.BlockSpec(a.shape, lambda i, b: (0, 0))
    in_specs = [row_spec, row_spec, whole(weights[0]), whole(weights[1])]
    outs = []
    specs = []
    if first:
        in_specs += [whole(extra[0]), whole(extra[1])]
        outs.append(jax.ShapeDtypeStruct((rows, width), bf16))
        specs.append(row_spec)
        aliases = {}
    else:
        in_specs += [row_spec, row_spec] + [pl.BlockSpec(memory_space=pl.ANY)] * 2 + [row_spec] * last
        aliases = {7: 2, 8: 3}
    acc_type = bf16 if last else f32
    outs += [jax.ShapeDtypeStruct((rows, width), acc_type)] * 2
    rest = width // 3 // 16 * 16
    heights = (weights[0].shape[0] + width - rest, rest)
    outs += [jax.ShapeDtypeStruct((count, h, width), bf16) for h in heights]
    specs += [row_spec, row_spec]
    specs += [pl.BlockSpec((1, h, width), lambda i, b: (b[0], 0, 0)) for h in heights]
    return pl.pallas_call(
        partial(expert_kernel, first, last, padded),
        grid_spec=pltpu.PrefetchScalarGridSpec(
            num_scalar_prefetch=1,
            grid=(steps,),
            in_specs=in_specs,
            out_specs=specs,
            scratch_shapes=[
                pltpu.VMEM((width, width), f32),
                pltpu.VMEM((width, width), f32),
                pltpu.VMEM((8, width), f32),
            ],
        ),
        out_shape=outs,
        input_output_aliases=aliases,
        compiler_params=pltpu.CompilerParams(
            vmem_limit_bytes=60 * 1024 * 1024, dimension_semantics=("arbitrary",)
        ),
        cost_estimate=pl.CostEstimate(flops=width, bytes_accessed=width, transcendentals=0),
        name="expert_step",
    )(block, x, g, *weights, *extra)


GROUP = 256


def lane_half(x, h):
    lanes = lax.broadcasted_iota(jnp.int32, (1, x.shape[1]), 1)
    inside = (lanes >= HEAD_DIM) if h else (lanes < HEAD_DIM)
    return jnp.where(inside, x, jnp.zeros_like(x))


def moments(x):
    average = jnp.mean(x, axis=1, keepdims=True)
    centred = x - average
    scale = lax.rsqrt(jnp.mean(centred * centred, axis=1, keepdims=True) + epsilon)
    return centred * scale, scale


def attend_kernel(
    tok_ref, vec_ref, wq_ref, wk_ref, wv_ref, qv_ref, wo_ref, mask_ref,
    n_ref, q_ref, k_ref, v_ref, m_ref, lse_ref, res_ref, sn_ref, acc,
):
    g = pl.program_id(0)

    @pl.when(g == 0)
    def _():
        tok = tok_ref[...].astype(f32)
        hat, _ = moments(tok)
        n_ref[...] = (hat * vec_ref[0:1, :] + vec_ref[1:2, :]).astype(bf16)
        acc[...] = tok + vec_ref[2:3, :]

    normed = n_ref[...]
    q = (jnp.dot(normed, wq_ref[...], preferred_element_type=f32) + qv_ref[0:1, :]).astype(bf16)
    k = jnp.dot(normed, wk_ref[...], preferred_element_type=f32).astype(bf16)
    v = (jnp.dot(normed, wv_ref[...], preferred_element_type=f32) + qv_ref[1:2, :]).astype(bf16)
    q = q * HEAD_DIM**-0.5
    q_ref[...] = q
    k_ref[...] = k
    v_ref[...] = v
    rows = q.shape[0]
    lanes = lax.broadcasted_iota(jnp.int32, (1, 128), 1)
    lse_all = jnp.zeros((rows, 128), f32)
    mixed = []
    for p in range(GROUP // 128):
        at = slice(128 * p, 128 * p + 128)
        qp, kp, vp = q[:, at], k[:, at], v[:, at]
        pair = None
        for h in range(2):
            scores = dot_nt(lane_half(qp, h), kp) + mask_ref[0:1, :]
            top = jnp.max(scores, axis=1, keepdims=True)
            weights = jnp.exp(scores - top)
            total = jnp.sum(weights, axis=1, keepdims=True)
            part = jnp.dot(weights.astype(bf16), lane_half(vp, h), preferred_element_type=f32)
            part = part * (1.0 / total)
            pair = part if pair is None else pair + part
            lse_all = jnp.where(lanes == 2 * p + h, top + jnp.log(total), lse_all)
        mixed.append(pair.astype(bf16))
    lse_ref[...] = lse_all.T[0:8, :]
    mixed = jnp.concatenate(mixed, axis=1)
    m_ref[...] = mixed
    acc[...] += jnp.dot(mixed, wo_ref[...], preferred_element_type=f32)

    @pl.when(g == pl.num_programs(0) - 1)
    def _():
        residual = acc[...]
        hat, _ = moments(residual)
        res_ref[...] = residual
        sn_ref[...] = (hat * vec_ref[3:4, :] + vec_ref[4:5, :]).astype(bf16)


def attend_forward(tok, vecs, wq, wk, wv, qv, wo, mask_row):
    rows, width = tok.shape
    groups = width // GROUP
    whole = lambda a: pl.BlockSpec(a.shape, lambda g: (0, 0))
    by_col = lambda r: pl.BlockSpec((r, GROUP), lambda g: (0, g))
    full = pl.BlockSpec((rows, width), lambda g: (0, 0))
    act = jax.ShapeDtypeStruct((rows, width), bf16)
    return pl.pallas_call(
        attend_kernel,
        grid=(groups,),
        in_specs=[
            whole(tok), whole(vecs), by_col(width), by_col(width), by_col(width), by_col(8),
            pl.BlockSpec((GROUP, width), lambda g: (g, 0)), whole(mask_row),
        ],
        out_specs=[
            full, by_col(rows), by_col(rows), by_col(rows), by_col(rows),
            pl.BlockSpec((8, rows), lambda g: (g, 0)), full, full,
        ],
        out_shape=[
            act, act, act, act, act, jax.ShapeDtypeStruct((8 * groups, rows), f32),
            jax.ShapeDtypeStruct((rows, width), f32), act,
        ],
        scratch_shapes=[pltpu.VMEM((rows, width), f32)],
        compiler_params=pltpu.CompilerParams(
            vmem_limit_bytes=40 * 1024 * 1024, dimension_semantics=("arbitrary",)
        ),
        cost_estimate=pl.CostEstimate(
            flops=width, bytes_accessed=width, transcendentals=0
        ),
        name="attend_forward",
    )(tok, vecs, wq, wk, wv, qv, wo, mask_row)


def put_halves(core, keep_ref, send_ref, start, columns, value):
    half = value.shape[0] // 2
    low, high = value[:half], value[half:]
    at = pl.ds(start, half)
    keep_ref[at, columns] = jnp.where(core == 0, low, high).astype(bf16)
    send_ref[at, columns] = jnp.where(core == 0, high, low).astype(bf16)


def attend_back_kernel(
    first, core_ref, n_ref, q_ref, k_ref, v_ref, lse_ref, mask_ref, ag_ref,
    wq_ref, wk_ref, wv_ref, wo_ref, *refs,
):
    refs = list(refs)
    if first:
        mix_ref, keep_ref, send_ref, db_ref, out_ref = refs
        start = n_ref.shape[1] // 2
        wide_grad = dot_tn(mix_ref[...], ag_ref[...])
        put_halves(core_ref[0], keep_ref, send_ref, 0, slice(None), wide_grad)
    else:
        acc_ref, tok_ref, vec_ref, rg_ref, keep_ref, send_ref, db_ref, tg_ref, ln_ref, acc = refs
        start = pl.multiple_of(pl.program_id(0) * (n_ref.shape[1] // 2), 16)
    mixed_grad = dot_nt(ag_ref[...], wo_ref[...]).astype(bf16)
    out = [[], [], []]
    for p in range(GROUP // 128):
        at = slice(128 * p, 128 * p + 128)
        qp, kp, vp, dp = q_ref[:, at], k_ref[:, at], v_ref[:, at], mixed_grad[:, at]
        dq_t = dk = dv = None
        for h in range(2):
            qh, kh, dh = lane_half(qp, h), lane_half(kp, h), lane_half(dp, h)
            row = 2 * p + h
            scores = dot_nt(kp, qh) + mask_ref[...]
            probs = jnp.exp(scores - lse_ref[row : row + 1, :])
            prob_grad = dot_nt(vp, dh)
            across = jnp.sum(probs * prob_grad, axis=0, keepdims=True)
            score_grad = (probs * (prob_grad - across)).astype(bf16)
            dv_h = jnp.dot(probs.astype(bf16), dh, preferred_element_type=f32)
            dk_h = jnp.dot(score_grad, qh, preferred_element_type=f32)
            dq_h = dot_tn(kh, score_grad)
            dv = dv_h if dv is None else dv + dv_h
            dk = dk_h if dk is None else dk + dk_h
            dq_t = dq_h if dq_t is None else dq_t + dq_h
        out[0].append((dq_t.T * HEAD_DIM**-0.5).astype(bf16))
        out[1].append(dk.astype(bf16))
        out[2].append(dv.astype(bf16))
    normed = n_ref[...]
    total = None
    sums = []
    for i, w_ref in enumerate((wq_ref, wk_ref, wv_ref)):
        grad = jnp.concatenate(out[i], axis=1)
        columns = slice(GROUP * i, GROUP * (i + 1))
        put_halves(core_ref[0], keep_ref, send_ref, start, columns, dot_tn(normed, grad))
        sums.append(jnp.sum(grad.astype(f32), axis=0, keepdims=True))
        back = dot_nt(grad, w_ref[...])
        total = back if total is None else total + back
    db_ref[0:1, :] = sums[0]
    db_ref[1:2, :] = sums[2]
    db_ref[2:8, :] = jnp.zeros((6, GROUP), f32)
    if first:
        out_ref[...] = total
        return
    step = pl.program_id(0)

    @pl.when(step == 0)
    def _():
        acc[...] = acc_ref[...] + total

    @pl.when(step > 0)
    def _():
        acc[...] += total

    @pl.when(step == pl.num_programs(0) - 1)
    def _():
        grad = acc[...]
        hat, scale_of = moments(tok_ref[...].astype(f32))
        inner = grad * vec_ref[0:1, :]
        mean = jnp.mean(inner, axis=1, keepdims=True)
        other = jnp.mean(inner * hat, axis=1, keepdims=True)
        tg_ref[...] = rg_ref[...] + (inner - mean - hat * other) * scale_of
        ln_ref[0:1, :] = jnp.sum(grad * hat, axis=0, keepdims=True)
        ln_ref[1:2, :] = jnp.sum(grad, axis=0, keepdims=True)
        ln_ref[2:8, :] = jnp.zeros((6, grad.shape[1]), f32)


def attend_backward(first, core, spare, n, q, k, v, lse, mask_col, ag, wq, wk, wv, wo, extra):
    rows, width = n.shape
    count = 1 if first else width // GROUP - 1
    skip = 0 if first else 1
    whole = lambda a: pl.BlockSpec(a.shape, lambda i, c: (0, 0))
    by_col = lambda r: pl.BlockSpec((r, GROUP), lambda i, c: (0, i + skip))
    by_row = lambda r, w: pl.BlockSpec((r, w), lambda i, c: (i + skip, 0))
    full = jax.ShapeDtypeStruct((rows, width), f32)
    half = jax.ShapeDtypeStruct(((count + first) * width // 2 + spare, width), bf16)
    outs = [half, half, jax.ShapeDtypeStruct((8, count * GROUP), f32), full]
    specs = [whole(half), whole(half), pl.BlockSpec((8, GROUP), lambda i, c: (0, i)), whole(full)]
    if not first:
        outs.append(jax.ShapeDtypeStruct((8, width), f32))
        specs.append(whole(outs[-1]))
    return pl.pallas_call(
        partial(attend_back_kernel, first),
        grid_spec=pltpu.PrefetchScalarGridSpec(
            num_scalar_prefetch=1,
            grid=(count,),
            in_specs=[
                whole(n), by_col(rows), by_col(rows), by_col(rows), by_row(8, rows), whole(mask_col), whole(ag),
                by_col(width), by_col(width), by_col(width), by_row(GROUP, width), *map(whole, extra),
            ],
            out_specs=specs,
            scratch_shapes=[] if first else [pltpu.VMEM((rows, width), f32)],
        ),
        out_shape=outs,
        compiler_params=pltpu.CompilerParams(
            vmem_limit_bytes=(40 if first else 60) * 1024 * 1024, dimension_semantics=("arbitrary",)
        ),
        cost_estimate=pl.CostEstimate(flops=width, bytes_accessed=width, transcendentals=0),
        name="attend_backward",
    )(core, n, q, k, v, lse, mask_col, ag, wq, wk, wv, wo, *extra)


def place_kernel(at_ref, *refs):
    early_refs, late_refs, (q_ref, k_ref, v_ref, o_ref, small_ref) = refs[0:2], refs[2:4], refs[4:]
    count, height = o_ref.shape[0], o_ref.shape[1]
    half = pl.num_programs(0) // 2
    own = (pl.program_id(0) // half) == at_ref[0]

    def put(early_ref, late_ref):
        for j in range(count):
            at = at_ref[2 + j]
            early, late = early_ref[0, at].astype(f32), late_ref[0, at].astype(f32)
            o_ref[j] = early[0:height]
            groups = (early[height : 2 * height], late[0:height], late[height : 2 * height])
            for g, grad in enumerate(groups):
                for i, ref in enumerate((q_ref, k_ref, v_ref)):
                    ref[j, :, GROUP * g : GROUP * (g + 1)] = grad[:, GROUP * i : GROUP * (i + 1)]
            small_ref[j] = late[2 * height :]

    @pl.when(own)
    def _():
        put(early_refs[0], late_refs[0])

    @pl.when(jnp.logical_not(own))
    def _():
        put(early_refs[1], late_refs[1])


def put_in_place(early, late, at, height):
    chips, narrow, _, width = early[0].shape
    heights = [height] * 4 + [late[0].shape[2] - 2 * height]

    def of_chip(received):
        def spot(i, at):
            return (jnp.clip(i - (at[0] ^ received) * chips, 0, chips - 1) ^ at[1], 0, 0, 0)

        return spot

    return pl.pallas_call(
        place_kernel,
        grid_spec=pltpu.PrefetchScalarGridSpec(
            num_scalar_prefetch=1,
            grid=(2 * chips,),
            in_specs=[
                pl.BlockSpec((1,) + a.shape[1:], of_chip(i)) for pair in (early, late) for i, a in enumerate(pair)
            ],
            out_specs=[pl.BlockSpec((narrow, h, width), lambda i, at: (i, 0, 0)) for h in heights],
        ),
        out_shape=[jax.ShapeDtypeStruct((2 * chips * narrow, h, width), f32) for h in heights],
        compiler_params=pltpu.CompilerParams(
            vmem_limit_bytes=60 * 1024 * 1024, dimension_semantics=("arbitrary",)
        ),
        name="put_in_place",
    )(at, *early, *late)


class Links:
    def __init__(self, wide, narrow):
        self.wide, self.narrow = wide, narrow
        self.chips = wide // 2
        self.w = lax.axis_index("wide")
        self.z = lax.axis_index("narrow")

    def swap(self, x, k):
        return lax.ppermute(x, "wide", [(i, i ^ k) for i in range(self.wide)])

    def shift(self, x, k=1):
        n = self.narrow
        return lax.ppermute(x, "narrow", [(i, (i + k) % n) for i in range(n)])

    def exchange(self, blocks):
        return lax.all_to_all(blocks, "wide", split_axis=0, concat_axis=0, tiled=True)

    def pick(self, a, i):
        return lax.dynamic_index_in_dim(a, i, 0, keepdims=False)

    def halve_end(self, begun):
        kept, got, rows = begun
        total = (kept.astype(f32) + got.astype(f32)).astype(bf16)
        cuts = [sum(rows[:i]) for i in range(len(rows) + 1)]
        return [total[a:b] for a, b in zip(cuts, cuts[1:])]

    def spread_chips(self, mats):
        chip = self.w >> 1
        part = lambda i: jnp.concatenate(
            [
                lax.dynamic_slice_in_dim(m, i * (m.shape[0] // self.chips), m.shape[0] // self.chips, 0)
                for m in mats
            ]
        )
        got = [self.swap(part(chip ^ k), 2 * k) for k in range(1, self.chips)]
        return (part(chip), got, [m.shape[0] // self.chips for m in mats])

    def spread_end(self, begun):
        kept, got, rows = begun
        total = sum((g.astype(f32) for g in got), kept.astype(f32)).astype(bf16)
        cuts = [sum(rows[:i]) for i in range(len(rows) + 1)]
        return jnp.concatenate(
            [total[a:b].reshape(self.narrow, -1, total.shape[1]) for a, b in zip(cuts, cuts[1:])], axis=1
        )

    def scatter_narrow(self, total):
        n = self.narrow
        part = self.pick(total, self.z).astype(f32)
        for k in range(1, n):
            part = part + self.shift(self.pick(total, (self.z + k) % n), k).astype(f32)
        return part.astype(bf16)

    def gather_narrow(self, part):
        return jnp.stack([part] + [self.shift(part, k) for k in range(1, self.narrow)])

    def gather_chips(self, pieces, *first):
        got = [self.swap(pieces, 2 * k) for k in range(1, self.chips - 1)]
        got.append(self.swap(after(pieces, first) if first else pieces, 2 * self.chips - 2))
        return jnp.stack([pieces] + got)

    def gather_cores(self, pieces):
        return (pieces, self.swap(pieces, 1))

    def places(self):
        spots = [(self.z - j) % self.narrow for j in range(self.narrow)]
        return jnp.stack([self.w & 1, self.w >> 1] + spots).astype(jnp.int32)


def after(value, *others):
    return lax.optimization_barrier((value, others))[0]


def local(
    wide,
    narrow,
    tokens,
    live_mask,
    routes,
    priority,
    cotangent,
    first_gain,
    first_shift,
    query_weight,
    query_bias,
    key_weight,
    value_weight,
    value_bias,
    out_weight,
    out_bias,
    second_gain,
    second_shift,
    router_weight,
    expert_in,
    expert_in_bias,
    expert_out,
    expert_out_bias,
):
    links = Links(wide, narrow)
    sequences, patches, features = tokens.shape
    patches_dev = sequences * patches
    experts = expert_out_bias.shape[0]
    capacity = max(2, (210 * patches_dev + 100 * experts - 1) // (100 * experts))
    padded = (capacity + 2 + 15) // 16 * 16
    scaling = HEAD_DIM ** (-0.5)
    head_shape = (patches, HEADS, HEAD_DIM)

    bias_rows = jnp.broadcast_to(expert_in_bias, (BIAS_ROWS, expert_in_bias.shape[1]))
    w_in, w_out = expert_in[0], expert_out[0]
    quarter = w_in.shape[1]
    if quarter < features:
        w_in = jnp.pad(w_in, ((0, 0), (0, features - quarter)))
        bias_rows = jnp.pad(bias_rows, ((0, 0), (0, features - quarter)))
        w_out = jnp.pad(w_out, ((0, features - quarter), (0, 0)))
    weights = [(jnp.concatenate([w_in, bias_rows], axis=0), w_out)]
    for _ in range(1, narrow):
        w_in, w_out = weights[-1]
        w_out = links.shift(w_out)
        weights.append((links.shift(w_in), w_out))

    order_key = (
        priority * sequences + lax.broadcasted_iota(jnp.int32, (sequences, patches), 0)
    ).reshape(patches_dev)
    first_pick, second, spread_first, spread_second, first_kept, second_kept = slot_columns(
        live_mask.reshape(patches_dev) > 0,
        routes.reshape(patches_dev, 2),
        order_key,
        experts,
        capacity,
        padded,
    )
    spread = spread_first + spread_second

    def to_slots(rows):
        return dot_tn(spread, rows).astype(bf16).reshape(experts, padded, features)

    upstream_b = cotangent.reshape(patches_dev, features)
    up_sent = to_slots(upstream_b)
    up_slots = links.exchange(up_sent).reshape(experts * padded, features)

    tok = tokens.reshape(patches_dev, features)
    bias = jnp.where(live_mask.reshape(patches_dev) > 0, 0.0, -1e30).astype(f32)
    none = jnp.zeros_like(first_gain)
    vecs = jnp.stack([first_gain, first_shift, out_bias, second_gain, second_shift, none, none, none])
    qv = jnp.stack([query_bias, value_bias] + [none] * 6)
    normed, queries, key_rows, value_rows, mixed_heads, lse, residual, second_normed = attend_forward(
        tok, vecs, query_weight, key_weight, value_weight, qv, out_weight,
        jnp.broadcast_to(bias[None, :], (8, patches_dev)),
    )
    logits = jnp.dot(second_normed, router_weight, preferred_element_type=f32)
    chance = jax.nn.softmax(logits, axis=-1)

    arrived = links.exchange(to_slots(second_normed)).reshape(experts * padded, features)

    router_wide = jnp.pad(router_weight, ((0, 0), (0, 128 - experts)))
    lanes = jnp.arange(128)
    pick_rows = jnp.stack(
        [jnp.where(lanes < experts, 0.0, -1e30), (lanes == links.w).astype(f32)] + [jnp.zeros(128)] * 6
    ).astype(f32)

    for s in range(narrow):
        block = ((links.z - s) % narrow).astype(jnp.int32).reshape(1)
        last = s == narrow - 1
        if s == 0:
            slot_grad, made, back, *grads = expert_step(
                True, last, padded, narrow, block, arrived, up_slots, weights[0], (router_wide, pick_rows)
            )
        else:
            made, back, *grads = expert_step(
                False, last, padded, narrow, block, arrived, slot_grad, weights[s],
                (made, back, *grads) + ((up_slots,) if last else ()),
            )
    def sum_owned(stacked):
        return lax.psum_scatter(stacked.reshape(-1, features), "narrow", scatter_dimension=0, tiled=True)

    grad_sum = sum_owned(grads[0])
    below = features + BIAS_ROWS
    expert_in_grad = grad_sum[None, :features, :quarter].astype(f32)
    expert_in_bias_grad = grad_sum[features : features + 1, :quarter].astype(f32)
    rest = grads[1].shape[1]
    expert_out_grad = jnp.pad(grad_sum[below:].astype(f32), ((0, rest), (0, 0)))

    back = back.reshape(experts, padded, features)
    back_tokens = links.exchange(back)
    upstream = upstream_b.astype(f32)
    gate_first = jnp.sum(chance * first_pick, axis=1, keepdims=True)
    gate_second = jnp.sum(chance * second, axis=1, keepdims=True)
    slot_dots = back_tokens[:, padded - 2, :padded].astype(f32) + back_tokens[
        :, padded - 1, :padded
    ].astype(f32)
    slot_dots = slot_dots.reshape(1, experts * padded)
    bias_dots = jnp.dot(upstream, expert_out_bias.T, precision=highest)
    gate_first_grad = jnp.sum(spread_first * slot_dots, axis=1, keepdims=True) + jnp.sum(
        first_kept * bias_dots, axis=1, keepdims=True
    )
    gate_second_grad = jnp.sum(spread_second * slot_dots, axis=1, keepdims=True) + jnp.sum(
        second_kept * bias_dots, axis=1, keepdims=True
    )
    out_bias_sum = jnp.dot(
        (gate_first * first_kept + gate_second * second_kept).T, upstream, precision=highest
    )
    chance_grad = first_pick * gate_first_grad + second * gate_second_grad
    logit_grad = chance * (chance_grad - jnp.sum(chance * chance_grad, axis=1, keepdims=True))
    logit_grad = logit_grad.astype(bf16)
    router_sum = jnp.dot(second_normed.T, logit_grad, preferred_element_type=f32)
    second_normed_grad = jnp.dot(logit_grad, router_weight.T, preferred_element_type=f32)
    second_normed_grad = second_normed_grad + jnp.dot(
        spread, back_tokens.reshape(experts * padded, features), preferred_element_type=f32
    )
    unused, second_back = jax.vjp(layer_norm, residual, second_gain, second_shift)
    residual_part, second_gain_grad, second_shift_grad = second_back(second_normed_grad)
    residual_grad = upstream + residual_part
    attended_grad = residual_grad.astype(bf16)
    out_bias_grad = jnp.sum(attended_grad.astype(f32), axis=0)
    shared = (normed, queries, key_rows, value_rows, lse, bias[:, None], attended_grad)
    shared += (query_weight, key_weight, value_weight, out_weight)
    parts = wide * narrow
    small_rows = -(-(8 + 2 * experts) // (8 * parts)) * 8
    spare = small_rows * parts // 2
    core = (links.w & 1).astype(jnp.int32)
    kept, sent, bias_first, running = attend_backward(True, core[None], 0, *shared, (mixed_heads,))
    begun = (kept, links.swap(sent, 1), [features // 2] * 2)
    returned = links.exchange(after(made, sent).reshape(experts, padded, features)).reshape(
        experts * padded, features
    )
    kept, sent, bias_rest, tokens_grad, norm_grads = attend_backward(
        False, core[None], spare, *shared, (running, tok, vecs, residual_grad)
    )
    begun = links.spread_chips(links.halve_end(begun))
    bias_grads = jnp.concatenate([bias_first, bias_rest], axis=1)

    small = jnp.concatenate(
        [norm_grads[0:2], bias_grads[0:2], out_bias_grad[None], second_gain_grad[None],
         second_shift_grad[None], jnp.zeros((1, features), f32), router_sum.T, out_bias_sum], axis=0
    )
    small = jnp.pad(small, ((0, 2 * spare - small.shape[0]), (0, 0))).astype(bf16).reshape(2, spare, features)
    filled = kept.shape[0] - spare
    kept = lax.dynamic_update_slice_in_dim(kept, links.pick(small, core), filled, 0)
    sent = lax.dynamic_update_slice_in_dim(sent, links.pick(small, 1 - core), filled, 0)
    late = (kept, links.swap(after(sent, returned), 1), [features // 2] * 2 + [spare])
    late = links.halve_end(late)
    early = links.scatter_narrow(after(links.spread_end(begun), late))
    late = links.spread_end(links.spread_chips(late))
    early = links.gather_narrow(early)
    early_pieces = links.gather_chips(early)
    picked_first = jnp.dot(spread_first, returned, preferred_element_type=f32)
    picked_second = jnp.dot(spread_second, returned, preferred_element_type=f32)
    gated_bias = jnp.dot(
        gate_first * first_kept + gate_second * second_kept, expert_out_bias, precision=highest
    )
    output = residual + gate_first * picked_first + gate_second * picked_second + gated_bias
    output = output.astype(bf16).reshape(sequences, patches, features)
    late = links.scatter_narrow(after(late, output))
    late = links.gather_narrow(after(late, early))
    late_pieces = links.gather_chips(
        after(late, early_pieces), expert_in_grad, expert_in_bias_grad, expert_out_grad
    )
    rest_sum = sum_owned(after(grads[1], late, early_pieces))
    totals = put_in_place(
        links.gather_cores(early_pieces),
        links.gather_cores(late_pieces),
        links.places(), features // parts)
    rest_sum = after(rest_sum, totals).astype(f32)
    expert_out_grad = lax.dynamic_update_slice_in_dim(expert_out_grad, rest_sum, features - rest, 0)
    expert_out_grad = expert_out_grad[None, :quarter]
    totals = [a.reshape(-1, features) for a in totals]
    small = totals[4]
    tokens_grad = tokens_grad.reshape(sequences, patches, features)

    return (
        output,
        tokens_grad,
        small[0],
        small[1],
        totals[0],
        small[2],
        totals[1],
        totals[2],
        small[3],
        totals[3],
        small[4],
        small[5],
        small[6],
        small[8 : 8 + experts].T,
        expert_in_grad,
        expert_in_bias_grad,
        expert_out_grad,
        small[8 + experts : 8 + 2 * experts],
    )


def solution(mesh):
    return jax.shard_map(
        partial(local, mesh.shape["wide"], mesh.shape["narrow"]),
        mesh=mesh,
        in_specs=(
            P(("wide", "narrow"), None, None),
            P(("wide", "narrow"), None),
            P(("wide", "narrow"), None, None),
            P(("wide", "narrow"), None),
            P(("wide", "narrow"), None, None),
            P(),
            P(),
            P(),
            P(),
            P(),
            P(),
            P(),
            P(),
            P(),
            P(),
            P(),
            P(),
            P("wide", None, "narrow"),
            P("wide", "narrow"),
            P("wide", "narrow", None),
            P(),
        ),
        out_specs=(
            P(("wide", "narrow"), None, None),
            P(("wide", "narrow"), None, None),
            P(),
            P(),
            P(),
            P(),
            P(),
            P(),
            P(),
            P(),
            P(),
            P(),
            P(),
            P(),
            P("wide", None, "narrow"),
            P("wide", "narrow"),
            P("wide", "narrow", None),
            P(),
        ),
        check_vma=False,
    )
```
